32 devices in a mesh: section: 2 (over y), dp: 4 (over z), ctx: 4 (over x, core).
Axes of the slice: x: 2, y: 2, z: 4, core: 2. Of those that a mesh axis runs over, the one named last changes fastest.
Arguments:
- token_ids: int32 [1024], P('ctx'), may hold values from 0 to 511
- embedding: bfloat16 [512, 4096], P(None, 'dp'), may hold values from -6 to 6
- project_in: bfloat16 [2, 4096, 3, 4096], P('section', 'ctx', None, 'dp'), may hold values from -0.09375 to 0.09375
- short_taps: float32 [2, 3, 3, 4096], P('section', None, None, 'dp'), may hold values from -3.5 to 3.5
- filter_taps: float32 [2, 128, 4096], P('section', None, 'dp'), may hold values from -0.5 to 0.5
- decay_rates: float32 [2, 4096], P('section', 'dp'), may hold values from 0.5 to 4
- project_out: bfloat16 [2, 4096, 4096], P('section', 'dp', 'ctx'), may hold values from -0.09375 to 0.09375
- cotangent: bfloat16 [1024, 4096], P('ctx', 'dp'), may hold values from -0.1875 to 0.1875
Outputs:
- grad_project_in: float32 [2, 4096, 3, 4096], P('section', 'ctx', None, 'dp')
- grad_project_out: float32 [2, 4096, 4096], P('section', 'dp', 'ctx')
- grad_filter: float32 [2, 128, 4096], P('section', None, 'dp')
- grad_decay: float32 [2, 4096], P('section', 'dp')
- grad_short: float32 [2, 3, 3, 4096], P('section', None, None, 'dp')
The draws below stay inside these ranges and needn't reach their ends.
All inputs are finite; a program needn't handle non-finite values.
Results may differ from the reference program's by a relative error of at most 0.03.
Values may be sent and summed in bfloat16 or wider, within the bound.
No kernel may reach another device: no remote copies, remote signals or barrier semaphores. Data moves between devices by JAX's collectives and lax.ppermute only.
A program may use at most 192 MiB of HBM per device.

```python
import math
import jax
import jax.numpy as jnp
from jax import lax

D = 4096
C = 4096
L = 128
VOCAB = 512
TOK_DEV = 256
SEQ = 1024
N_SECTION = 2
N_DP = 4
N_CTX = 4


def set_ends(entries, rng, low, top_value):
    dims = entries.shape
    place = [jax.random.randint(jax.random.fold_in(rng, axis), (), 0, dims[axis]) for axis in range(len(dims))]
    entries = entries.at[tuple(place)].set(low)
    longest = dims.index(max(dims))
    place[longest] = (place[longest] + 1) % dims[longest]
    return entries.at[tuple(place)].set(top_value)


def levels(key, shape, split, smallest, largest):
    loudness = 1.0
    for position, blocks in split:
        draws = jax.random.uniform(jax.random.fold_in(jax.random.fold_in(key, 6), position), (blocks,), jnp.float32, smallest / len(split), largest / len(split))
        loudness = loudness * jnp.repeat(jnp.exp(draws), shape[position] // blocks).reshape((-1,) + (1,) * (len(shape) - 1 - position))
    return loudness


def centred(key, shape, width, limit, cuts=(), kind=jnp.bfloat16):
    drawn = width * jax.random.normal(key, shape, jnp.float32)
    if cuts:
        drawn = drawn * levels(key, shape, cuts, -0.22, 0.18)
    return jnp.clip(drawn, -limit, limit).astype(kind)


def setup_inputs(seed: int = 0) -> dict:
    key_list = jax.random.split(jax.random.key(seed), 9)
    token_ids = set_ends(jax.random.randint(key_list[0], (SEQ,), 0, VOCAB), jax.random.fold_in(key_list[0], 1), 0, VOCAB - 1).astype(jnp.int32)
    embedding = centred(key_list[1], (VOCAB, D), 1.0, 6.0, ((1, 4),))
    project_in = centred(key_list[2], (N_SECTION, D, 3, C), D ** -0.5, 0.09375, ((0, 2), (1, 4), (3, 4)))
    short_taps = centred(key_list[3], (N_SECTION, 3, 3, C), 3 ** -0.5, 3.5, ((0, 2), (3, 4)), jnp.float32)
    filter_taps = centred(key_list[4], (N_SECTION, L, C), L ** -0.5, 0.5, ((0, 2), (2, 4)), jnp.float32)
    decay_rates = jnp.clip(jnp.exp(math.log(4.0) - 2.0794415 * jax.random.uniform(key_list[5], (N_SECTION, C), jnp.float32) ** levels(key_list[5], (N_SECTION, C), ((0, 2), (1, 4)), -0.2, 0.2)), 0.5, 4.0)
    project_out = centred(key_list[6], (N_SECTION, C, D), C ** -0.5, 0.09375, ((0, 2), (1, 4), (2, 4)))
    cotangent = centred(key_list[7], (SEQ, D), SEQ ** -0.5, 0.1875, ((0, 4), (1, 4)))
    return {"token_ids": token_ids, "embedding": embedding, "project_in": project_in, "short_taps": short_taps, "filter_taps": filter_taps, "decay_rates": decay_rates, "project_out": project_out, "cotangent": cotangent}


EPSILON = 1e-06

def correlate(signal, kernel):
    tap_count = kernel.shape[0]
    out_len = signal.shape[0] - tap_count + 1

    def add_tap(index, total):
        window = lax.dynamic_slice_in_dim(signal, index, out_len, 0)
        weight_row = lax.dynamic_slice_in_dim(kernel, index, 1, 0)
        return total + window * weight_row
    return lax.fori_loop(0, tap_count, add_tap, jnp.zeros((out_len, signal.shape[1]), signal.dtype))

def round_trip(values):
    return lax.optimization_barrier(values.astype(jnp.bfloat16)).astype(jnp.float32)

def forward_block(inputs, project_in, short_taps, filter_taps, decay_rates, project_out):
    seq_len = inputs.shape[0]
    rows_float = inputs.astype(jnp.float32)
    inv_rms = lax.rsqrt(lax.optimization_barrier(jnp.mean(rows_float * rows_float, axis=1, keepdims=True)) + EPSILON)
    normed = (rows_float * inv_rms).astype(jnp.bfloat16)
    projected = jnp.dot(normed, project_in.reshape(D, 3 * C), preferred_element_type=jnp.float32).reshape(seq_len, 3, C)
    padded_proj = jnp.concatenate([jnp.zeros((2, 3, C), jnp.float32), projected], axis=0)
    shortened = short_taps[0] * padded_proj[2:] + short_taps[1] * padded_proj[1:-1] + short_taps[2] * padded_proj[:-2]
    products = shortened[:, 1] * shortened[:, 2]
    padded_prod = jnp.concatenate([jnp.zeros((L - 1, C), jnp.float32), products], axis=0)
    positions = jnp.arange(L).astype(jnp.float32)
    damping = jnp.exp(-decay_rates[None, :] * positions[:, None] / L)
    kernel = filter_taps * damping
    filtered = correlate(padded_prod, kernel[::-1])
    gated_rows = (shortened[:, 0] * filtered).astype(jnp.bfloat16)
    group_width = C // N_DP
    running = jnp.zeros((seq_len, D), jnp.float32)
    for group_index in range(N_DP):
        lower_edge = group_index * group_width
        group_part = jnp.dot(gated_rows[:, lower_edge:lower_edge + group_width], project_out[lower_edge:lower_edge + group_width], preferred_element_type=jnp.float32)
        running = running + round_trip(group_part)
    outputs = (rows_float + running).astype(jnp.bfloat16)
    return (outputs, (rows_float, inv_rms, normed, padded_proj, shortened, padded_prod, filtered, gated_rows, kernel, damping, positions))

def backward_block(saved, grad_rows, project_in, short_taps, filter_taps, project_out, need_input):
    rows_float, inv_rms, normed, padded_proj, shortened, padded_prod, filtered, gated_rows, kernel, damping, positions = saved
    seq_len = grad_rows.shape[0]
    grad_gated = jnp.dot(grad_rows, project_out.T, preferred_element_type=jnp.float32)
    grad_query = grad_gated * filtered
    grad_filtered = grad_gated * shortened[:, 0]
    padded_grad = jnp.concatenate([grad_filtered, jnp.zeros((L - 1, C), jnp.float32)], axis=0)
    grad_prod = correlate(padded_grad, kernel)
    grad_kernel = correlate(padded_prod, grad_filtered)[::-1]
    grad_short_out = jnp.stack([grad_query, grad_prod * shortened[:, 2], grad_prod * shortened[:, 1]], axis=1)
    padded_short = jnp.concatenate([grad_short_out, jnp.zeros((2, 3, C), jnp.float32)], axis=0)
    grad_proj = short_taps[0] * padded_short[:-2] + short_taps[1] * padded_short[1:-1] + short_taps[2] * padded_short[2:]
    grad_taps = jnp.stack([lax.optimization_barrier(jnp.sum(grad_short_out * padded_proj[2:], axis=0)), lax.optimization_barrier(jnp.sum(grad_short_out * padded_proj[1:-1], axis=0)), lax.optimization_barrier(jnp.sum(grad_short_out * padded_proj[:-2], axis=0))], axis=0)
    grad_proj_b = grad_proj.astype(jnp.bfloat16)
    grad_filter = grad_kernel * damping
    grad_decay = -lax.optimization_barrier(jnp.sum(grad_kernel * filter_taps * damping * positions[:, None], axis=0)) / L
    flat_grad = grad_proj_b.reshape(seq_len, 3 * C)
    grad_in = jnp.zeros((D, 3 * C), jnp.float32)
    grad_out = jnp.zeros((C, D), jnp.float32)
    for slice_index in range(N_CTX):
        lower_edge = slice_index * TOK_DEV
        upper_edge = lower_edge + TOK_DEV
        grad_in = grad_in + round_trip(jnp.dot(normed[lower_edge:upper_edge].T, flat_grad[lower_edge:upper_edge], preferred_element_type=jnp.float32))
        grad_out = grad_out + round_trip(jnp.dot(gated_rows[lower_edge:upper_edge].T, grad_rows[lower_edge:upper_edge], preferred_element_type=jnp.float32))
    grad_in = grad_in.reshape(D, 3, C)
    grad_inputs = None
    if need_input:
        group_width = C // N_DP
        grad_normed = jnp.zeros((seq_len, D), jnp.float32)
        for group_index in range(N_DP):
            lower_edge = group_index * group_width
            upper_edge = lower_edge + group_width
            left_part = grad_proj_b[:, :, lower_edge:upper_edge].reshape(seq_len, 3 * group_width)
            right_part = project_in[:, :, lower_edge:upper_edge].reshape(D, 3 * group_width)
            grad_normed = grad_normed + round_trip(jnp.dot(left_part, right_part.T, preferred_element_type=jnp.float32))
        row_stat = lax.optimization_barrier(jnp.mean(rows_float * grad_normed, axis=1, keepdims=True))
        grad_inputs = (grad_rows.astype(jnp.float32) + inv_rms * grad_normed - rows_float * inv_rms ** 3 * row_stat).astype(jnp.bfloat16)
    return (grad_inputs, (grad_in, grad_out, grad_filter, grad_decay, grad_taps))

def reference(token_ids, embedding, project_in, short_taps, filter_taps, decay_rates, project_out, cotangent):
    first_rows = embedding[token_ids]
    middle_rows, saved_first = forward_block(first_rows, project_in[0], short_taps[0], filter_taps[0], decay_rates[0], project_out[0])
    final_rows, saved_second = forward_block(middle_rows, project_in[1], short_taps[1], filter_taps[1], decay_rates[1], project_out[1])
    back_grad, second_grads = backward_block(saved_second, cotangent, project_in[1], short_taps[1], filter_taps[1], project_out[1], True)
    unused_grad, first_grads = backward_block(saved_first, back_grad, project_in[0], short_taps[0], filter_taps[0], project_out[0], False)
    return (jnp.stack([first_grads[0], second_grads[0]]), jnp.stack([first_grads[1], second_grads[1]]), jnp.stack([first_grads[2], second_grads[2]]), jnp.stack([first_grads[3], second_grads[3]]), jnp.stack([first_grads[4], second_grads[4]]))
```

```python
import functools

import jax
import jax.numpy as jnp
import numpy as np
from jax import lax
from jax.experimental import pallas as pl
from jax.experimental.pallas import tpu as pltpu
from jax.sharding import PartitionSpec as P

EPSILON = 1e-06
F32 = jnp.float32
BF16 = jnp.bfloat16


def dot(left, right):
    return jnp.dot(left, right, preferred_element_type=F32)


def dot_t(left, right):
    return lax.dot_general(left, right, (((1,), (1,)), ((), ())), preferred_element_type=F32)


def exact(left, right):
    return jnp.dot(left, right, preferred_element_type=F32, precision=lax.Precision.HIGHEST)


def pick(stack, index):
    return lax.dynamic_index_in_dim(stack, index, 0, keepdims=False)


def send(value, axes, route):
    sizes = [lax.axis_size(axis) for axis in axes]
    pairs = []
    for source, place in enumerate(np.ndindex(*sizes)):
        target = route(*place)
        if target is not None:
            pairs.append((source, int(np.ravel_multi_index(target, sizes))))
    return lax.ppermute(value, axes, pairs)


def ctx_xor(value, mask, sections):
    return send(
        value, ("section", "ctx"), lambda s, k: (s, k ^ mask) if s in sections else None
    )


def ctx_gather(value, sections):
    count = lax.axis_size("ctx")
    held = {0: value}
    bit = count // 2
    while bit:
        for r in list(held):
            held[r | bit] = ctx_xor(held[r], bit, sections)
        bit //= 2
    return [held[r] for r in range(count)]


def scatter_order(count):
    if count == 1:
        return [0]
    inner = scatter_order(count // 2)
    return [2 * r for r in inner] + [2 * r + 1 for r in inner]


def dp_gather(value, section, parts):
    count = lax.axis_size("dp")
    pieces = [jnp.split(value, parts, axis=0)]
    for _ in range(count - 1):
        pieces.append(
            [
                send(
                    piece,
                    ("section", "dp"),
                    lambda s, z: (s, (z + 1) % count) if s == section else None,
                )
                for piece in pieces[-1]
            ]
        )
    return jnp.stack([jnp.concatenate(piece, axis=0) for piece in pieces])


def cross_sum(shares, source):
    count = lax.axis_size("dp")
    me = lax.axis_index("dp")
    total = 0.0
    for shift in range(count):
        arrived = send(
            pick(shares, (me + shift) % count),
            ("section", "dp"),
            lambda s, z: (1 - s, (z + shift) % count) if s == source else None,
        )
        total = total + arrived.astype(F32)
    return total


def in_order(stack, me):
    return [pick(stack, (me - q) % stack.shape[0]) for q in range(stack.shape[0])]


def spectra(taps):
    freq = np.arange(taps)[:, None]
    time = np.arange(taps)[None, :]
    angle = np.pi * freq * time / taps
    nyquist = np.where(time % 2 == 0, 1.0, -1.0)
    forward = np.concatenate(
        [np.cos(angle), np.where(freq == 0, nyquist, -np.sin(angle))], axis=0
    )
    weight = np.where(freq == 0, 1.0, 2.0) / (2 * taps)
    inverse = np.concatenate(
        [weight * np.cos(angle), np.where(freq == 0, nyquist, -2 * np.sin(angle)) * np.where(freq == 0, weight, 1.0 / (2 * taps))],
        axis=0,
    ).T
    sign = np.where(np.arange(2 * taps) % taps % 2 == 0, 1.0, -1.0)
    return [jnp.asarray(m, BF16) for m in (forward, inverse, inverse * sign[None, :])]


def later(current, before, steps, row):
    return jnp.where(row < steps, pltpu.roll(before, steps, 0), pltpu.roll(current, steps, 0))


def sooner(current, after, steps, row):
    count = current.shape[0]
    return jnp.where(
        row >= count - steps,
        pltpu.roll(after, count - steps, 0),
        pltpu.roll(current, count - steps, 0),
    )


def kernel_spectrum(fwd_ref, kern_ref, row):
    tap_count = kern_ref.shape[0]
    kern = dot(fwd_ref[...], kern_ref[...].astype(BF16))
    real, imag = kern[:tap_count], kern[tap_count:]
    return real, jnp.where(row == 0, 0.0, imag), jnp.where(row == 0, imag, real)


def proj_block(proj_ref, m, b, tap_count):
    chunk, start = divmod(b * tap_count, proj_ref.shape[2])
    return proj_ref[chunk, m, start : start + tap_count, :].astype(F32)


def short_filter(taps_ref, m, current, before, row):
    return (
        taps_ref[m : m + 1, :] * current
        + taps_ref[3 + m : 4 + m, :] * later(current, before, 1, row)
        + taps_ref[6 + m : 7 + m, :] * later(current, before, 2, row)
    )


def lookup_kernel(
    tokens_ref, table_ref, taps_ref, kern_ref, fwd_ref, inv_ref,
    gated_ref, filt_ref, spec_ref, proj_ref,
):
    tap_count, vocab = kern_ref.shape[0], table_ref.shape[1]
    entry = lax.broadcasted_iota(jnp.int32, (tap_count, vocab), 1)
    for b in range(filt_ref.shape[0] // tap_count):
        here = pl.ds(b * tap_count, tap_count)
        chosen = (entry == tokens_ref[here, :]).astype(F32).astype(BF16)
        for m in range(3):
            proj_ref[0, m, here, :] = dot(chosen, table_ref[m]).astype(BF16)
    forward_kernel(
        proj_ref, taps_ref, kern_ref, fwd_ref, inv_ref, gated_ref, filt_ref, spec_ref
    )


def collect_kernel(
    tokens_ref, scale_ref, gg_ref, proj_ref, taps_ref, kern_ref, fwd_ref, inv_ref, filt_ref, spec_ref,
    table_ref, gkern_ref, gtaps_ref, grad_spec, gproj_ref,
):
    backward_kernel(
        gg_ref, proj_ref, taps_ref, kern_ref, fwd_ref, inv_ref, filt_ref, spec_ref,
        gproj_ref, gkern_ref, gtaps_ref, grad_spec,
    )
    _, vocab, _ = table_ref.shape
    seq = filt_ref.shape[0]
    entry = lax.broadcasted_iota(jnp.int32, (vocab, seq), 0)
    chosen = (entry == tokens_ref[...]).astype(F32).astype(BF16)
    for m in range(3):
        table_ref[m] = (dot(chosen, gproj_ref[0, m]) * scale_ref[...]).astype(BF16)


def forward_kernel(proj_ref, taps_ref, kern_ref, fwd_ref, inv_ref, gated_ref, filt_ref, spec_ref):
    tap_count, chans = kern_ref.shape
    blocks = filt_ref.shape[0] // tap_count
    row = lax.broadcasted_iota(jnp.int32, (tap_count, chans), 0)
    sign = jnp.where(row % 2 == 0, 1.0, -1.0)
    kr, ki, kn = kernel_spectrum(fwd_ref, kern_ref, row)
    zero = jnp.zeros((tap_count, chans), F32)
    before = [zero] * 3
    last_r, last_i = zero, zero
    for b in range(blocks):
        here = pl.ds(b * tap_count, tap_count)
        streams = []
        for m in range(3):
            current = proj_block(proj_ref, m, b, tap_count)
            streams.append(short_filter(taps_ref, m, current, before[m], row))
            before[m] = current
        part = dot(fwd_ref[...], (streams[1] * streams[2]).astype(BF16))
        pr, pi = part[:tap_count], part[tap_count:]
        wr = last_r + sign * pr
        wi = last_i + sign * pi
        last_r, last_i = pr, pi
        spec_ref[b, :tap_count, :] = wr.astype(BF16)
        spec_ref[b, tap_count:, :] = wi.astype(BF16)
        mixed = jnp.concatenate([wr * kr - wi * ki, wr * ki + wi * kn], axis=0)
        filtered = dot(inv_ref[...], mixed.astype(BF16))
        filt_ref[here, :] = filtered.astype(BF16)
        gated_ref[here, :] = (streams[0] * filtered).astype(BF16)


def backward_kernel(
    gg_ref, proj_ref, taps_ref, kern_ref, fwd_ref, inv_ref, filt_ref, spec_ref,
    gproj_ref, gkern_ref, gtaps_ref, grad_spec,
):
    tap_count, chans = kern_ref.shape
    blocks = filt_ref.shape[0] // tap_count
    row = lax.broadcasted_iota(jnp.int32, (tap_count, chans), 0)
    sign = jnp.where(row % 2 == 0, 1.0, -1.0)
    kr, ki, kn = kernel_spectrum(fwd_ref, kern_ref, row)
    zero = jnp.zeros((tap_count, chans), F32)
    sum_r, sum_i = zero, zero
    last = zero
    for b in range(blocks):
        here = pl.ds(b * tap_count, tap_count)
        current = proj_block(proj_ref, 0, b, tap_count)
        query = short_filter(taps_ref, 0, current, last, row)
        last = current
        part = dot(fwd_ref[...], (gg_ref[here, :].astype(F32) * query).astype(BF16))
        grad_spec[b] = part
        gr, gi = sign * part[:tap_count], sign * part[tap_count:]
        wr = spec_ref[b, :tap_count, :].astype(F32)
        wi = spec_ref[b, tap_count:, :].astype(F32)
        rr, ii = wr * gr, wi * gi
        sum_r = sum_r + jnp.where(row == 0, rr, rr + ii)
        sum_i = sum_i + jnp.where(row == 0, ii, wr * gi - wi * gr)
    gkern_ref[...] = exact(
        inv_ref[...].astype(F32), jnp.concatenate([sum_r, sum_i], axis=0)
    )
    after = [zero] * 3
    next_r, next_i = zero, zero
    sums = [jnp.zeros((1, chans), F32) for _ in range(9)]
    for b in reversed(range(blocks)):
        chunk, start = divmod(b * tap_count, proj_ref.shape[2])
        here = pl.ds(b * tap_count, tap_count)
        gr, gi = grad_spec[b, :tap_count, :], grad_spec[b, tap_count:, :]
        vr, vi = gr + sign * next_r, gi + sign * next_i
        next_r, next_i = gr, gi
        mixed = jnp.concatenate([vr * kr + vi * ki, vi * kn - vr * ki], axis=0)
        grad_prod = dot(inv_ref[...], mixed.astype(BF16))
        shifts, shorts = [], []
        for m in range(3):
            current = proj_block(proj_ref, m, b, tap_count)
            before = proj_block(proj_ref, m, b - 1, tap_count) if b else zero
            shifts.append([current, later(current, before, 1, row), later(current, before, 2, row)])
            if m:
                shorts.append(sum(taps_ref[3 * j + m : 3 * j + m + 1, :] * shifts[m][j] for j in range(3)))
        grads = [
            gg_ref[here, :].astype(F32) * filt_ref[here, :].astype(F32),
            grad_prod * shorts[1],
            grad_prod * shorts[0],
        ]
        for m in range(3):
            grad = grads[m]
            out = (
                taps_ref[m : m + 1, :] * grad
                + taps_ref[3 + m : 4 + m, :] * sooner(grad, after[m], 1, row)
                + taps_ref[6 + m : 7 + m, :] * sooner(grad, after[m], 2, row)
            )
            after[m] = grad
            gproj_ref[chunk, m, start : start + tap_count, :] = out.astype(BF16)
            for j in range(3):
                sums[3 * j + m] = sums[3 * j + m] + jnp.sum(
                    grad * shifts[m][j], axis=0, keepdims=True
                )
    for index in range(9):
        gtaps_ref[index : index + 1, :] = sums[index]


PARAMS = pltpu.CompilerParams(vmem_limit_bytes=56 * 1024 * 1024)


def conv_forward(proj, taps, kern, matrices, tokens=None):
    tap_count, chans = kern.shape
    seq = proj.shape[0] * proj.shape[2] if tokens is None else tokens.shape[0]
    results = [
        jax.ShapeDtypeStruct((seq, chans), BF16),
        jax.ShapeDtypeStruct((seq, chans), BF16),
        jax.ShapeDtypeStruct((seq // tap_count, 2 * tap_count, chans), BF16),
    ]
    operands = (proj, taps, kern, matrices[0], matrices[2])
    if tokens is not None:
        results.append(jax.ShapeDtypeStruct((1, 3, seq, chans), BF16))
        operands = (tokens[:, None], *operands)
    return pl.pallas_call(
        forward_kernel if tokens is None else lookup_kernel,
        out_shape=results,
        compiler_params=PARAMS,
        name="conv_forward",
    )(*operands)


def conv_backward(gg, proj, taps, kern, matrices, saved, tokens=None, scale=None):
    tap_count, chans = kern.shape
    seq = gg.shape[0]
    scratch = [pltpu.VMEM((seq // tap_count, 2 * tap_count, chans), F32)]
    operands = (gg, proj, taps, kern, matrices[0], matrices[1], *saved)
    first = jax.ShapeDtypeStruct(proj.shape, BF16)
    if tokens is not None:
        first = jax.ShapeDtypeStruct((3, scale.shape[0], chans), BF16)
        scratch.append(pltpu.VMEM(proj.shape, BF16))
        operands = (tokens[None, :], scale, *operands)
    return pl.pallas_call(
        backward_kernel if tokens is None else collect_kernel,
        out_shape=(
            first,
            jax.ShapeDtypeStruct(kern.shape, F32),
            jax.ShapeDtypeStruct((9, chans), F32),
        ),
        scratch_shapes=scratch,
        compiler_params=PARAMS,
        name="conv_backward",
    )(*operands)


def table_projection(table, weights, ctx, order, kind):
    vocab, feats = table.shape
    sub = weights.shape[2] // lax.axis_size("ctx")
    if sub % 128:
        columns = jnp.stack(
            [lax.dynamic_slice_in_dim(weights, (ctx ^ r) * sub, sub, 2) for r in order]
        )
        return jnp.einsum("vd,rmdc->rmvc", table, columns, preferred_element_type=F32).astype(kind)

    def kernel(where_ref, table_ref, weights_ref, out_ref):
        for m in range(3):
            out_ref[0, m] = dot(table_ref[...], weights_ref[m]).astype(kind)

    return pl.pallas_call(
        kernel,
        grid_spec=pltpu.PrefetchScalarGridSpec(
            num_scalar_prefetch=1,
            grid=(len(order),),
            in_specs=[
                pl.BlockSpec((vocab, feats), lambda r, where: (0, 0)),
                pl.BlockSpec((3, feats, sub), lambda r, where: (0, 0, where[r])),
            ],
            out_specs=pl.BlockSpec((1, 3, vocab, sub), lambda r, where: (r, 0, 0, 0)),
        ),
        out_shape=jax.ShapeDtypeStruct((len(order), 3, vocab, sub), kind),
        compiler_params=PARAMS,
        name="table_projection",
    )(jnp.stack([ctx ^ r for r in order]), table, weights)


def input_projection(rows_in, pieces, ctx):
    rows, full_width = rows_in.shape
    feats, chans = pieces[0].shape[1:]
    count = len(pieces)
    sub = chans // count

    def kernel(ctx_ref, rows_ref, *refs):
        weights, (normed_ref, proj_ref, scale_ref) = refs[:count], refs[count:]

        @pl.when(pl.program_id(0) == 0)
        def _():
            total = jnp.zeros((rows, 1), F32)
            for q in range(count):
                part = rows_ref[:, q * feats : (q + 1) * feats].astype(F32)
                total = total + jnp.sum(part * part, axis=1, keepdims=True)
            scale_ref[...] = lax.rsqrt(total / full_width + EPSILON)
            for q in range(count):
                part = rows_ref[:, q * feats : (q + 1) * feats].astype(F32)
                normed_ref[q] = (part * scale_ref[...]).astype(BF16)

        total = jnp.zeros((rows, chans), F32)
        for r in range(count):
            start = pl.multiple_of((ctx_ref[0] ^ r) * feats, feats)
            total = total + dot(rows_ref[:, pl.ds(start, feats)], weights[r][0])
        total = (total * scale_ref[...]).astype(BF16)
        for q in range(count):
            proj_ref[q, 0] = total[:, q * sub : (q + 1) * sub]

    return pl.pallas_call(
        kernel,
        grid_spec=pltpu.PrefetchScalarGridSpec(
            num_scalar_prefetch=1,
            grid=(3,),
            in_specs=[pl.BlockSpec((rows, full_width), lambda m, ctx: (0, 0))]
            + [pl.BlockSpec((1, feats, chans), lambda m, ctx: (m, 0, 0))] * count,
            out_specs=[
                pl.BlockSpec((count, rows, feats), lambda m, ctx: (0, 0, 0)),
                pl.BlockSpec((count, 1, rows, sub), lambda m, ctx: (0, m, 0, 0)),
                pl.BlockSpec((rows, 1), lambda m, ctx: (0, 0)),
            ],
        ),
        out_shape=(
            jax.ShapeDtypeStruct((count, rows, feats), BF16),
            jax.ShapeDtypeStruct((count, 3, rows, sub), BF16),
            jax.ShapeDtypeStruct((rows, 1), F32),
        ),
        compiler_params=PARAMS,
        name="input_projection",
    )(ctx[None], rows_in, *pieces)


def input_gradient(gproj, pieces, rows_in, scale, ctx):
    rows, full_width = rows_in.shape
    feats, chans = pieces[0].shape[1:]
    count = len(pieces)
    sub = chans // count
    tile = min(256, feats)
    steps = feats // tile

    def kernel(ctx_ref, gproj_ref, rows_ref, scale_ref, *refs):
        weights, (out_ref, flat, grads) = refs[:count], refs[count:]
        step = pl.program_id(0)

        @pl.when(step == 0)
        def _():
            for m in range(3):
                for q in range(count):
                    flat[m, :, q * sub : (q + 1) * sub] = gproj_ref[q, m]

        columns = pl.ds(pl.multiple_of(step * tile, tile), tile)
        for r in range(count):
            total = dot_t(flat[0], weights[r][0])
            for m in (1, 2):
                total = total + dot_t(flat[m], weights[r][m])
            grads[ctx_ref[0] ^ r, :, columns] = total * scale_ref[...]

        @pl.when(step == steps - 1)
        def _():
            stat = jnp.zeros((rows, 1), F32)
            for q in range(count):
                part = rows_ref[:, q * feats : (q + 1) * feats].astype(F32)
                stat = stat + jnp.sum(part * grads[q], axis=1, keepdims=True)
            stat = stat * scale_ref[...] * scale_ref[...] / full_width
            for q in range(count):
                part = rows_ref[:, q * feats : (q + 1) * feats].astype(F32)
                out_ref[q] = (grads[q] - part * stat).astype(BF16)

    return pl.pallas_call(
        kernel,
        grid_spec=pltpu.PrefetchScalarGridSpec(
            num_scalar_prefetch=1,
            grid=(steps,),
            in_specs=[
                pl.BlockSpec(gproj.shape, lambda t, ctx: (0, 0, 0, 0)),
                pl.BlockSpec((rows, full_width), lambda t, ctx: (0, 0)),
                pl.BlockSpec((rows, 1), lambda t, ctx: (0, 0)),
            ]
            + [pl.BlockSpec((3, tile, chans), lambda t, ctx: (0, t, 0))] * count,
            out_specs=pl.BlockSpec((count, rows, feats), lambda t, ctx: (0, 0, 0)),
            scratch_shapes=[
                pltpu.VMEM((3, rows, chans), BF16),
                pltpu.VMEM((count, rows, feats), F32),
            ],
        ),
        out_shape=jax.ShapeDtypeStruct((count, rows, feats), BF16),
        compiler_params=PARAMS,
        name="input_gradient",
    )(ctx[None], gproj, rows_in, scale, *pieces)


def grad_in_kernel(left, pieces, ctx):
    feats, depth = left.shape
    count, sub = len(pieces), pieces[0].shape[2]
    if sub % 128:
        columns = jnp.concatenate([pick(jnp.stack(pieces), ctx ^ q) for q in range(count)], axis=2)
        return jnp.einsum("dk,mkc->mdc", left, columns, preferred_element_type=F32)

    tile = min(256, feats)

    def kernel(ctx_ref, left_ref, *refs):
        out_ref = refs[count]
        for r in range(count):
            columns = pl.ds(pl.multiple_of((ctx_ref[0] ^ r) * sub, sub), sub)
            for m in range(3):
                out_ref[m, :, columns] = dot(left_ref[...], refs[r][m])

    return pl.pallas_call(
        kernel,
        grid_spec=pltpu.PrefetchScalarGridSpec(
            num_scalar_prefetch=1,
            grid=(feats // tile,),
            in_specs=[pl.BlockSpec((tile, depth), lambda t, ctx: (t, 0))]
            + [pl.BlockSpec((3, depth, sub), lambda t, ctx: (0, 0, 0))] * count,
            out_specs=pl.BlockSpec((3, tile, sub * count), lambda t, ctx: (0, t, 0)),
        ),
        out_shape=jax.ShapeDtypeStruct((3, feats, sub * count), F32),
        compiler_params=PARAMS,
        name="grad_project_in",
    )(ctx[None], left, *pieces)


def grad_out_kernel(pieces, right, ctx):
    depth, feats = right.shape
    count, sub = len(pieces), pieces[0].shape[0]

    def kernel(where_ref, right_ref, *refs):
        out_ref = refs[count]
        for r in range(count):

            @pl.when(pl.program_id(0) == r)
            def _():
                out_ref[...] = dot(refs[r][...], right_ref[...])

    return pl.pallas_call(
        kernel,
        grid_spec=pltpu.PrefetchScalarGridSpec(
            num_scalar_prefetch=1,
            grid=(count,),
            in_specs=[pl.BlockSpec((depth, feats), lambda r, where: (0, 0))]
            + [pl.BlockSpec((sub, depth), lambda r, where: (0, 0))] * count,
            out_specs=pl.BlockSpec((sub, feats), lambda r, where: (where[r], 0)),
        ),
        out_shape=jax.ShapeDtypeStruct((sub * count, feats), F32),
        compiler_params=PARAMS,
        name="grad_project_out",
    )(jnp.stack([ctx ^ r for r in range(count)]), right, *pieces)


def together(*values):
    return lax.optimization_barrier(values)


def output_projection(gated, weights, chunks):
    count, rows, sub = gated.shape
    chans, full_width = weights.shape
    width = full_width // chunks

    def kernel(gated_ref, weights_ref, out_ref, flat):
        @pl.when(pl.program_id(0) == 0)
        def _():
            for q in range(count):
                flat[:, q * sub : (q + 1) * sub] = gated_ref[q]

        out_ref[0] = dot(flat[...], weights_ref[...]).astype(BF16)

    return pl.pallas_call(
        kernel,
        grid=(chunks,),
        in_specs=[
            pl.BlockSpec(gated.shape, lambda q: (0, 0, 0)),
            pl.BlockSpec((chans, width), lambda q: (0, q)),
        ],
        out_specs=pl.BlockSpec((1, rows, width), lambda q: (q, 0, 0)),
        out_shape=jax.ShapeDtypeStruct((chunks, rows, width), BF16),
        scratch_shapes=[pltpu.VMEM((rows, chans), BF16)],
        compiler_params=PARAMS,
        name="output_projection",
    )(gated, weights)


def ctx_swap(value):
    return lax.all_to_all(value, "ctx", split_axis=0, concat_axis=0, tiled=True)


def local(
    token_ids, embedding, project_in, short_taps, filter_taps, decay_rates, project_out, cotangent
):
    n_ctx, n_dp = lax.axis_size("ctx"), lax.axis_size("dp")
    sec, dp, ctx = (lax.axis_index(axis) for axis in ("section", "dp", "ctx"))
    first = sec == 0
    rows, vocab = token_ids.shape[0], embedding.shape[0]
    seq = rows * n_ctx
    weights_in = jnp.transpose(project_in[0], (1, 0, 2))
    weights_out = project_out[0]
    feats, chans = weights_out.shape[1], weights_out.shape[0]
    full_width = feats * n_ctx
    sub = chans // n_ctx

    if n_ctx == n_dp:
        half = vocab // 2
        mine = lax.dynamic_slice_in_dim(embedding, sec * half, half, 0)
        came = []
        for i in range(1, n_dp):
            shifts = (i, i % (n_dp - 1) + 1)
            came.append(
                send(
                    mine,
                    ("section", "dp", "ctx"),
                    lambda s, z, k: (0, (z + shifts[s]) % n_dp, k) if z == k else None,
                )
            )
        offset = (dp - ctx) % n_dp
        low, high = embedding[:half], embedding[half:]
        for i in range(1, n_dp):
            low = jnp.where(offset == i, came[i - 1], low)
            high = jnp.where(offset == i % (n_dp - 1) + 1, came[i - 1], high)
        table = jnp.concatenate([low, high], axis=0)
    else:
        table = lax.dynamic_slice_in_dim(
            lax.all_gather(embedding, "dp", axis=1, tiled=True), ctx * feats, feats, 1
        )
    table_float = embedding.astype(F32)
    shared = jnp.concatenate(
        [jnp.sum(table_float * table_float, axis=1), token_ids.astype(F32)]
    )
    shared = lax.all_gather(shared, ("dp", "ctx"), axis=0)
    table, shared = together(table, shared)
    shared = shared.reshape(n_dp, n_ctx, vocab + rows)
    table_inv = lax.rsqrt(
        jnp.sum(shared[:, 0, :vocab], axis=0)[:, None] / full_width + EPSILON
    )
    tokens = shared[0, :, vocab:].reshape(seq).astype(jnp.int32)

    def own(value):
        return lax.dynamic_slice_in_dim(value, ctx * sub, sub, value.ndim - 1)

    taps = own(short_taps[0]).reshape(9, sub)
    filters = own(filter_taps[0])
    tap_count = filters.shape[0]
    positions = jnp.arange(tap_count).astype(F32)[:, None]
    damping = jnp.exp(-own(decay_rates) * positions / tap_count)
    kern = filters * damping
    matrices = spectra(tap_count)

    vocabulary = jnp.arange(vocab, dtype=jnp.int32)[None, :]
    first_input = dot((token_ids[:, None] == vocabulary).astype(BF16), embedding)

    out_full = lax.all_gather(weights_out, "ctx", axis=1, tiled=True)
    in_far = {0: weights_in}
    bit = n_ctx // 2
    while bit > 1:
        for r in list(in_far):
            in_far[r | bit] = ctx_xor(in_far[r], bit, (1,))
        bit //= 2

    order = scatter_order(n_ctx)
    kept = order[: n_ctx // 2]
    sent = table_projection(table, weights_in, ctx, [r | 1 for r in kept], BF16)
    arrived = ctx_xor(sent, 1, (0,))
    partial = table_projection(table, weights_in, ctx, kept, F32) + arrived.astype(F32)
    bit = 2
    while bit < n_ctx:
        stays, gone = jnp.split(partial, 2, axis=0)
        partial = stays + ctx_xor(gone.astype(BF16), bit, (0,)).astype(F32)
        bit *= 2
    table_proj = (partial[0] * table_inv).astype(BF16)
    gated_0, *saved_0, proj_0 = conv_forward(table_proj, taps, kern, matrices, tokens)
    gated_rows = ctx_swap(gated_0.reshape(n_ctx, rows, sub))
    middle = cross_sum(output_projection(gated_rows, out_full, n_dp), 0)
    middle = (first_input + middle).astype(BF16)

    held = sorted(in_far)[1:]
    middle, *late = together(middle, *[in_far[r] for r in held])
    in_far.update(zip(held, late))
    in_pieces = []
    for r in sorted(in_far):
        in_pieces += [in_far[r], ctx_xor(in_far[r], 1, (1,))]
    middle_all = jnp.concatenate(in_order(dp_gather(middle, 1, 2), dp), axis=1)
    normed, proj_rows, scale = input_projection(middle_all, in_pieces, ctx)
    proj_1 = ctx_swap(proj_rows)
    gated_1, *saved_1 = conv_forward(proj_1, taps, kern, matrices)

    def gated_grad(rows_all):
        total = dot_t(rows_all, out_full).astype(BF16)
        split = jnp.transpose(total.reshape(rows, n_ctx, sub), (1, 0, 2))
        return ctx_swap(split).reshape(seq, sub)

    cot_parts = in_order(dp_gather(cotangent, 1, 1), dp)
    cot_all = jnp.concatenate(cot_parts, axis=1)
    gproj_1, gkern_1, gtaps_1 = conv_backward(
        gated_grad(cot_all), proj_1, taps, kern, matrices, saved_1
    )
    gproj_rows = ctx_swap(gproj_1)
    shares = input_gradient(gproj_rows, in_pieces, middle_all, scale, ctx)
    shares, normed, gproj_1, gated_1 = together(shares, normed, gproj_1, gated_1)
    grad_middle = (cotangent.astype(F32) + cross_sum(shares, 1)).astype(BF16)

    swapped = [pick(normed, ctx)]
    for r in range(1, n_ctx):
        swapped.append(ctx_xor(pick(normed, ctx ^ r), r, (1,)))
    swapped = jnp.stack(swapped)
    normed_cols = jnp.concatenate([pick(swapped, ctx ^ q).T for q in range(n_ctx)], axis=1)
    gproj_all = ctx_gather(gproj_1.transpose(1, 0, 2, 3).reshape(3, seq, sub), (1,))
    gated_all = ctx_gather(jnp.where(first, gated_0, gated_1).T, (0, 1))

    back_stack = dp_gather(grad_middle, 0, 2)
    back_stack, normed_cols, *rest = together(back_stack, normed_cols, *gproj_all, *gated_all)
    gproj_all, gated_all = rest[:n_ctx], rest[n_ctx:]
    back_parts = in_order(back_stack, dp)
    table_grad, gkern_0, gtaps_0 = conv_backward(
        gated_grad(jnp.concatenate(back_parts, axis=1)),
        proj_0, taps, kern, matrices, saved_0, tokens, table_inv,
    )

    if n_ctx == n_dp:
        grads = jnp.stack([jnp.where(first, a, b) for a, b in zip(back_parts, cot_parts)])
    else:
        grads = jnp.where(first, jnp.concatenate(back_parts, axis=1), cot_all)
        grads = jnp.transpose(grads.reshape(rows, n_ctx, feats), (1, 0, 2))
    grad_cols = ctx_swap(grads).reshape(seq, feats)
    grad_out = grad_out_kernel(gated_all, grad_cols, ctx)
    table_all = {0: table_grad}
    bit = n_ctx // 2
    while bit > 1:
        for r in list(table_all):
            table_all[r | bit] = ctx_xor(table_all[r], bit, (0,))
        bit //= 2
    held = sorted(table_all)[1:]
    grad_out, *late = together(grad_out, *[table_all[r] for r in held])
    table_all.update(zip(held, late))
    table_pieces = []
    for r in sorted(table_all):
        table_pieces += [table_all[r], ctx_xor(table_all[r], 1, (0,))]
    grad_in = lax.cond(
        first,
        lambda: grad_in_kernel(table.T, table_pieces, ctx),
        lambda: grad_in_kernel(normed_cols, gproj_all, ctx),
    )

    gkern = jnp.where(first, gkern_0, gkern_1)
    gtaps = jnp.where(first, gtaps_0, gtaps_1)
    gdecay = -jnp.sum(gkern * kern * positions, axis=0, keepdims=True) / tap_count
    small = jnp.concatenate([gkern * damping, gdecay, gtaps], axis=0)
    small = jnp.stack(ctx_gather(small, (0, 1)))
    small = jnp.concatenate([pick(small, ctx ^ q) for q in range(n_ctx)], axis=1)
    return (
        jnp.transpose(grad_in, (1, 0, 2))[None],
        grad_out[None],
        small[:tap_count][None],
        small[tap_count][None],
        small[tap_count + 1 :].reshape(1, 3, 3, chans),
    )


def solution(mesh):
    return jax.shard_map(
        local,
        mesh=mesh,
        in_specs=(
            P("ctx"),
            P(None, "dp"),
            P("section", "ctx", None, "dp"),
            P("section", None, None, "dp"),
            P("section", None, "dp"),
            P("section", "dp"),
            P("section", "dp", "ctx"),
            P("ctx", "dp"),
        ),
        out_specs=(
            P("section", "ctx", None, "dp"),
            P("section", "dp", "ctx"),
            P("section", None, "dp"),
            P("section", "dp"),
            P("section", None, None, "dp"),
        ),
        check_vma=False,
    )
```

```python
import functools

import jax
import jax.numpy as jnp
import numpy as np
from jax import lax
from jax.experimental import pallas as pl
from jax.experimental.pallas import tpu as pltpu
from jax.sharding import PartitionSpec as P

EPSILON = 1e-06
F32 = jnp.float32
BF16 = jnp.bfloat16


def dot(left, right):
    return jnp.dot(left, right, preferred_element_type=F32)


def dot_t(left, right):
    return lax.dot_general(left, right, (((1,), (1,)), ((), ())), preferred_element_type=F32)


def exact(left, right):
    return jnp.dot(left, right, preferred_element_type=F32, precision=lax.Precision.HIGHEST)


def pick(stack, index):
    return lax.dynamic_index_in_dim(stack, index, 0, keepdims=False)


def send(value, axes, route):
    sizes = [lax.axis_size(axis) for axis in axes]
    pairs = []
    for source, place in enumerate(np.ndindex(*sizes)):
        target = route(*place)
        if target is not None:
            pairs.append((source, int(np.ravel_multi_index(target, sizes))))
    return lax.ppermute(value, axes, pairs)


def ctx_xor(value, mask, sections):
    return send(
        value, ("section", "ctx"), lambda s, k: (s, k ^ mask) if s in sections else None
    )


def ctx_gather(value, sections):
    count = lax.axis_size("ctx")
    held = {0: value}
    bit = count // 2
    while bit:
        for r in list(held):
            held[r | bit] = ctx_xor(held[r], bit, sections)
        bit //= 2
    return [held[r] for r in range(count)]


def scatter_order(count):
    if count == 1:
        return [0]
    inner = scatter_order(count // 2)
    return [2 * r for r in inner] + [2 * r + 1 for r in inner]


def dp_gather(value, section):
    count = lax.axis_size("dp")
    pieces = [value]
    for _ in range(count - 1):
        pieces.append(
            send(
                pieces[-1],
                ("section", "dp"),
                lambda s, z: (s, (z + 1) % count) if s == section else None,
            )
        )
    return jnp.stack(pieces)


def cross_gather(shares, base, source, *waiting):
    count = lax.axis_size("dp")
    me = lax.axis_index("dp")
    half = base.shape[0] // 2
    parts = []
    for start in (0, half):
        total = base[start : start + half].astype(F32)
        for shift in range(count):
            arrived = send(
                pick(shares, (me + shift) % count)[start : start + half],
                ("section", "dp"),
                lambda s, z: (1 - s, (z + shift) % count) if s == source else None,
            )
            total = total + arrived.astype(F32)
        part = total.astype(BF16)
        if start == 0:
            part, *waiting = together(part, *waiting)
        parts.append(part)
    stacks = [dp_gather(part, 1 - source) for part in parts]
    return jnp.concatenate(stacks, axis=1), waiting


def in_order(stack, me):
    return [pick(stack, (me - q) % stack.shape[0]) for q in range(stack.shape[0])]


def spectra(taps):
    freq = np.arange(taps)[:, None]
    time = np.arange(taps)[None, :]
    angle = np.pi * freq * time / taps
    nyquist = np.where(time % 2 == 0, 1.0, -1.0)
    forward = np.concatenate(
        [np.cos(angle), np.where(freq == 0, nyquist, -np.sin(angle))], axis=0
    )
    weight = np.where(freq == 0, 1.0, 2.0) / (2 * taps)
    inverse = np.concatenate(
        [weight * np.cos(angle), np.where(freq == 0, nyquist, -2 * np.sin(angle)) * np.where(freq == 0, weight, 1.0 / (2 * taps))],
        axis=0,
    ).T
    sign = np.where(np.arange(2 * taps) % taps % 2 == 0, 1.0, -1.0)
    return [jnp.asarray(m, BF16) for m in (forward, inverse, inverse * sign[None, :])]


def later(current, before, steps, row):
    return jnp.where(row < steps, pltpu.roll(before, steps, 0), pltpu.roll(current, steps, 0))


def sooner(current, after, steps, row):
    count = current.shape[0]
    return jnp.where(
        row >= count - steps,
        pltpu.roll(after, count - steps, 0),
        pltpu.roll(current, count - steps, 0),
    )


def kernel_spectrum(fwd_ref, kern_ref, row):
    tap_count = kern_ref.shape[0]
    kern = dot(fwd_ref[...], kern_ref[...].astype(BF16))
    real, imag = kern[:tap_count], kern[tap_count:]
    return real, jnp.where(row == 0, 0.0, imag), jnp.where(row == 0, imag, real)


def proj_block(proj_ref, m, b, tap_count):
    chunk, start = divmod(b * tap_count, proj_ref.shape[2])
    return proj_ref[chunk, m, start : start + tap_count, :].astype(F32)


def short_filter(taps_ref, m, current, before, row):
    return (
        taps_ref[m : m + 1, :] * current
        + taps_ref[3 + m : 4 + m, :] * later(current, before, 1, row)
        + taps_ref[6 + m : 7 + m, :] * later(current, before, 2, row)
    )


def lookup_kernel(
    tokens_ref, table_ref, taps_ref, kern_ref, fwd_ref, inv_ref,
    gated_ref, filt_ref, spec_ref, proj_ref,
):
    tap_count, vocab = kern_ref.shape[0], table_ref.shape[1]
    entry = lax.broadcasted_iota(jnp.int32, (tap_count, vocab), 1)
    for b in range(filt_ref.shape[0] // tap_count):
        here = pl.ds(b * tap_count, tap_count)
        chosen = (entry == tokens_ref[here, :]).astype(F32).astype(BF16)
        for m in range(3):
            proj_ref[0, m, here, :] = dot(chosen, table_ref[m]).astype(BF16)
    forward_kernel(
        proj_ref, taps_ref, kern_ref, fwd_ref, inv_ref, gated_ref, filt_ref, spec_ref
    )


def collect_kernel(
    tokens_ref, scale_ref, gg_ref, proj_ref, taps_ref, kern_ref, fwd_ref, inv_ref, filt_ref, spec_ref,
    table_ref, gkern_ref, gtaps_ref, grad_spec, gproj_ref,
):
    backward_kernel(
        gg_ref, proj_ref, taps_ref, kern_ref, fwd_ref, inv_ref, filt_ref, spec_ref,
        gproj_ref, gkern_ref, gtaps_ref, grad_spec,
    )
    _, vocab, _ = table_ref.shape
    seq = filt_ref.shape[0]
    entry = lax.broadcasted_iota(jnp.int32, (vocab, seq), 0)
    chosen = (entry == tokens_ref[...]).astype(F32).astype(BF16)
    for m in range(3):
        table_ref[m] = (dot(chosen, gproj_ref[0, m]) * scale_ref[...]).astype(BF16)


def forward_kernel(proj_ref, taps_ref, kern_ref, fwd_ref, inv_ref, gated_ref, filt_ref, spec_ref):
    tap_count, chans = kern_ref.shape
    blocks = filt_ref.shape[0] // tap_count
    row = lax.broadcasted_iota(jnp.int32, (tap_count, chans), 0)
    sign = jnp.where(row % 2 == 0, 1.0, -1.0)
    kr, ki, kn = kernel_spectrum(fwd_ref, kern_ref, row)
    zero = jnp.zeros((tap_count, chans), F32)
    before = [zero] * 3
    last_r, last_i = zero, zero
    for b in range(blocks):
        here = pl.ds(b * tap_count, tap_count)
        streams = []
        for m in range(3):
            current = proj_block(proj_ref, m, b, tap_count)
            streams.append(short_filter(taps_ref, m, current, before[m], row))
            before[m] = current
        part = dot(fwd_ref[...], (streams[1] * streams[2]).astype(BF16))
        pr, pi = part[:tap_count], part[tap_count:]
        wr = last_r + sign * pr
        wi = last_i + sign * pi
        last_r, last_i = pr, pi
        spec_ref[b, :tap_count, :] = wr.astype(BF16)
        spec_ref[b, tap_count:, :] = wi.astype(BF16)
        mixed = jnp.concatenate([wr * kr - wi * ki, wr * ki + wi * kn], axis=0)
        filtered = dot(inv_ref[...], mixed.astype(BF16))
        filt_ref[here, :] = filtered.astype(BF16)
        gated_ref[here, :] = (streams[0] * filtered).astype(BF16)


def backward_kernel(
    gg_ref, proj_ref, taps_ref, kern_ref, fwd_ref, inv_ref, filt_ref, spec_ref,
    gproj_ref, gkern_ref, gtaps_ref, grad_spec,
):
    tap_count, chans = kern_ref.shape
    blocks = filt_ref.shape[0] // tap_count
    row = lax.broadcasted_iota(jnp.int32, (tap_count, chans), 0)
    sign = jnp.where(row % 2 == 0, 1.0, -1.0)
    kr, ki, kn = kernel_spectrum(fwd_ref, kern_ref, row)
    zero = jnp.zeros((tap_count, chans), F32)
    sum_r, sum_i = zero, zero
    last = zero
    for b in range(blocks):
        here = pl.ds(b * tap_count, tap_count)
        current = proj_block(proj_ref, 0, b, tap_count)
        query = short_filter(taps_ref, 0, current, last, row)
        last = current
        part = dot(fwd_ref[...], (gg_ref[here, :].astype(F32) * query).astype(BF16))
        grad_spec[b] = part
        gr, gi = sign * part[:tap_count], sign * part[tap_count:]
        wr = spec_ref[b, :tap_count, :].astype(F32)
        wi = spec_ref[b, tap_count:, :].astype(F32)
        rr, ii = wr * gr, wi * gi
        sum_r = sum_r + jnp.where(row == 0, rr, rr + ii)
        sum_i = sum_i + jnp.where(row == 0, ii, wr * gi - wi * gr)
    gkern_ref[...] = exact(
        inv_ref[...].astype(F32), jnp.concatenate([sum_r, sum_i], axis=0)
    )
    after = [zero] * 3
    next_r, next_i = zero, zero
    sums = [jnp.zeros((1, chans), F32) for _ in range(9)]
    for b in reversed(range(blocks)):
        chunk, start = divmod(b * tap_count, proj_ref.shape[2])
        here = pl.ds(b * tap_count, tap_count)
        gr, gi = grad_spec[b, :tap_count, :], grad_spec[b, tap_count:, :]
        vr, vi = gr + sign * next_r, gi + sign * next_i
        next_r, next_i = gr, gi
        mixed = jnp.concatenate([vr * kr + vi * ki, vi * kn - vr * ki], axis=0)
        grad_prod = dot(inv_ref[...], mixed.astype(BF16))
        shifts, shorts = [], []
        for m in range(3):
            current = proj_block(proj_ref, m, b, tap_count)
            before = proj_block(proj_ref, m, b - 1, tap_count) if b else zero
            shifts.append([current, later(current, before, 1, row), later(current, before, 2, row)])
            if m:
                shorts.append(sum(taps_ref[3 * j + m : 3 * j + m + 1, :] * shifts[m][j] for j in range(3)))
        grads = [
            gg_ref[here, :].astype(F32) * filt_ref[here, :].astype(F32),
            grad_prod * shorts[1],
            grad_prod * shorts[0],
        ]
        for m in range(3):
            grad = grads[m]
            out = (
                taps_ref[m : m + 1, :] * grad
                + taps_ref[3 + m : 4 + m, :] * sooner(grad, after[m], 1, row)
                + taps_ref[6 + m : 7 + m, :] * sooner(grad, after[m], 2, row)
            )
            after[m] = grad
            gproj_ref[chunk, m, start : start + tap_count, :] = out.astype(BF16)
            for j in range(3):
                sums[3 * j + m] = sums[3 * j + m] + jnp.sum(
                    grad * shifts[m][j], axis=0, keepdims=True
                )
    for index in range(9):
        gtaps_ref[index : index + 1, :] = sums[index]


PARAMS = pltpu.CompilerParams(vmem_limit_bytes=56 * 1024 * 1024)


def conv_forward(proj, taps, kern, matrices, tokens=None):
    tap_count, chans = kern.shape
    seq = proj.shape[0] * proj.shape[2] if tokens is None else tokens.shape[0]
    results = [
        jax.ShapeDtypeStruct((seq, chans), BF16),
        jax.ShapeDtypeStruct((seq, chans), BF16),
        jax.ShapeDtypeStruct((seq // tap_count, 2 * tap_count, chans), BF16),
    ]
    operands = (proj, taps, kern, matrices[0], matrices[2])
    if tokens is not None:
        results.append(jax.ShapeDtypeStruct((1, 3, seq, chans), BF16))
        operands = (tokens[:, None], *operands)
    return pl.pallas_call(
        forward_kernel if tokens is None else lookup_kernel,
        out_shape=results,
        compiler_params=PARAMS,
        name="conv_forward",
    )(*operands)


def conv_backward(gg, proj, taps, kern, matrices, saved, tokens=None, scale=None):
    tap_count, chans = kern.shape
    seq = gg.shape[0]
    scratch = [pltpu.VMEM((seq // tap_count, 2 * tap_count, chans), F32)]
    operands = (gg, proj, taps, kern, matrices[0], matrices[1], *saved)
    first = jax.ShapeDtypeStruct(proj.shape, BF16)
    if tokens is not None:
        first = jax.ShapeDtypeStruct((3, scale.shape[0], chans), BF16)
        scratch.append(pltpu.VMEM(proj.shape, BF16))
        operands = (tokens[None, :], scale, *operands)
    return pl.pallas_call(
        backward_kernel if tokens is None else collect_kernel,
        out_shape=(
            first,
            jax.ShapeDtypeStruct(kern.shape, F32),
            jax.ShapeDtypeStruct((9, chans), F32),
        ),
        scratch_shapes=scratch,
        compiler_params=PARAMS,
        name="conv_backward",
    )(*operands)


def table_projection(table, weights, ctx, order, kind):
    vocab, feats = table.shape
    sub = weights.shape[2] // lax.axis_size("ctx")
    if sub % 128:
        columns = jnp.stack(
            [lax.dynamic_slice_in_dim(weights, (ctx ^ r) * sub, sub, 2) for r in order]
        )
        return jnp.einsum("vd,rmdc->rmvc", table, columns, preferred_element_type=F32).astype(kind)

    def kernel(where_ref, table_ref, weights_ref, out_ref):
        for m in range(3):
            out_ref[0, m] = dot(table_ref[...], weights_ref[m]).astype(kind)

    return pl.pallas_call(
        kernel,
        grid_spec=pltpu.PrefetchScalarGridSpec(
            num_scalar_prefetch=1,
            grid=(len(order),),
            in_specs=[
                pl.BlockSpec((vocab, feats), lambda r, where: (0, 0)),
                pl.BlockSpec((3, feats, sub), lambda r, where: (0, 0, where[r])),
            ],
            out_specs=pl.BlockSpec((1, 3, vocab, sub), lambda r, where: (r, 0, 0, 0)),
        ),
        out_shape=jax.ShapeDtypeStruct((len(order), 3, vocab, sub), kind),
        compiler_params=PARAMS,
        name="table_projection",
    )(jnp.stack([ctx ^ r for r in order]), table, weights)


def input_projection(rows_in, pieces, ctx):
    rows, full_width = rows_in.shape
    feats, chans = pieces[0].shape[1:]
    count = len(pieces)
    sub = chans // count

    def kernel(ctx_ref, rows_ref, *refs):
        weights, (normed_ref, proj_ref, scale_ref) = refs[:count], refs[count:]

        @pl.when(pl.program_id(0) == 0)
        def _():
            total = jnp.zeros((rows, 1), F32)
            for q in range(count):
                part = rows_ref[:, q * feats : (q + 1) * feats].astype(F32)
                total = total + jnp.sum(part * part, axis=1, keepdims=True)
            scale_ref[...] = lax.rsqrt(total / full_width + EPSILON)
            for q in range(count):
                part = rows_ref[:, q * feats : (q + 1) * feats].astype(F32)
                normed_ref[q] = (part * scale_ref[...]).astype(BF16)

        total = jnp.zeros((rows, chans), F32)
        for r in range(count):
            start = pl.multiple_of((ctx_ref[0] ^ r) * feats, feats)
            total = total + dot(rows_ref[:, pl.ds(start, feats)], weights[r][0])
        total = (total * scale_ref[...]).astype(BF16)
        for q in range(count):
            proj_ref[q, 0] = total[:, q * sub : (q + 1) * sub]

    return pl.pallas_call(
        kernel,
        grid_spec=pltpu.PrefetchScalarGridSpec(
            num_scalar_prefetch=1,
            grid=(3,),
            in_specs=[pl.BlockSpec((rows, full_width), lambda m, ctx: (0, 0))]
            + [pl.BlockSpec((1, feats, chans), lambda m, ctx: (m, 0, 0))] * count,
            out_specs=[
                pl.BlockSpec((count, rows, feats), lambda m, ctx: (0, 0, 0)),
                pl.BlockSpec((count, 1, rows, sub), lambda m, ctx: (0, m, 0, 0)),
                pl.BlockSpec((rows, 1), lambda m, ctx: (0, 0)),
            ],
        ),
        out_shape=(
            jax.ShapeDtypeStruct((count, rows, feats), BF16),
            jax.ShapeDtypeStruct((count, 3, rows, sub), BF16),
            jax.ShapeDtypeStruct((rows, 1), F32),
        ),
        compiler_params=PARAMS,
        name="input_projection",
    )(ctx[None], rows_in, *pieces)


def input_gradient(gproj, pieces, rows_in, scale, ctx):
    rows, full_width = rows_in.shape
    feats, chans = pieces[0].shape[1:]
    count = len(pieces)
    sub = chans // count
    tile = min(256, feats)
    steps = feats // tile

    def kernel(ctx_ref, gproj_ref, rows_ref, scale_ref, *refs):
        weights, (out_ref, flat, grads) = refs[:count], refs[count:]
        step = pl.program_id(0)

        @pl.when(step == 0)
        def _():
            for m in range(3):
                for q in range(count):
                    flat[m, :, q * sub : (q + 1) * sub] = gproj_ref[q, m]

        columns = pl.ds(pl.multiple_of(step * tile, tile), tile)
        for r in range(count):
            total = dot_t(flat[0], weights[r][0])
            for m in (1, 2):
                total = total + dot_t(flat[m], weights[r][m])
            grads[ctx_ref[0] ^ r, :, columns] = total * scale_ref[...]

        @pl.when(step == steps - 1)
        def _():
            stat = jnp.zeros((rows, 1), F32)
            for q in range(count):
                part = rows_ref[:, q * feats : (q + 1) * feats].astype(F32)
                stat = stat + jnp.sum(part * grads[q], axis=1, keepdims=True)
            stat = stat * scale_ref[...] * scale_ref[...] / full_width
            for q in range(count):
                part = rows_ref[:, q * feats : (q + 1) * feats].astype(F32)
                out_ref[q] = (grads[q] - part * stat).astype(BF16)

    return pl.pallas_call(
        kernel,
        grid_spec=pltpu.PrefetchScalarGridSpec(
            num_scalar_prefetch=1,
            grid=(steps,),
            in_specs=[
                pl.BlockSpec(gproj.shape, lambda t, ctx: (0, 0, 0, 0)),
                pl.BlockSpec((rows, full_width), lambda t, ctx: (0, 0)),
                pl.BlockSpec((rows, 1), lambda t, ctx: (0, 0)),
            ]
            + [pl.BlockSpec((3, tile, chans), lambda t, ctx: (0, t, 0))] * count,
            out_specs=pl.BlockSpec((count, rows, feats), lambda t, ctx: (0, 0, 0)),
            scratch_shapes=[
                pltpu.VMEM((3, rows, chans), BF16),
                pltpu.VMEM((count, rows, feats), F32),
            ],
        ),
        out_shape=jax.ShapeDtypeStruct((count, rows, feats), BF16),
        compiler_params=PARAMS,
        name="input_gradient",
    )(ctx[None], gproj, rows_in, scale, *pieces)


def grad_in_kernel(left, pieces, ctx):
    feats, depth = left.shape
    count, sub = len(pieces), pieces[0].shape[2]
    if sub % 128:
        columns = jnp.concatenate([pick(jnp.stack(pieces), ctx ^ q) for q in range(count)], axis=2)
        return jnp.einsum("dk,mkc->mdc", left, columns, preferred_element_type=F32)

    tile = min(256, feats)

    def kernel(ctx_ref, left_ref, *refs):
        out_ref = refs[count]
        for r in range(count):
            columns = pl.ds(pl.multiple_of((ctx_ref[0] ^ r) * sub, sub), sub)
            for m in range(3):
                out_ref[m, :, columns] = dot(left_ref[...], refs[r][m])

    return pl.pallas_call(
        kernel,
        grid_spec=pltpu.PrefetchScalarGridSpec(
            num_scalar_prefetch=1,
            grid=(feats // tile,),
            in_specs=[pl.BlockSpec((tile, depth), lambda t, ctx: (t, 0))]
            + [pl.BlockSpec((3, depth, sub), lambda t, ctx: (0, 0, 0))] * count,
            out_specs=pl.BlockSpec((3, tile, sub * count), lambda t, ctx: (0, t, 0)),
        ),
        out_shape=jax.ShapeDtypeStruct((3, feats, sub * count), F32),
        compiler_params=PARAMS,
        name="grad_project_in",
    )(ctx[None], left, *pieces)


def grad_out_kernel(pieces, right, ctx):
    depth, feats = right.shape
    count, sub = len(pieces), pieces[0].shape[0]

    def kernel(where_ref, right_ref, *refs):
        out_ref = refs[count]
        for r in range(count):

            @pl.when(pl.program_id(0) == r)
            def _():
                out_ref[...] = dot(refs[r][...], right_ref[...])

    return pl.pallas_call(
        kernel,
        grid_spec=pltpu.PrefetchScalarGridSpec(
            num_scalar_prefetch=1,
            grid=(count,),
            in_specs=[pl.BlockSpec((depth, feats), lambda r, where: (0, 0))]
            + [pl.BlockSpec((sub, depth), lambda r, where: (0, 0))] * count,
            out_specs=pl.BlockSpec((sub, feats), lambda r, where: (where[r], 0)),
        ),
        out_shape=jax.ShapeDtypeStruct((sub * count, feats), F32),
        compiler_params=PARAMS,
        name="grad_project_out",
    )(jnp.stack([ctx ^ r for r in range(count)]), right, *pieces)


def together(*values):
    return lax.optimization_barrier(values)


def output_projection(gated, weights, chunks):
    count, rows, sub = gated.shape
    chans, full_width = weights.shape
    width = full_width // chunks

    def kernel(gated_ref, weights_ref, out_ref, flat):
        @pl.when(pl.program_id(0) == 0)
        def _():
            for q in range(count):
                flat[:, q * sub : (q + 1) * sub] = gated_ref[q]

        out_ref[0] = dot(flat[...], weights_ref[...]).astype(BF16)

    return pl.pallas_call(
        kernel,
        grid=(chunks,),
        in_specs=[
            pl.BlockSpec(gated.shape, lambda q: (0, 0, 0)),
            pl.BlockSpec((chans, width), lambda q: (0, q)),
        ],
        out_specs=pl.BlockSpec((1, rows, width), lambda q: (q, 0, 0)),
        out_shape=jax.ShapeDtypeStruct((chunks, rows, width), BF16),
        scratch_shapes=[pltpu.VMEM((rows, chans), BF16)],
        compiler_params=PARAMS,
        name="output_projection",
    )(gated, weights)


def ctx_swap_in(value, section):
    me = lax.axis_index("ctx")
    count = value.shape[0]
    came = [pick(value, me)]
    for r in range(1, count):
        came.append(ctx_xor(pick(value, me ^ r), r, (section,)))
    came = jnp.stack(came)
    return [pick(came, me ^ q) for q in range(count)]


def ctx_swap(value):
    return lax.all_to_all(value, "ctx", split_axis=0, concat_axis=0, tiled=True)


def local(
    token_ids, embedding, project_in, short_taps, filter_taps, decay_rates, project_out, cotangent
):
    n_ctx, n_dp = lax.axis_size("ctx"), lax.axis_size("dp")
    sec, dp, ctx = (lax.axis_index(axis) for axis in ("section", "dp", "ctx"))
    first = sec == 0
    rows, vocab = token_ids.shape[0], embedding.shape[0]
    seq = rows * n_ctx
    weights_in = jnp.transpose(project_in[0], (1, 0, 2))
    weights_out = project_out[0]
    feats, chans = weights_out.shape[1], weights_out.shape[0]
    full_width = feats * n_ctx
    sub = chans // n_ctx

    if n_ctx == n_dp:
        half = vocab // 2
        mine = lax.dynamic_slice_in_dim(embedding, sec * half, half, 0)
        came = []
        for i in range(1, n_dp):
            shifts = (i, i % (n_dp - 1) + 1)
            came.append(
                send(
                    mine,
                    ("section", "dp", "ctx"),
                    lambda s, z, k: (0, (z + shifts[s]) % n_dp, k) if z == k else None,
                )
            )
        offset = (dp - ctx) % n_dp
        low, high = embedding[:half], embedding[half:]
        for i in range(1, n_dp):
            low = jnp.where(offset == i, came[i - 1], low)
            high = jnp.where(offset == i % (n_dp - 1) + 1, came[i - 1], high)
        table = jnp.concatenate([low, high], axis=0)
    else:
        table = lax.dynamic_slice_in_dim(
            lax.all_gather(embedding, "dp", axis=1, tiled=True), ctx * feats, feats, 1
        )
    table_float = table.astype(F32)
    squares = jnp.sum(table_float * table_float, axis=1)
    tokens = token_ids.astype(F32)[None]
    held = [0]
    bit = n_ctx // 2
    while bit:
        came = ctx_xor(jnp.concatenate([squares, tokens.reshape(-1)]), bit, (0,))
        squares = squares + came[:vocab]
        tokens = jnp.concatenate([tokens, came[vocab:].reshape(-1, rows)], axis=0)
        held += [r | bit for r in held]
        bit //= 2
    table_inv = lax.rsqrt(squares[:, None] / full_width + EPSILON)
    tokens = jnp.stack([tokens[held.index(r)] for r in range(n_ctx)])
    tokens = jnp.concatenate([pick(tokens, ctx ^ q) for q in range(n_ctx)]).astype(jnp.int32)

    def own(value):
        return lax.dynamic_slice_in_dim(value, ctx * sub, sub, value.ndim - 1)

    taps = own(short_taps[0]).reshape(9, sub)
    filters = own(filter_taps[0])
    tap_count = filters.shape[0]
    positions = jnp.arange(tap_count).astype(F32)[:, None]
    damping = jnp.exp(-own(decay_rates) * positions / tap_count)
    kern = filters * damping
    matrices = spectra(tap_count)

    vocabulary = jnp.arange(vocab, dtype=jnp.int32)[None, :]
    first_input = dot((token_ids[:, None] == vocabulary).astype(BF16), embedding)

    out_full = lax.all_gather(weights_out, "ctx", axis=1, tiled=True)
    in_far = {0: weights_in}
    bit = n_ctx // 2
    while bit > 1:
        for r in list(in_far):
            in_far[r | bit] = ctx_xor(in_far[r], bit, (1,))
        bit //= 2

    order = scatter_order(n_ctx)
    kept = order[: n_ctx // 2]
    sent = table_projection(table, weights_in, ctx, [r | 1 for r in kept], BF16)
    arrived = ctx_xor(sent, 1, (0,))
    partial = table_projection(table, weights_in, ctx, kept, F32) + arrived.astype(F32)
    bit = 2
    while bit < n_ctx:
        stays, gone = jnp.split(partial, 2, axis=0)
        partial = stays + ctx_xor(gone.astype(BF16), bit, (0,)).astype(F32)
        bit *= 2
    table_proj = (partial[0] * table_inv).astype(BF16)
    gated_0, *saved_0, proj_0 = conv_forward(table_proj, taps, kern, matrices, tokens)
    cot_stack = dp_gather(cotangent, 1)
    gated_0, cot_stack = together(gated_0, cot_stack)
    gated_rows = jnp.stack(ctx_swap_in(gated_0.reshape(n_ctx, rows, sub), 0))
    shares = output_projection(gated_rows, out_full, n_dp)
    held = sorted(in_far)[1:]
    middle_stack, late = cross_gather(shares, first_input, 0, *[in_far[r] for r in held])

    in_far.update(zip(held, late))
    in_pieces = []
    for r in sorted(in_far):
        in_pieces += [in_far[r], ctx_xor(in_far[r], 1, (1,))]
    middle_all = jnp.concatenate(in_order(middle_stack, dp), axis=1)
    normed, proj_rows, scale = input_projection(middle_all, in_pieces, ctx)
    proj_1 = ctx_swap(proj_rows)
    gated_1, *saved_1 = conv_forward(proj_1, taps, kern, matrices)

    def gated_grad(rows_all):
        total = dot_t(rows_all, out_full).astype(BF16)
        split = jnp.transpose(total.reshape(rows, n_ctx, sub), (1, 0, 2))
        return ctx_swap(split).reshape(seq, sub)

    cot_parts = in_order(cot_stack, dp)
    cot_all = jnp.concatenate(cot_parts, axis=1)
    gproj_1, gkern_1, gtaps_1 = conv_backward(
        gated_grad(cot_all), proj_1, taps, kern, matrices, saved_1
    )
    gproj_rows = ctx_swap(gproj_1)
    shares = input_gradient(gproj_rows, in_pieces, middle_all, scale, ctx)
    back_stack, late = cross_gather(shares, cotangent, 1, normed, gproj_1, gated_1)
    normed, gproj_1, gated_1 = late

    normed_cols = jnp.concatenate([part.T for part in ctx_swap_in(normed, 1)], axis=1)
    gproj_all = ctx_gather(gproj_1.transpose(1, 0, 2, 3).reshape(3, seq, sub), (1,))
    gated_all = ctx_gather(jnp.where(first, gated_0, gated_1).T, (0, 1))

    back_stack, normed_cols, *rest = together(back_stack, normed_cols, *gproj_all, *gated_all)
    gproj_all, gated_all = rest[:n_ctx], rest[n_ctx:]
    back_parts = in_order(back_stack, dp)
    table_grad, gkern_0, gtaps_0 = conv_backward(
        gated_grad(jnp.concatenate(back_parts, axis=1)),
        proj_0, taps, kern, matrices, saved_0, tokens, table_inv,
    )

    if n_ctx == n_dp:
        grads = jnp.stack([jnp.where(first, a, b) for a, b in zip(back_parts, cot_parts)])
    else:
        grads = jnp.where(first, jnp.concatenate(back_parts, axis=1), cot_all)
        grads = jnp.transpose(grads.reshape(rows, n_ctx, feats), (1, 0, 2))
    grad_cols = ctx_swap(grads).reshape(seq, feats)
    grad_out = grad_out_kernel(gated_all, grad_cols, ctx)
    table_all = {0: table_grad}
    bit = n_ctx // 2
    while bit > 1:
        for r in list(table_all):
            table_all[r | bit] = ctx_xor(table_all[r], bit, (0,))
        bit //= 2
    held = sorted(table_all)[1:]
    grad_out, *late = together(grad_out, *[table_all[r] for r in held])
    table_all.update(zip(held, late))
    table_pieces = []
    for r in sorted(table_all):
        table_pieces += [table_all[r], ctx_xor(table_all[r], 1, (0,))]
    grad_in = lax.cond(
        first,
        lambda: grad_in_kernel(table.T, table_pieces, ctx),
        lambda: grad_in_kernel(normed_cols, gproj_all, ctx),
    )

    gkern = jnp.where(first, gkern_0, gkern_1)
    gtaps = jnp.where(first, gtaps_0, gtaps_1)
    gdecay = -jnp.sum(gkern * kern * positions, axis=0, keepdims=True) / tap_count
    small = jnp.concatenate([gkern * damping, gdecay, gtaps], axis=0)
    small = jnp.stack(ctx_gather(small, (0, 1)))
    small = jnp.concatenate([pick(small, ctx ^ q) for q in range(n_ctx)], axis=1)
    return (
        jnp.transpose(grad_in, (1, 0, 2))[None],
        grad_out[None],
        small[:tap_count][None],
        small[tap_count][None],
        small[tap_count + 1 :].reshape(1, 3, 3, chans),
    )


def solution(mesh):
    return jax.shard_map(
        local,
        mesh=mesh,
        in_specs=(
            P("ctx"),
            P(None, "dp"),
            P("section", "ctx", None, "dp"),
            P("section", None, None, "dp"),
            P("section", None, "dp"),
            P("section", "dp"),
            P("section", "dp", "ctx"),
            P("ctx", "dp"),
        ),
        out_specs=(
            P("section", "ctx", None, "dp"),
            P("section", "dp", "ctx"),
            P("section", None, "dp"),
            P("section", "dp"),
            P("section", None, None, "dp"),
        ),
        check_vma=False,
    )
```

```python
import functools

import jax
import jax.numpy as jnp
import numpy as np
from jax import lax
from jax.experimental import pallas as pl
from jax.experimental.pallas import tpu as pltpu
from jax.sharding import PartitionSpec as P

EPSILON = 1e-06
F32 = jnp.float32
BF16 = jnp.bfloat16


def dot(left, right):
    return jnp.dot(left, right, preferred_element_type=F32)


def dot_t(left, right):
    return lax.dot_general(left, right, (((1,), (1,)), ((), ())), preferred_element_type=F32)


def exact(left, right):
    return jnp.dot(left, right, preferred_element_type=F32, precision=lax.Precision.HIGHEST)


def pick(stack, index):
    return lax.dynamic_index_in_dim(stack, index, 0, keepdims=False)


def send(value, axes, route):
    sizes = [lax.axis_size(axis) for axis in axes]
    pairs = []
    for source, place in enumerate(np.ndindex(*sizes)):
        target = route(*place)
        if target is not None:
            pairs.append((source, int(np.ravel_multi_index(target, sizes))))
    return lax.ppermute(value, axes, pairs)


def ctx_xor(value, mask, sections):
    return send(
        value, ("section", "ctx"), lambda s, k: (s, k ^ mask) if s in sections else None
    )


def ctx_gather(value, sections):
    count = lax.axis_size("ctx")
    held = {0: value}
    bit = count // 2
    while bit:
        for r in list(held):
            held[r | bit] = ctx_xor(held[r], bit, sections)
        bit //= 2
    return [held[r] for r in range(count)]


def far_gather(value, sections):
    held = {0: value}
    bit = lax.axis_size("ctx") // 2
    while bit > 1:
        for r in list(held):
            held[r | bit] = ctx_xor(held[r], bit, sections)
        bit //= 2
    return held


def scatter_order(count):
    if count == 1:
        return [0]
    inner = scatter_order(count // 2)
    return [2 * r for r in inner] + [2 * r + 1 for r in inner]


def dp_gather(value, section):
    count = lax.axis_size("dp")
    pieces = [value]
    for _ in range(count - 1):
        pieces.append(
            send(
                pieces[-1],
                ("section", "dp"),
                lambda s, z: (s, (z + 1) % count) if s == section else None,
            )
        )
    return pieces


def cross_gather(shares, base, source, early, late=()):
    count = lax.axis_size("dp")
    me = lax.axis_index("dp")
    half = base.shape[0] // 2
    arrivals = [
        [
            send(
                pick(shares, (me + shift) % count)[start : start + half],
                ("section", "dp"),
                lambda s, z: (1 - s, (z + shift) % count) if s == source else None,
            )
            for shift in range(count)
        ]
        for start in (0, half)
    ]

    def total(index, values):
        start = index * half
        result = base[start : start + half].astype(F32)
        for value in values:
            result = result + value.astype(F32)
        return result.astype(BF16)

    part, *early = together(total(0, arrivals[0]), *early)
    first = dp_gather(part, 1 - source)
    first[1], *arrivals[1] = together(first[1], *arrivals[1])
    part, *late = together(total(1, arrivals[1]), *late)
    second = dp_gather(part, 1 - source)
    stack = jnp.stack([jnp.concatenate(pair, axis=0) for pair in zip(first, second)])
    return stack, early, late


def in_order(stack, me):
    return [pick(stack, (me - q) % stack.shape[0]) for q in range(stack.shape[0])]


def spectra(taps):
    freq = np.arange(taps)[:, None]
    time = np.arange(taps)[None, :]
    angle = np.pi * freq * time / taps
    nyquist = np.where(time % 2 == 0, 1.0, -1.0)
    forward = np.concatenate(
        [np.cos(angle), np.where(freq == 0, nyquist, -np.sin(angle))], axis=0
    )
    weight = np.where(freq == 0, 1.0, 2.0) / (2 * taps)
    inverse = np.concatenate(
        [weight * np.cos(angle), np.where(freq == 0, nyquist, -2 * np.sin(angle)) * np.where(freq == 0, weight, 1.0 / (2 * taps))],
        axis=0,
    ).T
    sign = np.where(np.arange(2 * taps) % taps % 2 == 0, 1.0, -1.0)
    return [jnp.asarray(m, BF16) for m in (forward, inverse, inverse * sign[None, :])]


def later(current, before, steps, row):
    return jnp.where(row < steps, pltpu.roll(before, steps, 0), pltpu.roll(current, steps, 0))


def sooner(current, after, steps, row):
    count = current.shape[0]
    return jnp.where(
        row >= count - steps,
        pltpu.roll(after, count - steps, 0),
        pltpu.roll(current, count - steps, 0),
    )


def kernel_spectrum(fwd_ref, kern_ref, row):
    tap_count = kern_ref.shape[0]
    kern = dot(fwd_ref[...], kern_ref[...].astype(BF16))
    real, imag = kern[:tap_count], kern[tap_count:]
    return real, jnp.where(row == 0, 0.0, imag), jnp.where(row == 0, imag, real)


def proj_block(proj_ref, m, b, tap_count):
    chunk, start = divmod(b * tap_count, proj_ref.shape[2])
    return proj_ref[chunk, m, start : start + tap_count, :].astype(F32)


def short_filter(taps_ref, m, current, before, row):
    return (
        taps_ref[m : m + 1, :] * current
        + taps_ref[3 + m : 4 + m, :] * later(current, before, 1, row)
        + taps_ref[6 + m : 7 + m, :] * later(current, before, 2, row)
    )


def lookup_kernel(
    tokens_ref, table_ref, taps_ref, kern_ref, fwd_ref, inv_ref,
    gated_ref, filt_ref, spec_ref, proj_ref,
):
    tap_count, vocab = kern_ref.shape[0], table_ref.shape[1]
    entry = lax.broadcasted_iota(jnp.int32, (tap_count, vocab), 1)
    for b in range(filt_ref.shape[0] // tap_count):
        here = pl.ds(b * tap_count, tap_count)
        chosen = (entry == tokens_ref[here, :]).astype(F32).astype(BF16)
        for m in range(3):
            proj_ref[0, m, here, :] = dot(chosen, table_ref[m]).astype(BF16)
    forward_kernel(
        proj_ref, taps_ref, kern_ref, fwd_ref, inv_ref, gated_ref, filt_ref, spec_ref
    )


def collect_kernel(
    tokens_ref, scale_ref, gg_ref, proj_ref, taps_ref, kern_ref, fwd_ref, inv_ref, filt_ref, spec_ref,
    table_ref, gkern_ref, gtaps_ref, grad_spec, gproj_ref,
):
    backward_kernel(
        gg_ref, proj_ref, taps_ref, kern_ref, fwd_ref, inv_ref, filt_ref, spec_ref,
        gproj_ref, gkern_ref, gtaps_ref, grad_spec,
    )
    _, vocab, _ = table_ref.shape
    seq = filt_ref.shape[0]
    entry = lax.broadcasted_iota(jnp.int32, (vocab, seq), 0)
    chosen = (entry == tokens_ref[...]).astype(F32).astype(BF16)
    for m in range(3):
        table_ref[m] = (dot(chosen, gproj_ref[0, m]) * scale_ref[...]).astype(BF16)


def forward_kernel(proj_ref, taps_ref, kern_ref, fwd_ref, inv_ref, gated_ref, filt_ref, spec_ref):
    tap_count, chans = kern_ref.shape
    blocks = filt_ref.shape[0] // tap_count
    row = lax.broadcasted_iota(jnp.int32, (tap_count, chans), 0)
    sign = jnp.where(row % 2 == 0, 1.0, -1.0)
    kr, ki, kn = kernel_spectrum(fwd_ref, kern_ref, row)
    zero = jnp.zeros((tap_count, chans), F32)
    before = [zero] * 3
    last_r, last_i = zero, zero
    for b in range(blocks):
        here = pl.ds(b * tap_count, tap_count)
        streams = []
        for m in range(3):
            current = proj_block(proj_ref, m, b, tap_count)
            streams.append(short_filter(taps_ref, m, current, before[m], row))
            before[m] = current
        part = dot(fwd_ref[...], (streams[1] * streams[2]).astype(BF16))
        pr, pi = part[:tap_count], part[tap_count:]
        wr = last_r + sign * pr
        wi = last_i + sign * pi
        last_r, last_i = pr, pi
        spec_ref[b, :tap_count, :] = wr.astype(BF16)
        spec_ref[b, tap_count:, :] = wi.astype(BF16)
        mixed = jnp.concatenate([wr * kr - wi * ki, wr * ki + wi * kn], axis=0)
        filtered = dot(inv_ref[...], mixed.astype(BF16))
        filt_ref[here, :] = filtered.astype(BF16)
        gated_ref[here, :] = (streams[0] * filtered).astype(BF16)


def backward_kernel(
    gg_ref, proj_ref, taps_ref, kern_ref, fwd_ref, inv_ref, filt_ref, spec_ref,
    gproj_ref, gkern_ref, gtaps_ref, grad_spec,
):
    tap_count, chans = kern_ref.shape
    blocks = filt_ref.shape[0] // tap_count
    row = lax.broadcasted_iota(jnp.int32, (tap_count, chans), 0)
    sign = jnp.where(row % 2 == 0, 1.0, -1.0)
    kr, ki, kn = kernel_spectrum(fwd_ref, kern_ref, row)
    zero = jnp.zeros((tap_count, chans), F32)
    sum_r, sum_i = zero, zero
    last = zero
    for b in range(blocks):
        here = pl.ds(b * tap_count, tap_count)
        current = proj_block(proj_ref, 0, b, tap_count)
        query = short_filter(taps_ref, 0, current, last, row)
        last = current
        part = dot(fwd_ref[...], (gg_ref[here, :].astype(F32) * query).astype(BF16))
        grad_spec[b] = part
        gr, gi = sign * part[:tap_count], sign * part[tap_count:]
        wr = spec_ref[b, :tap_count, :].astype(F32)
        wi = spec_ref[b, tap_count:, :].astype(F32)
        rr, ii = wr * gr, wi * gi
        sum_r = sum_r + jnp.where(row == 0, rr, rr + ii)
        sum_i = sum_i + jnp.where(row == 0, ii, wr * gi - wi * gr)
    gkern_ref[...] = exact(
        inv_ref[...].astype(F32), jnp.concatenate([sum_r, sum_i], axis=0)
    )
    after = [zero] * 3
    next_r, next_i = zero, zero
    sums = [jnp.zeros((1, chans), F32) for _ in range(9)]
    for b in reversed(range(blocks)):
        chunk, start = divmod(b * tap_count, proj_ref.shape[2])
        here = pl.ds(b * tap_count, tap_count)
        gr, gi = grad_spec[b, :tap_count, :], grad_spec[b, tap_count:, :]
        vr, vi = gr + sign * next_r, gi + sign * next_i
        next_r, next_i = gr, gi
        mixed = jnp.concatenate([vr * kr + vi * ki, vi * kn - vr * ki], axis=0)
        grad_prod = dot(inv_ref[...], mixed.astype(BF16))
        shifts, shorts = [], []
        for m in range(3):
            current = proj_block(proj_ref, m, b, tap_count)
            before = proj_block(proj_ref, m, b - 1, tap_count) if b else zero
            shifts.append([current, later(current, before, 1, row), later(current, before, 2, row)])
            if m:
                shorts.append(sum(taps_ref[3 * j + m : 3 * j + m + 1, :] * shifts[m][j] for j in range(3)))
        grads = [
            gg_ref[here, :].astype(F32) * filt_ref[here, :].astype(F32),
            grad_prod * shorts[1],
            grad_prod * shorts[0],
        ]
        for m in range(3):
            grad = grads[m]
            out = (
                taps_ref[m : m + 1, :] * grad
                + taps_ref[3 + m : 4 + m, :] * sooner(grad, after[m], 1, row)
                + taps_ref[6 + m : 7 + m, :] * sooner(grad, after[m], 2, row)
            )
            after[m] = grad
            gproj_ref[chunk, m, start : start + tap_count, :] = out.astype(BF16)
            for j in range(3):
                sums[3 * j + m] = sums[3 * j + m] + jnp.sum(
                    grad * shifts[m][j], axis=0, keepdims=True
                )
    for index in range(9):
        gtaps_ref[index : index + 1, :] = sums[index]


PARAMS = pltpu.CompilerParams(vmem_limit_bytes=56 * 1024 * 1024)


def conv_forward(proj, taps, kern, matrices, tokens=None):
    tap_count, chans = kern.shape
    seq = proj.shape[0] * proj.shape[2] if tokens is None else tokens.shape[0]
    results = [
        jax.ShapeDtypeStruct((seq, chans), BF16),
        jax.ShapeDtypeStruct((seq, chans), BF16),
        jax.ShapeDtypeStruct((seq // tap_count, 2 * tap_count, chans), BF16),
    ]
    operands = (proj, taps, kern, matrices[0], matrices[2])
    if tokens is not None:
        results.append(jax.ShapeDtypeStruct((1, 3, seq, chans), BF16))
        operands = (tokens[:, None], *operands)
    return pl.pallas_call(
        forward_kernel if tokens is None else lookup_kernel,
        out_shape=results,
        compiler_params=PARAMS,
        name="conv_forward",
    )(*operands)


def conv_backward(gg, proj, taps, kern, matrices, saved, tokens=None, scale=None):
    tap_count, chans = kern.shape
    seq = gg.shape[0]
    scratch = [pltpu.VMEM((seq // tap_count, 2 * tap_count, chans), F32)]
    operands = (gg, proj, taps, kern, matrices[0], matrices[1], *saved)
    first = jax.ShapeDtypeStruct(proj.shape, BF16)
    if tokens is not None:
        first = jax.ShapeDtypeStruct((3, scale.shape[0], chans), BF16)
        scratch.append(pltpu.VMEM(proj.shape, BF16))
        operands = (tokens[None, :], scale, *operands)
    return pl.pallas_call(
        backward_kernel if tokens is None else collect_kernel,
        out_shape=(
            first,
            jax.ShapeDtypeStruct(kern.shape, F32),
            jax.ShapeDtypeStruct((9, chans), F32),
        ),
        scratch_shapes=scratch,
        compiler_params=PARAMS,
        name="conv_backward",
    )(*operands)


def table_projection(table, weights, ctx, order, kind):
    vocab, feats = table.shape
    sub = weights.shape[2] // lax.axis_size("ctx")
    if sub % 128:
        columns = jnp.stack(
            [lax.dynamic_slice_in_dim(weights, (ctx ^ r) * sub, sub, 2) for r in order]
        )
        return jnp.einsum("vd,rmdc->rmvc", table, columns, preferred_element_type=F32).astype(kind)

    def kernel(where_ref, table_ref, weights_ref, out_ref):
        for m in range(3):
            out_ref[0, m] = dot(table_ref[...], weights_ref[m]).astype(kind)

    return pl.pallas_call(
        kernel,
        grid_spec=pltpu.PrefetchScalarGridSpec(
            num_scalar_prefetch=1,
            grid=(len(order),),
            in_specs=[
                pl.BlockSpec((vocab, feats), lambda r, where: (0, 0)),
                pl.BlockSpec((3, feats, sub), lambda r, where: (0, 0, where[r])),
            ],
            out_specs=pl.BlockSpec((1, 3, vocab, sub), lambda r, where: (r, 0, 0, 0)),
        ),
        out_shape=jax.ShapeDtypeStruct((len(order), 3, vocab, sub), kind),
        compiler_params=PARAMS,
        name="table_projection",
    )(jnp.stack([ctx ^ r for r in order]), table, weights)


def input_projection(rows_in, pieces, ctx):
    rows, full_width = rows_in.shape
    feats, chans = pieces[0].shape[1:]
    count = len(pieces)
    sub = chans // count

    def kernel(ctx_ref, rows_ref, *refs):
        weights, (normed_ref, proj_ref, scale_ref) = refs[:count], refs[count:]

        @pl.when(pl.program_id(0) == 0)
        def _():
            total = jnp.zeros((rows, 1), F32)
            for q in range(count):
                part = rows_ref[:, q * feats : (q + 1) * feats].astype(F32)
                total = total + jnp.sum(part * part, axis=1, keepdims=True)
            scale_ref[...] = lax.rsqrt(total / full_width + EPSILON)
            for q in range(count):
                part = rows_ref[:, q * feats : (q + 1) * feats].astype(F32)
                normed_ref[q] = (part * scale_ref[...]).astype(BF16)

        total = jnp.zeros((rows, chans), F32)
        for r in range(count):
            start = pl.multiple_of((ctx_ref[0] ^ r) * feats, feats)
            total = total + dot(rows_ref[:, pl.ds(start, feats)], weights[r][0])
        total = (total * scale_ref[...]).astype(BF16)
        for q in range(count):
            proj_ref[q, 0] = total[:, q * sub : (q + 1) * sub]

    return pl.pallas_call(
        kernel,
        grid_spec=pltpu.PrefetchScalarGridSpec(
            num_scalar_prefetch=1,
            grid=(3,),
            in_specs=[pl.BlockSpec((rows, full_width), lambda m, ctx: (0, 0))]
            + [pl.BlockSpec((1, feats, chans), lambda m, ctx: (m, 0, 0))] * count,
            out_specs=[
                pl.BlockSpec((count, rows, feats), lambda m, ctx: (0, 0, 0)),
                pl.BlockSpec((count, 1, rows, sub), lambda m, ctx: (0, m, 0, 0)),
                pl.BlockSpec((rows, 1), lambda m, ctx: (0, 0)),
            ],
        ),
        out_shape=(
            jax.ShapeDtypeStruct((count, rows, feats), BF16),
            jax.ShapeDtypeStruct((count, 3, rows, sub), BF16),
            jax.ShapeDtypeStruct((rows, 1), F32),
        ),
        compiler_params=PARAMS,
        name="input_projection",
    )(ctx[None], rows_in, *pieces)


def input_gradient(gproj, pieces, rows_in, scale, ctx):
    rows, full_width = rows_in.shape
    feats, chans = pieces[0].shape[1:]
    count = len(pieces)
    sub = chans // count
    tile = min(256, feats)
    steps = feats // tile

    def kernel(ctx_ref, gproj_ref, rows_ref, scale_ref, *refs):
        weights, (out_ref, flat, grads) = refs[:count], refs[count:]
        step = pl.program_id(0)

        @pl.when(step == 0)
        def _():
            for m in range(3):
                for q in range(count):
                    flat[m, :, q * sub : (q + 1) * sub] = gproj_ref[q, m]

        columns = pl.ds(pl.multiple_of(step * tile, tile), tile)
        for r in range(count):
            total = dot_t(flat[0], weights[r][0])
            for m in (1, 2):
                total = total + dot_t(flat[m], weights[r][m])
            grads[ctx_ref[0] ^ r, :, columns] = total * scale_ref[...]

        @pl.when(step == steps - 1)
        def _():
            stat = jnp.zeros((rows, 1), F32)
            for q in range(count):
                part = rows_ref[:, q * feats : (q + 1) * feats].astype(F32)
                stat = stat + jnp.sum(part * grads[q], axis=1, keepdims=True)
            stat = stat * scale_ref[...] * scale_ref[...] / full_width
            for q in range(count):
                part = rows_ref[:, q * feats : (q + 1) * feats].astype(F32)
                out_ref[q] = (grads[q] - part * stat).astype(BF16)

    return pl.pallas_call(
        kernel,
        grid_spec=pltpu.PrefetchScalarGridSpec(
            num_scalar_prefetch=1,
            grid=(steps,),
            in_specs=[
                pl.BlockSpec(gproj.shape, lambda t, ctx: (0, 0, 0, 0)),
                pl.BlockSpec((rows, full_width), lambda t, ctx: (0, 0)),
                pl.BlockSpec((rows, 1), lambda t, ctx: (0, 0)),
            ]
            + [pl.BlockSpec((3, tile, chans), lambda t, ctx: (0, t, 0))] * count,
            out_specs=pl.BlockSpec((count, rows, feats), lambda t, ctx: (0, 0, 0)),
            scratch_shapes=[
                pltpu.VMEM((3, rows, chans), BF16),
                pltpu.VMEM((count, rows, feats), F32),
            ],
        ),
        out_shape=jax.ShapeDtypeStruct((count, rows, feats), BF16),
        compiler_params=PARAMS,
        name="input_gradient",
    )(ctx[None], gproj, rows_in, scale, *pieces)


def grad_in_kernel(left, pieces, ctx):
    feats, depth = left.shape
    count, sub = len(pieces), pieces[0].shape[2]
    if sub % 128:
        columns = jnp.concatenate([pick(jnp.stack(pieces), ctx ^ q) for q in range(count)], axis=2)
        columns = columns[:3]
        return jnp.einsum("dk,mkc->mdc", left, columns, preferred_element_type=F32)

    tile = min(256, feats)

    def kernel(ctx_ref, left_ref, *refs):
        out_ref = refs[count]
        for r in range(count):
            columns = pl.ds(pl.multiple_of((ctx_ref[0] ^ r) * sub, sub), sub)
            for m in range(3):
                out_ref[m, :, columns] = dot(left_ref[...], refs[r][m])

    return pl.pallas_call(
        kernel,
        grid_spec=pltpu.PrefetchScalarGridSpec(
            num_scalar_prefetch=1,
            grid=(feats // tile,),
            in_specs=[pl.BlockSpec((tile, depth), lambda t, ctx: (t, 0))]
            + [pl.BlockSpec((3, depth, sub), lambda t, ctx: (0, 0, 0))] * count,
            out_specs=pl.BlockSpec((3, tile, sub * count), lambda t, ctx: (0, t, 0)),
        ),
        out_shape=jax.ShapeDtypeStruct((3, feats, sub * count), F32),
        compiler_params=PARAMS,
        name="grad_project_in",
    )(ctx[None], left, *pieces)


def grad_out_kernel(pieces, right, ctx):
    depth, feats = right.shape
    count, sub = len(pieces), pieces[0].shape[1]

    def kernel(where_ref, right_ref, *refs):
        out_ref = refs[count]
        for r in range(count):

            @pl.when(pl.program_id(0) == r)
            def _():
                out_ref[...] = lax.dot_general(
                    refs[r][...],
                    right_ref[...],
                    (((0,), (0,)), ((), ())),
                    preferred_element_type=F32,
                )

    return pl.pallas_call(
        kernel,
        grid_spec=pltpu.PrefetchScalarGridSpec(
            num_scalar_prefetch=1,
            grid=(count,),
            in_specs=[pl.BlockSpec((depth, feats), lambda r, where: (0, 0))]
            + [pl.BlockSpec((depth, sub), lambda r, where: (0, 0))] * count,
            out_specs=pl.BlockSpec((sub, feats), lambda r, where: (where[r], 0)),
        ),
        out_shape=jax.ShapeDtypeStruct((sub * count, feats), F32),
        compiler_params=PARAMS,
        name="grad_project_out",
    )(jnp.stack([ctx ^ r for r in range(count)]), right, *pieces)


def together(*values):
    return lax.optimization_barrier(values)


def projection_specs(pieces, tile):
    specs, operands = [], []
    for piece in pieces:
        for array, place in piece:
            height = array.shape[0] if place is None else array.shape[0] // 2
            specs.append(pl.BlockSpec((height, tile), functools.partial(place_of, place or 0)))
            operands.append(array)
    return specs, operands


def place_of(row, t, ctx):
    return (row, t)


def output_projection(gated, pieces, ctx):
    count, rows, sub = gated.shape
    chans, feats = count * sub, pieces[0][0][0].shape[1]
    half, tile = chans // 2, min(256, feats)
    specs, operands = projection_specs(pieces, tile)

    def kernel(ctx_ref, gated_ref, *refs):
        weights, (out_ref, flat) = refs[: 2 * count], refs[2 * count :]

        @pl.when(pl.program_id(0) == 0)
        def _():
            for q in range(count):
                flat[:, q * sub : (q + 1) * sub] = gated_ref[q]

        for r in range(count):
            total = dot(flat[:, :half], weights[2 * r][...])
            total = total + dot(flat[:, half:], weights[2 * r + 1][...])
            out_ref[ctx_ref[0] ^ r] = total.astype(BF16)

    return pl.pallas_call(
        kernel,
        grid_spec=pltpu.PrefetchScalarGridSpec(
            num_scalar_prefetch=1,
            grid=(feats // tile,),
            in_specs=[pl.BlockSpec(gated.shape, lambda t, ctx: (0, 0, 0))] + specs,
            out_specs=pl.BlockSpec((count, rows, tile), lambda t, ctx: (0, 0, t)),
            scratch_shapes=[pltpu.VMEM((rows, chans), BF16)],
        ),
        out_shape=jax.ShapeDtypeStruct((count, rows, feats), BF16),
        compiler_params=PARAMS,
        name="output_projection",
    )(ctx[None], gated, *operands)


def gated_gradient(grads, pieces, ctx):
    count, rows, feats = grads.shape
    chans = pieces[0][0][0].shape[0]
    half, tile, sub = chans // 2, min(256, feats), chans // count
    specs, operands = projection_specs(pieces, tile)

    def kernel(ctx_ref, grads_ref, *refs):
        weights, (out_ref, total) = refs[: 2 * count], refs[2 * count :]
        step = pl.program_id(0)

        @pl.when(step == 0)
        def _():
            total[...] = jnp.zeros_like(total)

        for side in range(2):
            part = dot_t(grads_ref[ctx_ref[0]], weights[side][...])
            for r in range(1, count):
                part = part + dot_t(grads_ref[ctx_ref[0] ^ r], weights[2 * r + side][...])
            total[:, side * half : (side + 1) * half] += part

        @pl.when(step == feats // tile - 1)
        def _():
            for q in range(count):
                out_ref[q] = total[:, q * sub : (q + 1) * sub].astype(BF16)

    return pl.pallas_call(
        kernel,
        grid_spec=pltpu.PrefetchScalarGridSpec(
            num_scalar_prefetch=1,
            grid=(feats // tile,),
            in_specs=[pl.BlockSpec((count, rows, tile), lambda t, ctx: (0, 0, t))] + specs,
            out_specs=pl.BlockSpec((count, rows, sub), lambda t, ctx: (0, 0, 0)),
            scratch_shapes=[pltpu.VMEM((rows, chans), F32)],
        ),
        out_shape=jax.ShapeDtypeStruct((count, rows, sub), BF16),
        compiler_params=PARAMS,
        name="gated_gradient",
    )(ctx[None], grads, *operands)


def ctx_swap_in(value, section):
    me = lax.axis_index("ctx")
    count = value.shape[0]
    came = [pick(value, me)]
    for r in range(1, count):
        came.append(ctx_xor(pick(value, me ^ r), r, (section,)))
    came = jnp.stack(came)
    return [pick(came, me ^ q) for q in range(count)]


def ctx_swap(value):
    return lax.all_to_all(value, "ctx", split_axis=0, concat_axis=0, tiled=True)


def local(
    token_ids, embedding, project_in, short_taps, filter_taps, decay_rates, project_out, cotangent
):
    n_ctx, n_dp = lax.axis_size("ctx"), lax.axis_size("dp")
    sec, dp, ctx = (lax.axis_index(axis) for axis in ("section", "dp", "ctx"))
    first = sec == 0
    rows, vocab = token_ids.shape[0], embedding.shape[0]
    seq = rows * n_ctx
    weights_in = jnp.transpose(project_in[0], (1, 0, 2))
    weights_out = project_out[0]
    feats, chans = weights_out.shape[1], weights_out.shape[0]
    full_width = feats * n_ctx
    sub = chans // n_ctx

    if n_ctx == n_dp:
        half = vocab // 2
        mine = lax.dynamic_slice_in_dim(embedding, sec * half, half, 0)
        came = []
        for i in range(1, n_dp):
            shifts = (i, i % (n_dp - 1) + 1)
            came.append(
                send(
                    mine,
                    ("section", "dp", "ctx"),
                    lambda s, z, k: (0, (z + shifts[s]) % n_dp, k) if z == k else None,
                )
            )
        offset = (dp - ctx) % n_dp
        low, high = embedding[:half], embedding[half:]
        for i in range(1, n_dp):
            low = jnp.where(offset == i, came[i - 1], low)
            high = jnp.where(offset == i % (n_dp - 1) + 1, came[i - 1], high)
        table = jnp.concatenate([low, high], axis=0)
    else:
        table = lax.dynamic_slice_in_dim(
            lax.all_gather(embedding, "dp", axis=1, tiled=True), ctx * feats, feats, 1
        )
    half = chans // 2
    out_far = [far_gather(weights_out[start : start + half], (0,)) for start in (0, half)]
    far = sorted(out_far[0])[1:]
    table, *late = together(table, *[out_far[0][r] for r in far])
    out_far[0].update(zip(far, late))
    table_float = table.astype(F32)
    squares = jnp.sum(table_float * table_float, axis=1)
    tokens = token_ids.astype(F32)[None]
    held = [0]
    bit = n_ctx // 2
    while bit:
        came = ctx_xor(jnp.concatenate([squares, tokens.reshape(-1)]), bit, (0,))
        squares = squares + came[:vocab]
        tokens = jnp.concatenate([tokens, came[vocab:].reshape(-1, rows)], axis=0)
        held += [r | bit for r in held]
        bit //= 2
    table_inv = lax.rsqrt(squares[:, None] / full_width + EPSILON)
    tokens = jnp.stack([tokens[held.index(r)] for r in range(n_ctx)])
    tokens = jnp.concatenate([pick(tokens, ctx ^ q) for q in range(n_ctx)]).astype(jnp.int32)

    def own(value):
        return lax.dynamic_slice_in_dim(value, ctx * sub, sub, value.ndim - 1)

    taps = own(short_taps[0]).reshape(9, sub)
    filters = own(filter_taps[0])
    tap_count = filters.shape[0]
    positions = jnp.arange(tap_count).astype(F32)[:, None]
    damping = jnp.exp(-own(decay_rates) * positions / tap_count)
    kern = filters * damping
    matrices = spectra(tap_count)

    vocabulary = jnp.arange(vocab, dtype=jnp.int32)[None, :]
    first_input = dot((token_ids[:, None] == vocabulary).astype(BF16), embedding)

    in_far = far_gather(weights_in, (1,))

    order = scatter_order(n_ctx)
    kept = order[: n_ctx // 2]
    sent = table_projection(table, weights_in, ctx, [r | 1 for r in kept], BF16)
    arrived = ctx_xor(sent, 1, (0,))
    partial = table_projection(table, weights_in, ctx, kept, F32) + arrived.astype(F32)
    partial, *late = together(partial, *[out_far[1][r] for r in far])
    out_far[1].update(zip(far, late))
    bit = 2
    while bit < n_ctx:
        stays, gone = jnp.split(partial, 2, axis=0)
        partial = stays + ctx_xor(gone.astype(BF16), bit, (0,)).astype(F32)
        bit *= 2
    table_proj = (partial[0] * table_inv).astype(BF16)
    out_pieces = [[(weights_out, 0), (weights_out, 1)]]
    for r in sorted(out_far[0]):
        if r:
            out_pieces.append([(side[r], None) for side in out_far])
        out_pieces.append([(ctx_xor(side[r], 1, (0,)), None) for side in out_far])
    gated_0, *saved_0, proj_0 = conv_forward(table_proj, taps, kern, matrices, tokens)
    cot_stack = jnp.stack(dp_gather(cotangent, 1))
    gated_0, cot_stack = together(gated_0, cot_stack)
    gated_rows = jnp.stack(ctx_swap_in(gated_0.reshape(n_ctx, rows, sub), 0))
    shares = output_projection(gated_rows, out_pieces, ctx)
    middle_stack, (gated_0,), late = cross_gather(
        shares, first_input, 0, [gated_0], [in_far[r] for r in far]
    )
    gated_all_0 = ctx_gather(gated_0, (0,))

    in_far.update(zip(far, late))
    in_pieces = []
    for r in sorted(in_far):
        in_pieces += [in_far[r], ctx_xor(in_far[r], 1, (1,))]
    weights_late, *_ = together(weights_out, *late)
    late_far = far_gather(weights_late, (1,))
    middle_all = jnp.concatenate(in_order(middle_stack, dp), axis=1)
    normed, proj_rows, scale = input_projection(middle_all, in_pieces, ctx)
    proj_rows, *late = together(proj_rows, *[late_far[r] for r in far])
    late_far.update(zip(far, late))
    out_late = []
    for r in sorted(late_far):
        out_late += [late_far[r], ctx_xor(late_far[r], 1, (1,))]
    out_late = [[(piece, 0), (piece, 1)] for piece in out_late]
    proj_1 = ctx_swap(proj_rows)
    gated_1, *saved_1 = conv_forward(proj_1, taps, kern, matrices)

    cot_parts = jnp.stack(in_order(cot_stack, dp))
    gated_grad = ctx_swap(gated_gradient(cot_parts, out_late, ctx)).reshape(seq, sub)
    gproj_1, gkern_1, gtaps_1 = conv_backward(
        gated_grad, proj_1, taps, kern, matrices, saved_1
    )
    gproj_1, *gated_all_0 = together(gproj_1, *gated_all_0)
    gproj_rows = ctx_swap(gproj_1)
    shares = input_gradient(gproj_rows, in_pieces, middle_all, scale, ctx)
    back_stack, (normed, gproj_1, gated_1), _ = cross_gather(
        shares, cotangent, 1, [normed, gproj_1, gated_1]
    )

    normed_cols = jnp.concatenate([part.T for part in ctx_swap_in(normed, 1)], axis=1)
    gproj_1 = gproj_1.transpose(1, 0, 2, 3).reshape(3, seq, sub)
    gproj_all = ctx_gather(jnp.concatenate([gproj_1, gated_1[None]]), (1,))
    gated_all = [jnp.where(first, a, b[3]) for a, b in zip(gated_all_0, gproj_all)]

    back_stack, normed_cols, *rest = together(back_stack, normed_cols, *gproj_all, *gated_all)
    gproj_all, gated_all = rest[:n_ctx], rest[n_ctx:]
    back_parts = jnp.stack(in_order(back_stack, dp))
    gated_grad = ctx_swap(gated_gradient(back_parts, out_pieces, ctx)).reshape(seq, sub)
    table_grad, gkern_0, gtaps_0 = conv_backward(
        gated_grad, proj_0, taps, kern, matrices, saved_0, tokens, table_inv
    )

    grads = jnp.where(first, back_parts, cot_parts)
    grad_cols = ctx_swap(grads).reshape(seq, feats)
    grad_out = grad_out_kernel(gated_all, grad_cols, ctx)
    table_pieces = ctx_gather(table_grad, (0,))
    grad_in = lax.cond(
        first,
        lambda: grad_in_kernel(table.T, table_pieces, ctx),
        lambda: grad_in_kernel(normed_cols, gproj_all, ctx),
    )

    gkern = jnp.where(first, gkern_0, gkern_1)
    gtaps = jnp.where(first, gtaps_0, gtaps_1)
    gdecay = -jnp.sum(gkern * kern * positions, axis=0, keepdims=True) / tap_count
    small = jnp.concatenate([gkern * damping, gdecay, gtaps], axis=0)
    small = jnp.stack(ctx_gather(small, (0, 1)))
    small = jnp.concatenate([pick(small, ctx ^ q) for q in range(n_ctx)], axis=1)
    return (
        jnp.transpose(grad_in, (1, 0, 2))[None],
        grad_out[None],
        small[:tap_count][None],
        small[tap_count][None],
        small[tap_count + 1 :].reshape(1, 3, 3, chans),
    )


def solution(mesh):
    return jax.shard_map(
        local,
        mesh=mesh,
        in_specs=(
            P("ctx"),
            P(None, "dp"),
            P("section", "ctx", None, "dp"),
            P("section", None, None, "dp"),
            P("section", None, "dp"),
            P("section", "dp"),
            P("section", "dp", "ctx"),
            P("ctx", "dp"),
        ),
        out_specs=(
            P("section", "ctx", None, "dp"),
            P("section", "dp", "ctx"),
            P("section", None, "dp"),
            P("section", "dp"),
            P("section", None, None, "dp"),
        ),
        check_vma=False,
    )
```

```python
import functools

import jax
import jax.numpy as jnp
import numpy as np
from jax import lax
from jax.experimental import pallas as pl
from jax.experimental.pallas import tpu as pltpu
from jax.sharding import PartitionSpec as P

EPSILON = 1e-06
F32 = jnp.float32
BF16 = jnp.bfloat16


def dot(left, right):
    return jnp.dot(left, right, preferred_element_type=F32)


def dot_t(left, right):
    return lax.dot_general(left, right, (((1,), (1,)), ((), ())), preferred_element_type=F32)


def exact(left, right):
    return jnp.dot(left, right, preferred_element_type=F32, precision=lax.Precision.HIGHEST)


def pick(stack, index):
    return lax.dynamic_index_in_dim(stack, index, 0, keepdims=False)


def send(value, axes, route):
    sizes = [lax.axis_size(axis) for axis in axes]
    pairs = []
    for source, place in enumerate(np.ndindex(*sizes)):
        target = route(*place)
        if target is not None:
            pairs.append((source, int(np.ravel_multi_index(target, sizes))))
    return lax.ppermute(value, axes, pairs)


def ctx_xor(value, mask, sections):
    return send(
        value, ("section", "ctx"), lambda s, k: (s, k ^ mask) if s in sections else None
    )


def ctx_gather(value, sections):
    count = lax.axis_size("ctx")
    held = {0: value}
    bit = count // 2
    while bit:
        for r in list(held):
            held[r | bit] = ctx_xor(held[r], bit, sections)
        bit //= 2
    return [held[r] for r in range(count)]


def far_gather(value, sections):
    held = {0: value}
    bit = lax.axis_size("ctx") // 2
    while bit > 1:
        for r in list(held):
            held[r | bit] = ctx_xor(held[r], bit, sections)
        bit //= 2
    return held


def scatter_order(count):
    if count == 1:
        return [0]
    inner = scatter_order(count // 2)
    return [2 * r for r in inner] + [2 * r + 1 for r in inner]


def dp_gather(value, section):
    count = lax.axis_size("dp")
    pieces = [value]
    for _ in range(count - 1):
        pieces.append(
            send(
                pieces[-1],
                ("section", "dp"),
                lambda s, z: (s, (z + 1) % count) if s == section else None,
            )
        )
    return pieces


def cross_gather(shares, base, source, early, late=()):
    count = lax.axis_size("dp")
    half = base.shape[0] // 2
    arrivals = [
        [
            send(
                side[shift],
                ("section", "dp"),
                lambda s, z: (1 - s, (z + shift) % count) if s == source else None,
            )
            for shift in range(count)
        ]
        for side in shares
    ]

    def total(index, values):
        start = index * half
        result = base[start : start + half].astype(F32)
        for value in values:
            result = result + value.astype(F32)
        return result.astype(BF16)

    part, *early = together(total(0, arrivals[0]), *early)
    first = dp_gather(part, 1 - source)
    first[1], *arrivals[1] = together(first[1], *arrivals[1])
    part, *late = together(total(1, arrivals[1]), *late)
    second = dp_gather(part, 1 - source)
    stack = jnp.stack([jnp.concatenate(pair, axis=0) for pair in zip(first, second)])
    return stack, early, late


def in_order(stack, me):
    return [pick(stack, (me - q) % stack.shape[0]) for q in range(stack.shape[0])]


def spectra(taps):
    freq = np.arange(taps)[:, None]
    time = np.arange(taps)[None, :]
    angle = np.pi * freq * time / taps
    nyquist = np.where(time % 2 == 0, 1.0, -1.0)
    forward = np.concatenate(
        [np.cos(angle), np.where(freq == 0, nyquist, -np.sin(angle))], axis=0
    )
    weight = np.where(freq == 0, 1.0, 2.0) / (2 * taps)
    inverse = np.concatenate(
        [weight * np.cos(angle), np.where(freq == 0, nyquist, -2 * np.sin(angle)) * np.where(freq == 0, weight, 1.0 / (2 * taps))],
        axis=0,
    ).T
    sign = np.where(np.arange(2 * taps) % taps % 2 == 0, 1.0, -1.0)
    return [jnp.asarray(m, BF16) for m in (forward, inverse, inverse * sign[None, :])]


def later(current, before, steps, row):
    return jnp.where(row < steps, pltpu.roll(before, steps, 0), pltpu.roll(current, steps, 0))


def sooner(current, after, steps, row):
    count = current.shape[0]
    return jnp.where(
        row >= count - steps,
        pltpu.roll(after, count - steps, 0),
        pltpu.roll(current, count - steps, 0),
    )


def kernel_spectrum(fwd_ref, kern_ref, row):
    tap_count = kern_ref.shape[0]
    kern = dot(fwd_ref[...], kern_ref[...].astype(BF16))
    real, imag = kern[:tap_count], kern[tap_count:]
    return real, jnp.where(row == 0, 0.0, imag), jnp.where(row == 0, imag, real)


def proj_block(projs, m, b, tap_count):
    chunk, start = divmod(b * tap_count, projs[m].shape[1])
    return projs[m][chunk, start : start + tap_count, :].astype(F32)


def short_filter(taps_ref, m, current, before, row):
    return (
        taps_ref[m : m + 1, :] * current
        + taps_ref[3 + m : 4 + m, :] * later(current, before, 1, row)
        + taps_ref[6 + m : 7 + m, :] * later(current, before, 2, row)
    )


def lookup_kernel(
    tokens_ref, table_ref, taps_ref, kern_ref, fwd_ref, inv_ref,
    gated_ref, filt_ref, spec_ref, proj_ref,
):
    tap_count, vocab = kern_ref.shape[0], table_ref.shape[1]
    entry = lax.broadcasted_iota(jnp.int32, (tap_count, vocab), 1)
    for b in range(filt_ref.shape[0] // tap_count):
        here = pl.ds(b * tap_count, tap_count)
        chosen = (entry == tokens_ref[here, :]).astype(F32).astype(BF16)
        for m in range(3):
            proj_ref[0, m, here, :] = dot(chosen, table_ref[m]).astype(BF16)
    forward_kernel(
        proj_ref, taps_ref, kern_ref, fwd_ref, inv_ref, gated_ref, filt_ref, spec_ref
    )


def collect_kernel(
    tokens_ref, scale_ref, gg_ref, proj_ref, taps_ref, kern_ref, fwd_ref, inv_ref, filt_ref, spec_ref,
    table_ref, gkern_ref, gtaps_ref, grad_spec, gproj_ref,
):
    backward_kernel(
        gg_ref, proj_ref, taps_ref, kern_ref, fwd_ref, inv_ref, filt_ref, spec_ref,
        gproj_ref, gkern_ref, gtaps_ref, grad_spec,
    )
    _, vocab, _ = table_ref.shape
    seq = filt_ref.shape[0]
    entry = lax.broadcasted_iota(jnp.int32, (vocab, seq), 0)
    chosen = (entry == tokens_ref[...]).astype(F32).astype(BF16)
    for m in range(3):
        table_ref[m] = (dot(chosen, gproj_ref[0, m]) * scale_ref[...]).astype(BF16)


def forward_kernel(proj_ref, taps_ref, kern_ref, fwd_ref, inv_ref, gated_ref, filt_ref, spec_ref):
    projs = [proj_ref.at[:, m] for m in range(3)]
    tap_count, chans = kern_ref.shape
    blocks = filt_ref.shape[0] // tap_count
    row = lax.broadcasted_iota(jnp.int32, (tap_count, chans), 0)
    sign = jnp.where(row % 2 == 0, 1.0, -1.0)
    kr, ki, kn = kernel_spectrum(fwd_ref, kern_ref, row)
    zero = jnp.zeros((tap_count, chans), F32)
    before = [zero] * 3
    last_r, last_i = zero, zero
    for b in range(blocks):
        here = pl.ds(b * tap_count, tap_count)
        streams = []
        for m in range(3):
            current = proj_block(projs, m, b, tap_count)
            streams.append(short_filter(taps_ref, m, current, before[m], row))
            before[m] = current
        part = dot(fwd_ref[...], (streams[1] * streams[2]).astype(BF16))
        pr, pi = part[:tap_count], part[tap_count:]
        wr = last_r + sign * pr
        wi = last_i + sign * pi
        last_r, last_i = pr, pi
        spec_ref[b, :tap_count, :] = wr.astype(BF16)
        spec_ref[b, tap_count:, :] = wi.astype(BF16)
        mixed = jnp.concatenate([wr * kr - wi * ki, wr * ki + wi * kn], axis=0)
        filtered = dot(inv_ref[...], mixed.astype(BF16))
        filt_ref[here, :] = filtered.astype(BF16)
        gated_ref[here, :] = (streams[0] * filtered).astype(BF16)


def backward_kernel(
    gg_ref, proj_ref, taps_ref, kern_ref, fwd_ref, inv_ref, filt_ref, spec_ref,
    gproj_ref, gkern_ref, gtaps_ref, grad_spec,
):
    projs = [proj_ref.at[:, m] for m in range(3)]
    tap_count, chans = kern_ref.shape
    blocks = filt_ref.shape[0] // tap_count
    row = lax.broadcasted_iota(jnp.int32, (tap_count, chans), 0)
    sign = jnp.where(row % 2 == 0, 1.0, -1.0)
    kr, ki, kn = kernel_spectrum(fwd_ref, kern_ref, row)
    zero = jnp.zeros((tap_count, chans), F32)
    sum_r, sum_i = zero, zero
    last = zero
    for b in range(blocks):
        here = pl.ds(b * tap_count, tap_count)
        current = proj_block(projs, 0, b, tap_count)
        query = short_filter(taps_ref, 0, current, last, row)
        last = current
        part = dot(fwd_ref[...], (gg_ref[here, :].astype(F32) * query).astype(BF16))
        grad_spec[b] = part
        gr, gi = sign * part[:tap_count], sign * part[tap_count:]
        wr = spec_ref[b, :tap_count, :].astype(F32)
        wi = spec_ref[b, tap_count:, :].astype(F32)
        rr, ii = wr * gr, wi * gi
        sum_r = sum_r + jnp.where(row == 0, rr, rr + ii)
        sum_i = sum_i + jnp.where(row == 0, ii, wr * gi - wi * gr)
    gkern_ref[...] = exact(
        inv_ref[...].astype(F32), jnp.concatenate([sum_r, sum_i], axis=0)
    )
    after = [zero] * 3
    next_r, next_i = zero, zero
    sums = [jnp.zeros((1, chans), F32) for _ in range(9)]
    for b in reversed(range(blocks)):
        chunk, start = divmod(b * tap_count, projs[0].shape[1])
        here = pl.ds(b * tap_count, tap_count)
        gr, gi = grad_spec[b, :tap_count, :], grad_spec[b, tap_count:, :]
        vr, vi = gr + sign * next_r, gi + sign * next_i
        next_r, next_i = gr, gi
        mixed = jnp.concatenate([vr * kr + vi * ki, vi * kn - vr * ki], axis=0)
        grad_prod = dot(inv_ref[...], mixed.astype(BF16))
        shifts, shorts = [], []
        for m in range(3):
            current = proj_block(projs, m, b, tap_count)
            before = proj_block(projs, m, b - 1, tap_count) if b else zero
            shifts.append([current, later(current, before, 1, row), later(current, before, 2, row)])
            if m:
                shorts.append(sum(taps_ref[3 * j + m : 3 * j + m + 1, :] * shifts[m][j] for j in range(3)))
        grads = [
            gg_ref[here, :].astype(F32) * filt_ref[here, :].astype(F32),
            grad_prod * shorts[1],
            grad_prod * shorts[0],
        ]
        for m in range(3):
            grad = grads[m]
            out = (
                taps_ref[m : m + 1, :] * grad
                + taps_ref[3 + m : 4 + m, :] * sooner(grad, after[m], 1, row)
                + taps_ref[6 + m : 7 + m, :] * sooner(grad, after[m], 2, row)
            )
            after[m] = grad
            gproj_ref[chunk, m, start : start + tap_count, :] = out.astype(BF16)
            for j in range(3):
                sums[3 * j + m] = sums[3 * j + m] + jnp.sum(
                    grad * shifts[m][j], axis=0, keepdims=True
                )
    for index in range(9):
        gtaps_ref[index : index + 1, :] = sums[index]


PARAMS = pltpu.CompilerParams(vmem_limit_bytes=56 * 1024 * 1024)


def conv_forward(proj, taps, kern, matrices, tokens=None):
    tap_count, chans = kern.shape
    seq = proj.shape[0] * proj.shape[2] if tokens is None else tokens.shape[0]
    results = [
        jax.ShapeDtypeStruct((seq, chans), BF16),
        jax.ShapeDtypeStruct((seq, chans), BF16),
        jax.ShapeDtypeStruct((seq // tap_count, 2 * tap_count, chans), BF16),
    ]
    operands = (proj, taps, kern, matrices[0], matrices[2])
    if tokens is not None:
        results.append(jax.ShapeDtypeStruct((1, 3, seq, chans), BF16))
        operands = (tokens[:, None], *operands)
    return pl.pallas_call(
        forward_kernel if tokens is None else lookup_kernel,
        out_shape=results,
        compiler_params=PARAMS,
        name="conv_forward",
    )(*operands)


def conv_backward(gg, proj, taps, kern, matrices, saved, tokens=None, scale=None):
    tap_count, chans = kern.shape
    seq = gg.shape[0]
    scratch = [pltpu.VMEM((seq // tap_count, 2 * tap_count, chans), F32)]
    operands = (gg, proj, taps, kern, matrices[0], matrices[1], *saved)
    first = jax.ShapeDtypeStruct(proj.shape, BF16)
    if tokens is not None:
        first = jax.ShapeDtypeStruct((3, scale.shape[0], chans), BF16)
        scratch.append(pltpu.VMEM(proj.shape, BF16))
        operands = (tokens[None, :], scale, *operands)
    return pl.pallas_call(
        backward_kernel if tokens is None else collect_kernel,
        out_shape=(
            first,
            jax.ShapeDtypeStruct(kern.shape, F32),
            jax.ShapeDtypeStruct((9, chans), F32),
        ),
        scratch_shapes=scratch,
        compiler_params=PARAMS,
        name="conv_backward",
    )(*operands)


def table_projection(table, weights, ctx, order, kind):
    vocab, feats = table.shape
    sub = weights.shape[2] // lax.axis_size("ctx")
    if sub % 128:
        columns = jnp.stack(
            [lax.dynamic_slice_in_dim(weights, (ctx ^ r) * sub, sub, 2) for r in order]
        )
        return jnp.einsum("vd,rmdc->rmvc", table, columns, preferred_element_type=F32).astype(kind)

    def kernel(where_ref, table_ref, weights_ref, out_ref):
        for m in range(3):
            out_ref[0, m] = dot(table_ref[...], weights_ref[m]).astype(kind)

    return pl.pallas_call(
        kernel,
        grid_spec=pltpu.PrefetchScalarGridSpec(
            num_scalar_prefetch=1,
            grid=(len(order),),
            in_specs=[
                pl.BlockSpec((vocab, feats), lambda r, where: (0, 0)),
                pl.BlockSpec((3, feats, sub), lambda r, where: (0, 0, where[r])),
            ],
            out_specs=pl.BlockSpec((1, 3, vocab, sub), lambda r, where: (r, 0, 0, 0)),
        ),
        out_shape=jax.ShapeDtypeStruct((len(order), 3, vocab, sub), kind),
        compiler_params=PARAMS,
        name="table_projection",
    )(jnp.stack([ctx ^ r for r in order]), table, weights)


def input_projection(rows_in, pieces, ctx):
    rows, full_width = rows_in.shape
    feats, chans = pieces[0].shape[1:]
    count = len(pieces)
    sub = chans // count

    def kernel(ctx_ref, rows_ref, *refs):
        weights, (normed_ref, proj_ref, scale_ref) = refs[:count], refs[count:]

        @pl.when(pl.program_id(0) == 0)
        def _():
            total = jnp.zeros((rows, 1), F32)
            for q in range(count):
                part = rows_ref[:, q * feats : (q + 1) * feats].astype(F32)
                total = total + jnp.sum(part * part, axis=1, keepdims=True)
            scale_ref[...] = lax.rsqrt(total / full_width + EPSILON)
            for q in range(count):
                part = rows_ref[:, q * feats : (q + 1) * feats].astype(F32)
                normed_ref[q] = (part * scale_ref[...]).astype(BF16)

        total = jnp.zeros((rows, chans), F32)
        for r in range(count):
            start = pl.multiple_of((ctx_ref[0] ^ r) * feats, feats)
            total = total + dot(rows_ref[:, pl.ds(start, feats)], weights[r][0])
        total = (total * scale_ref[...]).astype(BF16)
        for q in range(count):
            proj_ref[q, 0] = total[:, q * sub : (q + 1) * sub]

    return pl.pallas_call(
        kernel,
        grid_spec=pltpu.PrefetchScalarGridSpec(
            num_scalar_prefetch=1,
            grid=(3,),
            in_specs=[pl.BlockSpec((rows, full_width), lambda m, ctx: (0, 0))]
            + [pl.BlockSpec((1, feats, chans), lambda m, ctx: (m, 0, 0))] * count,
            out_specs=[
                pl.BlockSpec((count, rows, feats), lambda m, ctx: (0, 0, 0)),
                pl.BlockSpec((count, 1, rows, sub), lambda m, ctx: (0, m, 0, 0)),
                pl.BlockSpec((rows, 1), lambda m, ctx: (0, 0)),
            ],
        ),
        out_shape=(
            jax.ShapeDtypeStruct((count, rows, feats), BF16),
            jax.ShapeDtypeStruct((count, 3, rows, sub), BF16),
            jax.ShapeDtypeStruct((rows, 1), F32),
        ),
        compiler_params=PARAMS,
        name="input_projection",
    )(ctx[None], rows_in, *pieces)


def input_gradient(gproj, pieces, rows_in, scale, ctx, dp):
    rows, full_width = rows_in.shape
    feats, chans = pieces[0].shape[1:]
    count = len(pieces)
    sub = chans // count
    tile = min(256, feats)
    steps, half = feats // tile, rows // 2

    def kernel(ctx_ref, gproj_ref, rows_ref, scale_ref, *refs):
        weights, outs, (flat, grads) = refs[:count], refs[count:-2], refs[-2:]
        step = pl.program_id(0)

        @pl.when(step == 0)
        def _():
            for m in range(3):
                for q in range(count):
                    flat[m, :, q * sub : (q + 1) * sub] = gproj_ref[q, m]

        columns = pl.ds(pl.multiple_of(step * tile, tile), tile)
        for r in range(count):
            total = dot_t(flat[0], weights[r][0])
            for m in (1, 2):
                total = total + dot_t(flat[m], weights[r][m])
            grads[ctx_ref[0] ^ r, :, columns] = total * scale_ref[...]

        @pl.when(step == steps - 1)
        def _():
            stat = jnp.zeros((rows, 1), F32)
            for q in range(count):
                part = rows_ref[:, q * feats : (q + 1) * feats].astype(F32)
                stat = stat + jnp.sum(part * grads[q], axis=1, keepdims=True)
            stat = stat * scale_ref[...] * scale_ref[...] / full_width
            for shift in range(count):
                q = ctx_ref[1 + shift]
                start = pl.multiple_of(q * feats, feats)
                part = rows_ref[:, pl.ds(start, feats)].astype(F32)
                total = (grads[q] - part * stat).astype(BF16)
                outs[shift][...] = total[:half]
                outs[count + shift][...] = total[half:]

    outs = pl.pallas_call(
        kernel,
        grid_spec=pltpu.PrefetchScalarGridSpec(
            num_scalar_prefetch=1,
            grid=(steps,),
            in_specs=[
                pl.BlockSpec(gproj.shape, lambda t, ctx: (0, 0, 0, 0)),
                pl.BlockSpec((rows, full_width), lambda t, ctx: (0, 0)),
                pl.BlockSpec((rows, 1), lambda t, ctx: (0, 0)),
            ]
            + [pl.BlockSpec((3, tile, chans), lambda t, ctx: (0, t, 0))] * count,
            out_specs=[pl.BlockSpec((half, feats), lambda t, ctx: (0, 0))] * (2 * count),
            scratch_shapes=[
                pltpu.VMEM((3, rows, chans), BF16),
                pltpu.VMEM((count, rows, feats), F32),
            ],
        ),
        out_shape=[jax.ShapeDtypeStruct((half, feats), BF16)] * (2 * count),
        compiler_params=PARAMS,
        name="input_gradient",
    )(jnp.concatenate([ctx[None], targets(dp, count)]), gproj, rows_in, scale, *pieces)
    return outs[:count], outs[count:]


def grad_in_kernel(left, pieces, ctx):
    feats, depth = left.shape
    count, sub = len(pieces), pieces[0].shape[2]
    if sub % 128:
        columns = jnp.concatenate([pick(jnp.stack(pieces), ctx ^ q) for q in range(count)], axis=2)
        columns = columns[:3]
        return jnp.einsum("dk,mkc->mdc", left, columns, preferred_element_type=F32)

    tile = min(256, feats)

    def kernel(ctx_ref, left_ref, *refs):
        out_ref = refs[count]
        for r in range(count):
            columns = pl.ds(pl.multiple_of((ctx_ref[0] ^ r) * sub, sub), sub)
            for m in range(3):
                out_ref[m, :, columns] = dot(left_ref[...], refs[r][m])

    return pl.pallas_call(
        kernel,
        grid_spec=pltpu.PrefetchScalarGridSpec(
            num_scalar_prefetch=1,
            grid=(feats // tile,),
            in_specs=[pl.BlockSpec((tile, depth), lambda t, ctx: (t, 0))]
            + [pl.BlockSpec((3, depth, sub), lambda t, ctx: (0, 0, 0))] * count,
            out_specs=pl.BlockSpec((3, tile, sub * count), lambda t, ctx: (0, t, 0)),
        ),
        out_shape=jax.ShapeDtypeStruct((3, feats, sub * count), F32),
        compiler_params=PARAMS,
        name="grad_project_in",
    )(ctx[None], left, *pieces)


def grad_out_kernel(early, late, right, ctx, sec):
    depth, feats = right.shape
    count, sub = len(early), early[0].shape[1]

    def kernel(where_ref, right_ref, *refs):
        out_ref = refs[2 * count]
        for r in range(count):
            for index, piece in ((0, refs[r].at[...]), (1, refs[count + r].at[0])):

                @pl.when((pl.program_id(0) == r) & (where_ref[count] == index))
                def _():
                    out_ref[...] = lax.dot_general(
                        piece[...],
                        right_ref[...],
                        (((0,), (0,)), ((), ())),
                        preferred_element_type=F32,
                    )

    return pl.pallas_call(
        kernel,
        grid_spec=pltpu.PrefetchScalarGridSpec(
            num_scalar_prefetch=1,
            grid=(count,),
            in_specs=[pl.BlockSpec((depth, feats), lambda r, where: (0, 0))]
            + [pl.BlockSpec((depth, sub), lambda r, where: (0, 0))] * count
            + [pl.BlockSpec((1, depth, sub), lambda r, where: (3, 0, 0))] * count,
            out_specs=pl.BlockSpec((sub, feats), lambda r, where: (where[r], 0)),
        ),
        out_shape=jax.ShapeDtypeStruct((sub * count, feats), F32),
        compiler_params=PARAMS,
        name="grad_project_out",
    )(jnp.stack([ctx ^ r for r in range(count)] + [sec]), right, *early, *late)


def together(*values):
    return lax.optimization_barrier(values)


def targets(dp, count):
    return (dp + jnp.arange(count, dtype=jnp.int32)) % count


def output_projection(gated, weights, dp):
    count, rows, sub = gated.shape
    chans, full_width = weights.shape
    parts = lax.axis_size("dp")
    width, half = full_width // parts, rows // 2

    def kernel(where_ref, gated_ref, weights_ref, *refs):
        outs, flat = refs[:-1], refs[-1]

        @pl.when(pl.program_id(0) == 0)
        def _():
            for q in range(count):
                flat[:, q * sub : (q + 1) * sub] = gated_ref[q]

        total = dot(flat[...], weights_ref[...]).astype(BF16)
        for shift in range(parts):

            @pl.when(pl.program_id(0) == shift)
            def _():
                outs[shift][...] = total[:half]
                outs[parts + shift][...] = total[half:]

    outs = pl.pallas_call(
        kernel,
        grid_spec=pltpu.PrefetchScalarGridSpec(
            num_scalar_prefetch=1,
            grid=(parts,),
            in_specs=[
                pl.BlockSpec(gated.shape, lambda q, where: (0, 0, 0)),
                pl.BlockSpec((chans, width), lambda q, where: (0, where[q])),
            ],
            out_specs=[pl.BlockSpec((half, width), lambda q, where: (0, 0))] * (2 * parts),
            scratch_shapes=[pltpu.VMEM((rows, chans), BF16)],
        ),
        out_shape=[jax.ShapeDtypeStruct((half, width), BF16)] * (2 * parts),
        compiler_params=PARAMS,
        name="output_projection",
    )(targets(dp, parts), gated, weights)
    return outs[:parts], outs[parts:]


def ctx_swap_in(value, section):
    me = lax.axis_index("ctx")
    count = value.shape[0]
    came = [pick(value, me)]
    for r in range(1, count):
        came.append(ctx_xor(pick(value, me ^ r), r, (section,)))
    came = jnp.stack(came)
    return [pick(came, me ^ q) for q in range(count)]


def ctx_swap(value):
    return lax.all_to_all(value, "ctx", split_axis=0, concat_axis=0, tiled=True)


def local(
    token_ids, embedding, project_in, short_taps, filter_taps, decay_rates, project_out, cotangent
):
    n_ctx, n_dp = lax.axis_size("ctx"), lax.axis_size("dp")
    sec, dp, ctx = (lax.axis_index(axis) for axis in ("section", "dp", "ctx"))
    first = sec == 0
    rows, vocab = token_ids.shape[0], embedding.shape[0]
    seq = rows * n_ctx
    weights_in = jnp.transpose(project_in[0], (1, 0, 2))
    weights_out = project_out[0]
    feats, chans = weights_out.shape[1], weights_out.shape[0]
    full_width = feats * n_ctx
    sub = chans // n_ctx

    if n_ctx == n_dp:
        half = vocab // 2
        mine = lax.dynamic_slice_in_dim(embedding, sec * half, half, 0)
        came = []
        for i in range(1, n_dp):
            shifts = (i, i % (n_dp - 1) + 1)
            came.append(
                send(
                    mine,
                    ("section", "dp", "ctx"),
                    lambda s, z, k: (0, (z + shifts[s]) % n_dp, k) if z == k else None,
                )
            )
        offset = (dp - ctx) % n_dp
        low, high = embedding[:half], embedding[half:]
        for i in range(1, n_dp):
            low = jnp.where(offset == i, came[i - 1], low)
            high = jnp.where(offset == i % (n_dp - 1) + 1, came[i - 1], high)
        table = jnp.concatenate([low, high], axis=0)
    else:
        table = lax.dynamic_slice_in_dim(
            lax.all_gather(embedding, "dp", axis=1, tiled=True), ctx * feats, feats, 1
        )
    table_float = table.astype(F32)
    squares = jnp.sum(table_float * table_float, axis=1)
    tokens = token_ids.astype(F32)[None]
    held = [0]
    bit = n_ctx // 2
    while bit:
        came = ctx_xor(jnp.concatenate([squares, tokens.reshape(-1)]), bit, (0,))
        squares = squares + came[:vocab]
        tokens = jnp.concatenate([tokens, came[vocab:].reshape(-1, rows)], axis=0)
        held += [r | bit for r in held]
        bit //= 2
    table_inv = lax.rsqrt(squares[:, None] / full_width + EPSILON)
    tokens = jnp.stack([tokens[held.index(r)] for r in range(n_ctx)])
    tokens = jnp.concatenate([pick(tokens, ctx ^ q) for q in range(n_ctx)]).astype(jnp.int32)

    def own(value):
        return lax.dynamic_slice_in_dim(value, ctx * sub, sub, value.ndim - 1)

    taps = own(short_taps[0]).reshape(9, sub)
    filters = own(filter_taps[0])
    tap_count = filters.shape[0]
    positions = jnp.arange(tap_count).astype(F32)[:, None]
    damping = jnp.exp(-own(decay_rates) * positions / tap_count)
    kern = filters * damping
    matrices = spectra(tap_count)

    vocabulary = jnp.arange(vocab, dtype=jnp.int32)[None, :]
    first_input = dot((token_ids[:, None] == vocabulary).astype(BF16), embedding)

    out_full = lax.all_gather(weights_out, "ctx", axis=1, tiled=True)
    in_far = far_gather(weights_in, (1,))
    far = sorted(in_far)[1:]

    order = scatter_order(n_ctx)
    kept = order[: n_ctx // 2]
    sent = table_projection(table, weights_in, ctx, [r | 1 for r in kept], BF16)
    arrived = ctx_xor(sent, 1, (0,))
    partial = table_projection(table, weights_in, ctx, kept, F32) + arrived.astype(F32)
    bit = 2
    while bit < n_ctx:
        stays, gone = jnp.split(partial, 2, axis=0)
        partial = stays + ctx_xor(gone.astype(BF16), bit, (0,)).astype(F32)
        bit *= 2
    table_proj = (partial[0] * table_inv).astype(BF16)
    gated_0, *saved_0, proj_0 = conv_forward(table_proj, taps, kern, matrices, tokens)
    cot_stack = jnp.stack(dp_gather(cotangent, 1))
    gated_0, cot_stack = together(gated_0, cot_stack)
    gated_rows = jnp.stack(ctx_swap_in(gated_0.reshape(n_ctx, rows, sub), 0))
    shares = output_projection(gated_rows, out_full, dp)
    middle_stack, (gated_0,), late = cross_gather(
        shares, first_input, 0, [gated_0], [in_far[r] for r in far]
    )
    gated_all_0 = ctx_gather(gated_0, (0,))

    in_far.update(zip(far, late))
    in_pieces = []
    for r in sorted(in_far):
        in_pieces += [in_far[r], ctx_xor(in_far[r], 1, (1,))]
    middle_all = jnp.concatenate(in_order(middle_stack, dp), axis=1)
    normed, proj_rows, scale = input_projection(middle_all, in_pieces, ctx)
    proj_1 = ctx_swap(proj_rows)
    gated_1, *saved_1 = conv_forward(proj_1, taps, kern, matrices)

    def gated_gradient(parts):
        total = dot_t(jnp.concatenate(parts, axis=1), out_full).astype(BF16)
        split = jnp.transpose(total.reshape(rows, n_ctx, sub), (1, 0, 2))
        return ctx_swap(split).reshape(seq, sub)

    cot_parts = in_order(cot_stack, dp)
    gproj_1, gkern_1, gtaps_1 = conv_backward(
        gated_gradient(cot_parts), proj_1, taps, kern, matrices, saved_1
    )
    gproj_1, *gated_all_0 = together(gproj_1, *gated_all_0)
    gproj_rows = ctx_swap(gproj_1)
    shares = input_gradient(gproj_rows, in_pieces, middle_all, scale, ctx, dp)
    back_stack, (normed, gproj_1, gated_1), _ = cross_gather(
        shares, cotangent, 1, [normed, gproj_1, gated_1]
    )

    normed_cols = jnp.concatenate([part.T for part in ctx_swap_in(normed, 1)], axis=1)
    gproj_1 = gproj_1.transpose(1, 0, 2, 3).reshape(3, seq, sub)
    gproj_all = ctx_gather(jnp.concatenate([gproj_1, gated_1[None]]), (1,))

    back_stack, normed_cols, *gproj_all = together(back_stack, normed_cols, *gproj_all)
    back_parts = in_order(back_stack, dp)
    table_grad, gkern_0, gtaps_0 = conv_backward(
        gated_gradient(back_parts), proj_0, taps, kern, matrices, saved_0, tokens, table_inv
    )

    grads = jnp.stack([jnp.where(first, a, b) for a, b in zip(back_parts, cot_parts)])
    grad_cols = ctx_swap(grads).reshape(seq, feats)
    grad_out = grad_out_kernel(gated_all_0, gproj_all, grad_cols, ctx, sec)
    table_pieces = ctx_gather(table_grad, (0,))
    grad_in = lax.cond(
        first,
        lambda: grad_in_kernel(table.T, table_pieces, ctx),
        lambda: grad_in_kernel(normed_cols, gproj_all, ctx),
    )

    gkern = jnp.where(first, gkern_0, gkern_1)
    gtaps = jnp.where(first, gtaps_0, gtaps_1)
    gdecay = -jnp.sum(gkern * kern * positions, axis=0, keepdims=True) / tap_count
    small = jnp.concatenate([gkern * damping, gdecay, gtaps], axis=0)
    small = jnp.stack(ctx_gather(small, (0, 1)))
    small = jnp.concatenate([pick(small, ctx ^ q) for q in range(n_ctx)], axis=1)
    return (
        jnp.transpose(grad_in, (1, 0, 2))[None],
        grad_out[None],
        small[:tap_count][None],
        small[tap_count][None],
        small[tap_count + 1 :].reshape(1, 3, 3, chans),
    )


def solution(mesh):
    return jax.shard_map(
        local,
        mesh=mesh,
        in_specs=(
            P("ctx"),
            P(None, "dp"),
            P("section", "ctx", None, "dp"),
            P("section", None, None, "dp"),
            P("section", None, "dp"),
            P("section", "dp"),
            P("section", "dp", "ctx"),
            P("ctx", "dp"),
        ),
        out_specs=(
            P("section", "ctx", None, "dp"),
            P("section", "dp", "ctx"),
            P("section", None, "dp"),
            P("section", "dp"),
            P("section", None, None, "dp"),
        ),
        check_vma=False,
    )
```

```python
import functools

import jax
import jax.numpy as jnp
import numpy as np
from jax import lax
from jax.experimental import pallas as pl
from jax.experimental.pallas import tpu as pltpu
from jax.sharding import PartitionSpec as P

EPSILON = 1e-06
F32 = jnp.float32
BF16 = jnp.bfloat16


def dot(left, right):
    return jnp.dot(left, right, preferred_element_type=F32)


def dot_t(left, right):
    return lax.dot_general(left, right, (((1,), (1,)), ((), ())), preferred_element_type=F32)


def exact(left, right):
    return jnp.dot(left, right, preferred_element_type=F32, precision=lax.Precision.HIGHEST)


def pick(stack, index):
    return lax.dynamic_index_in_dim(stack, index, 0, keepdims=False)


def send(value, axes, route):
    sizes = [lax.axis_size(axis) for axis in axes]
    pairs = []
    for source, place in enumerate(np.ndindex(*sizes)):
        target = route(*place)
        if target is not None:
            pairs.append((source, int(np.ravel_multi_index(target, sizes))))
    return lax.ppermute(value, axes, pairs)


def ctx_xor(value, mask, sections):
    return send(
        value, ("section", "ctx"), lambda s, k: (s, k ^ mask) if s in sections else None
    )


def ctx_gather(value, sections):
    count = lax.axis_size("ctx")
    held = {0: value}
    bit = count // 2
    while bit:
        for r in list(held):
            held[r | bit] = ctx_xor(held[r], bit, sections)
        bit //= 2
    return [held[r] for r in range(count)]


def far_gather(value, sections):
    held = {0: value}
    bit = lax.axis_size("ctx") // 2
    while bit > 1:
        for r in list(held):
            held[r | bit] = ctx_xor(held[r], bit, sections)
        bit //= 2
    return held


def scatter_order(count):
    if count == 1:
        return [0]
    inner = scatter_order(count // 2)
    return [2 * r for r in inner] + [2 * r + 1 for r in inner]


def dp_gather(value, section):
    count = lax.axis_size("dp")
    pieces = [value]
    for _ in range(count - 1):
        pieces.append(
            send(
                pieces[-1],
                ("section", "dp"),
                lambda s, z: (s, (z + 1) % count) if s == section else None,
            )
        )
    return pieces


def cross_gather(shares, base, source, early, late=()):
    count = lax.axis_size("dp")
    half = base.shape[0] // 2
    straight, *shares = shares
    straight = send(straight, ("section", "dp"), lambda s, z: (1 - s, z) if s == source else None)
    arrivals = [
        [straight[start : start + half]]
        + [
            send(
                side[shift - 1],
                ("section", "dp"),
                lambda s, z: (1 - s, (z + shift) % count) if s == source else None,
            )
            for shift in range(1, count)
        ]
        for start, side in zip((0, half), shares)
    ]

    def total(index, values):
        start = index * half
        result = base[start : start + half].astype(F32)
        for value in values:
            result = result + value.astype(F32)
        return result.astype(BF16)

    part = total(0, arrivals[0])
    if early:
        part, *early = together(part, *early)
    first = dp_gather(part, 1 - source)
    marker = min(2, count - 1)
    first[marker], *arrivals[1] = together(first[marker], *arrivals[1])
    part, *late = together(total(1, arrivals[1]), *late)
    second = dp_gather(part, 1 - source)
    stack = jnp.stack([jnp.concatenate(pair, axis=0) for pair in zip(first, second)])
    return stack, early, late


def in_order(stack, me):
    return [pick(stack, (me - q) % stack.shape[0]) for q in range(stack.shape[0])]


def spectra(taps):
    freq = np.arange(taps)[:, None]
    time = np.arange(taps)[None, :]
    angle = np.pi * freq * time / taps
    nyquist = np.where(time % 2 == 0, 1.0, -1.0)
    forward = np.concatenate(
        [np.cos(angle), np.where(freq == 0, nyquist, -np.sin(angle))], axis=0
    )
    weight = np.where(freq == 0, 1.0, 2.0) / (2 * taps)
    inverse = np.concatenate(
        [weight * np.cos(angle), np.where(freq == 0, nyquist, -2 * np.sin(angle)) * np.where(freq == 0, weight, 1.0 / (2 * taps))],
        axis=0,
    ).T
    sign = np.where(np.arange(2 * taps) % taps % 2 == 0, 1.0, -1.0)
    return [jnp.asarray(m, BF16) for m in (forward, inverse, inverse * sign[None, :])]


def later(current, before, steps, row):
    return jnp.where(row < steps, pltpu.roll(before, steps, 0), pltpu.roll(current, steps, 0))


def sooner(current, after, steps, row):
    count = current.shape[0]
    return jnp.where(
        row >= count - steps,
        pltpu.roll(after, count - steps, 0),
        pltpu.roll(current, count - steps, 0),
    )


def kernel_spectrum(fwd_ref, kern_ref, row):
    tap_count = kern_ref.shape[0]
    kern = dot(fwd_ref[...], kern_ref[...].astype(BF16))
    real, imag = kern[:tap_count], kern[tap_count:]
    return real, jnp.where(row == 0, 0.0, imag), jnp.where(row == 0, imag, real)


def proj_block(projs, m, b, tap_count):
    chunk, start = divmod(b * tap_count, projs[m].shape[1])
    return projs[m][chunk, start : start + tap_count, :].astype(F32)


def short_filter(taps_ref, m, current, before, row):
    return (
        taps_ref[m : m + 1, :] * current
        + taps_ref[3 + m : 4 + m, :] * later(current, before, 1, row)
        + taps_ref[6 + m : 7 + m, :] * later(current, before, 2, row)
    )


def lookup_kernel(
    tokens_ref, table_ref, taps_ref, kern_ref, fwd_ref, inv_ref,
    gated_ref, filt_ref, spec_ref, proj_ref,
):
    tap_count, vocab = kern_ref.shape[0], table_ref.shape[1]
    entry = lax.broadcasted_iota(jnp.int32, (tap_count, vocab), 1)
    for b in range(filt_ref.shape[0] // tap_count):
        here = pl.ds(b * tap_count, tap_count)
        chosen = (entry == tokens_ref[here, :]).astype(F32).astype(BF16)
        for m in range(3):
            proj_ref[0, m, here, :] = dot(chosen, table_ref[m]).astype(BF16)
    forward_kernel(
        proj_ref, taps_ref, kern_ref, fwd_ref, inv_ref, gated_ref, filt_ref, spec_ref
    )


def collect_kernel(
    tokens_ref, scale_ref, gg_ref, proj_ref, taps_ref, kern_ref, fwd_ref, inv_ref, filt_ref, spec_ref,
    table_ref, gkern_ref, gtaps_ref, grad_spec, gproj_ref,
):
    backward_kernel(
        gg_ref, proj_ref, taps_ref, kern_ref, fwd_ref, inv_ref, filt_ref, spec_ref,
        gproj_ref, gkern_ref, gtaps_ref, grad_spec,
    )
    _, vocab, _ = table_ref.shape
    seq = filt_ref.shape[0]
    entry = lax.broadcasted_iota(jnp.int32, (vocab, seq), 0)
    chosen = (entry == tokens_ref[...]).astype(F32).astype(BF16)
    for m in range(3):
        table_ref[m] = (dot(chosen, gproj_ref[0, m]) * scale_ref[...]).astype(BF16)


def forward_kernel(proj_ref, taps_ref, kern_ref, fwd_ref, inv_ref, gated_ref, filt_ref, spec_ref):
    projs = [proj_ref.at[:, m] for m in range(3)]
    tap_count, chans = kern_ref.shape
    blocks = filt_ref.shape[0] // tap_count
    row = lax.broadcasted_iota(jnp.int32, (tap_count, chans), 0)
    sign = jnp.where(row % 2 == 0, 1.0, -1.0)
    kr, ki, kn = kernel_spectrum(fwd_ref, kern_ref, row)
    zero = jnp.zeros((tap_count, chans), F32)
    before = [zero] * 3
    last_r, last_i = zero, zero
    for b in range(blocks):
        here = pl.ds(b * tap_count, tap_count)
        streams = []
        for m in range(3):
            current = proj_block(projs, m, b, tap_count)
            streams.append(short_filter(taps_ref, m, current, before[m], row))
            before[m] = current
        part = dot(fwd_ref[...], (streams[1] * streams[2]).astype(BF16))
        pr, pi = part[:tap_count], part[tap_count:]
        wr = last_r + sign * pr
        wi = last_i + sign * pi
        last_r, last_i = pr, pi
        spec_ref[b, :tap_count, :] = wr.astype(BF16)
        spec_ref[b, tap_count:, :] = wi.astype(BF16)
        mixed = jnp.concatenate([wr * kr - wi * ki, wr * ki + wi * kn], axis=0)
        filtered = dot(inv_ref[...], mixed.astype(BF16))
        filt_ref[here, :] = filtered.astype(BF16)
        gated_ref[here, :] = (streams[0] * filtered).astype(BF16)


def backward_kernel(
    gg_ref, proj_ref, taps_ref, kern_ref, fwd_ref, inv_ref, filt_ref, spec_ref,
    gproj_ref, gkern_ref, gtaps_ref, grad_spec,
):
    projs = [proj_ref.at[:, m] for m in range(3)]
    tap_count, chans = kern_ref.shape
    blocks = filt_ref.shape[0] // tap_count
    row = lax.broadcasted_iota(jnp.int32, (tap_count, chans), 0)
    sign = jnp.where(row % 2 == 0, 1.0, -1.0)
    kr, ki, kn = kernel_spectrum(fwd_ref, kern_ref, row)
    zero = jnp.zeros((tap_count, chans), F32)
    sum_r, sum_i = zero, zero
    last = zero
    for b in range(blocks):
        here = pl.ds(b * tap_count, tap_count)
        current = proj_block(projs, 0, b, tap_count)
        query = short_filter(taps_ref, 0, current, last, row)
        last = current
        part = dot(fwd_ref[...], (gg_ref[here, :].astype(F32) * query).astype(BF16))
        grad_spec[b] = part
        gr, gi = sign * part[:tap_count], sign * part[tap_count:]
        wr = spec_ref[b, :tap_count, :].astype(F32)
        wi = spec_ref[b, tap_count:, :].astype(F32)
        rr, ii = wr * gr, wi * gi
        sum_r = sum_r + jnp.where(row == 0, rr, rr + ii)
        sum_i = sum_i + jnp.where(row == 0, ii, wr * gi - wi * gr)
    gkern_ref[...] = exact(
        inv_ref[...].astype(F32), jnp.concatenate([sum_r, sum_i], axis=0)
    )
    after = [zero] * 3
    next_r, next_i = zero, zero
    sums = [jnp.zeros((1, chans), F32) for _ in range(9)]
    for b in reversed(range(blocks)):
        chunk, start = divmod(b * tap_count, projs[0].shape[1])
        here = pl.ds(b * tap_count, tap_count)
        gr, gi = grad_spec[b, :tap_count, :], grad_spec[b, tap_count:, :]
        vr, vi = gr + sign * next_r, gi + sign * next_i
        next_r, next_i = gr, gi
        mixed = jnp.concatenate([vr * kr + vi * ki, vi * kn - vr * ki], axis=0)
        grad_prod = dot(inv_ref[...], mixed.astype(BF16))
        shifts, shorts = [], []
        for m in range(3):
            current = proj_block(projs, m, b, tap_count)
            before = proj_block(projs, m, b - 1, tap_count) if b else zero
            shifts.append([current, later(current, before, 1, row), later(current, before, 2, row)])
            if m:
                shorts.append(sum(taps_ref[3 * j + m : 3 * j + m + 1, :] * shifts[m][j] for j in range(3)))
        grads = [
            gg_ref[here, :].astype(F32) * filt_ref[here, :].astype(F32),
            grad_prod * shorts[1],
            grad_prod * shorts[0],
        ]
        for m in range(3):
            grad = grads[m]
            out = (
                taps_ref[m : m + 1, :] * grad
                + taps_ref[3 + m : 4 + m, :] * sooner(grad, after[m], 1, row)
                + taps_ref[6 + m : 7 + m, :] * sooner(grad, after[m], 2, row)
            )
            after[m] = grad
            gproj_ref[chunk, m, start : start + tap_count, :] = out.astype(BF16)
            for j in range(3):
                sums[3 * j + m] = sums[3 * j + m] + jnp.sum(
                    grad * shifts[m][j], axis=0, keepdims=True
                )
    for index in range(9):
        gtaps_ref[index : index + 1, :] = sums[index]


PARAMS = pltpu.CompilerParams(vmem_limit_bytes=56 * 1024 * 1024)


def conv_forward(proj, taps, kern, matrices, tokens=None):
    tap_count, chans = kern.shape
    seq = proj.shape[0] * proj.shape[2] if tokens is None else tokens.shape[0]
    results = [
        jax.ShapeDtypeStruct((seq, chans), BF16),
        jax.ShapeDtypeStruct((seq, chans), BF16),
        jax.ShapeDtypeStruct((seq // tap_count, 2 * tap_count, chans), BF16),
    ]
    operands = (proj, taps, kern, matrices[0], matrices[2])
    if tokens is not None:
        results.append(jax.ShapeDtypeStruct((1, 3, seq, chans), BF16))
        operands = (tokens[:, None], *operands)
    return pl.pallas_call(
        forward_kernel if tokens is None else lookup_kernel,
        out_shape=results,
        compiler_params=PARAMS,
        name="conv_forward",
    )(*operands)


def conv_backward(gg, proj, taps, kern, matrices, saved, tokens=None, scale=None):
    tap_count, chans = kern.shape
    seq = gg.shape[0]
    scratch = [pltpu.VMEM((seq // tap_count, 2 * tap_count, chans), F32)]
    operands = (gg, proj, taps, kern, matrices[0], matrices[1], *saved)
    first = jax.ShapeDtypeStruct(proj.shape, BF16)
    if tokens is not None:
        first = jax.ShapeDtypeStruct((3, scale.shape[0], chans), BF16)
        scratch.append(pltpu.VMEM(proj.shape, BF16))
        operands = (tokens[None, :], scale, *operands)
    return pl.pallas_call(
        backward_kernel if tokens is None else collect_kernel,
        out_shape=(
            first,
            jax.ShapeDtypeStruct(kern.shape, F32),
            jax.ShapeDtypeStruct((9, chans), F32),
        ),
        scratch_shapes=scratch,
        compiler_params=PARAMS,
        name="conv_backward",
    )(*operands)


def table_projection(table, weights, ctx, order, kind):
    vocab, feats = table.shape
    sub = weights.shape[2] // lax.axis_size("ctx")
    if sub % 128:
        columns = jnp.stack(
            [lax.dynamic_slice_in_dim(weights, (ctx ^ r) * sub, sub, 2) for r in order]
        )
        return jnp.einsum("vd,rmdc->rmvc", table, columns, preferred_element_type=F32).astype(kind)

    def kernel(where_ref, table_ref, weights_ref, out_ref):
        for m in range(3):
            out_ref[0, m] = dot(table_ref[...], weights_ref[m]).astype(kind)

    return pl.pallas_call(
        kernel,
        grid_spec=pltpu.PrefetchScalarGridSpec(
            num_scalar_prefetch=1,
            grid=(len(order),),
            in_specs=[
                pl.BlockSpec((vocab, feats), lambda r, where: (0, 0)),
                pl.BlockSpec((3, feats, sub), lambda r, where: (0, 0, where[r])),
            ],
            out_specs=pl.BlockSpec((1, 3, vocab, sub), lambda r, where: (r, 0, 0, 0)),
        ),
        out_shape=jax.ShapeDtypeStruct((len(order), 3, vocab, sub), kind),
        compiler_params=PARAMS,
        name="table_projection",
    )(jnp.stack([ctx ^ r for r in order]), table, weights)


def input_projection(rows_in, pieces, ctx):
    rows, full_width = rows_in.shape
    feats, chans = pieces[0].shape[1:]
    count = len(pieces)
    sub = chans // count

    def kernel(ctx_ref, rows_ref, *refs):
        weights, (normed_ref, proj_ref, scale_ref) = refs[:count], refs[count:]

        @pl.when(pl.program_id(0) == 0)
        def _():
            total = jnp.zeros((rows, 1), F32)
            for q in range(count):
                part = rows_ref[:, q * feats : (q + 1) * feats].astype(F32)
                total = total + jnp.sum(part * part, axis=1, keepdims=True)
            scale_ref[...] = lax.rsqrt(total / full_width + EPSILON)
            for q in range(count):
                part = rows_ref[:, q * feats : (q + 1) * feats].astype(F32)
                normed_ref[q] = (part * scale_ref[...]).astype(BF16)

        total = jnp.zeros((rows, chans), F32)
        for r in range(count):
            start = pl.multiple_of((ctx_ref[0] ^ r) * feats, feats)
            total = total + dot(rows_ref[:, pl.ds(start, feats)], weights[r][0])
        total = (total * scale_ref[...]).astype(BF16)
        for q in range(count):
            proj_ref[q, 0] = total[:, q * sub : (q + 1) * sub]

    return pl.pallas_call(
        kernel,
        grid_spec=pltpu.PrefetchScalarGridSpec(
            num_scalar_prefetch=1,
            grid=(3,),
            in_specs=[pl.BlockSpec((rows, full_width), lambda m, ctx: (0, 0))]
            + [pl.BlockSpec((1, feats, chans), lambda m, ctx: (m, 0, 0))] * count,
            out_specs=[
                pl.BlockSpec((count, rows, feats), lambda m, ctx: (0, 0, 0)),
                pl.BlockSpec((count, 1, rows, sub), lambda m, ctx: (0, m, 0, 0)),
                pl.BlockSpec((rows, 1), lambda m, ctx: (0, 0)),
            ],
        ),
        out_shape=(
            jax.ShapeDtypeStruct((count, rows, feats), BF16),
            jax.ShapeDtypeStruct((count, 3, rows, sub), BF16),
            jax.ShapeDtypeStruct((rows, 1), F32),
        ),
        compiler_params=PARAMS,
        name="input_projection",
    )(ctx[None], rows_in, *pieces)


def input_gradient(gproj, pieces, rows_in, scale, ctx, dp):
    rows, full_width = rows_in.shape
    feats, chans = pieces[0].shape[1:]
    count = len(pieces)
    sub = chans // count
    tile = min(256, feats)
    steps, half = feats // tile, rows // 2

    def kernel(ctx_ref, gproj_ref, rows_ref, scale_ref, *refs):
        weights, outs, (flat, grads) = refs[:count], refs[count:-2], refs[-2:]
        step = pl.program_id(0)

        @pl.when(step == 0)
        def _():
            for m in range(3):
                for q in range(count):
                    flat[m, :, q * sub : (q + 1) * sub] = gproj_ref[q, m]

        columns = pl.ds(pl.multiple_of(step * tile, tile), tile)
        for r in range(count):
            total = dot_t(flat[0], weights[r][0])
            for m in (1, 2):
                total = total + dot_t(flat[m], weights[r][m])
            grads[ctx_ref[0] ^ r, :, columns] = total * scale_ref[...]

        @pl.when(step == steps - 1)
        def _():
            stat = jnp.zeros((rows, 1), F32)
            for q in range(count):
                part = rows_ref[:, q * feats : (q + 1) * feats].astype(F32)
                stat = stat + jnp.sum(part * grads[q], axis=1, keepdims=True)
            stat = stat * scale_ref[...] * scale_ref[...] / full_width
            for shift in range(count):
                q = ctx_ref[1 + shift]
                start = pl.multiple_of(q * feats, feats)
                part = rows_ref[:, pl.ds(start, feats)].astype(F32)
                total = (grads[q] - part * stat).astype(BF16)
                if shift == 0:
                    outs[0][...] = total
                else:
                    outs[shift][...] = total[:half]
                    outs[count - 1 + shift][...] = total[half:]

    outs = pl.pallas_call(
        kernel,
        grid_spec=pltpu.PrefetchScalarGridSpec(
            num_scalar_prefetch=1,
            grid=(steps,),
            in_specs=[
                pl.BlockSpec(gproj.shape, lambda t, ctx: (0, 0, 0, 0)),
                pl.BlockSpec((rows, full_width), lambda t, ctx: (0, 0)),
                pl.BlockSpec((rows, 1), lambda t, ctx: (0, 0)),
            ]
            + [pl.BlockSpec((3, tile, chans), lambda t, ctx: (0, t, 0))] * count,
            out_specs=[pl.BlockSpec((rows, feats), lambda t, ctx: (0, 0))]
            + [pl.BlockSpec((half, feats), lambda t, ctx: (0, 0))] * (2 * count - 2),
            scratch_shapes=[
                pltpu.VMEM((3, rows, chans), BF16),
                pltpu.VMEM((count, rows, feats), F32),
            ],
        ),
        out_shape=[jax.ShapeDtypeStruct((rows, feats), BF16)]
        + [jax.ShapeDtypeStruct((half, feats), BF16)] * (2 * count - 2),
        compiler_params=PARAMS,
        name="input_gradient",
    )(jnp.concatenate([ctx[None], targets(dp, count)]), gproj, rows_in, scale, *pieces)
    return outs[0], outs[1:count], outs[count:]


def grad_in_kernel(left, pieces, ctx):
    feats, depth = left.shape
    count, sub = len(pieces), pieces[0].shape[2]
    if sub % 128:
        columns = jnp.concatenate([pick(jnp.stack(pieces), ctx ^ q) for q in range(count)], axis=2)
        columns = columns[:3]
        return jnp.einsum("dk,mkc->mdc", left, columns, preferred_element_type=F32)

    tile = min(256, feats)

    def kernel(ctx_ref, left_ref, *refs):
        out_ref = refs[count]
        for r in range(count):
            columns = pl.ds(pl.multiple_of((ctx_ref[0] ^ r) * sub, sub), sub)
            for m in range(3):
                out_ref[m, :, columns] = dot(left_ref[...], refs[r][m])

    return pl.pallas_call(
        kernel,
        grid_spec=pltpu.PrefetchScalarGridSpec(
            num_scalar_prefetch=1,
            grid=(feats // tile,),
            in_specs=[pl.BlockSpec((tile, depth), lambda t, ctx: (t, 0))]
            + [pl.BlockSpec((3, depth, sub), lambda t, ctx: (0, 0, 0))] * count,
            out_specs=pl.BlockSpec((3, tile, sub * count), lambda t, ctx: (0, t, 0)),
        ),
        out_shape=jax.ShapeDtypeStruct((3, feats, sub * count), F32),
        compiler_params=PARAMS,
        name="grad_project_in",
    )(ctx[None], left, *pieces)


def grad_out_kernel(early, late, right, ctx, sec):
    depth, feats = right.shape
    count, sub = len(early), early[0].shape[1]

    def kernel(where_ref, right_ref, *refs):
        out_ref = refs[2 * count]
        for r in range(count):
            for index, piece in ((0, refs[r].at[...]), (1, refs[count + r].at[0])):

                @pl.when((pl.program_id(0) == r) & (where_ref[count] == index))
                def _():
                    out_ref[...] = lax.dot_general(
                        piece[...],
                        right_ref[...],
                        (((0,), (0,)), ((), ())),
                        preferred_element_type=F32,
                    )

    return pl.pallas_call(
        kernel,
        grid_spec=pltpu.PrefetchScalarGridSpec(
            num_scalar_prefetch=1,
            grid=(count,),
            in_specs=[pl.BlockSpec((depth, feats), lambda r, where: (0, 0))]
            + [pl.BlockSpec((depth, sub), lambda r, where: (0, 0))] * count
            + [pl.BlockSpec((1, depth, sub), lambda r, where: (3, 0, 0))] * count,
            out_specs=pl.BlockSpec((sub, feats), lambda r, where: (where[r], 0)),
        ),
        out_shape=jax.ShapeDtypeStruct((sub * count, feats), F32),
        compiler_params=PARAMS,
        name="grad_project_out",
    )(jnp.stack([ctx ^ r for r in range(count)] + [sec]), right, *early, *late)


def together(*values):
    return lax.optimization_barrier(values)


def targets(dp, count):
    return (dp + jnp.arange(count, dtype=jnp.int32)) % count


def output_projection(gated, weights, dp):
    count, rows, sub = gated.shape
    chans, full_width = weights.shape
    parts = lax.axis_size("dp")
    width, half = full_width // parts, rows // 2

    def kernel(where_ref, gated_ref, weights_ref, *refs):
        outs, flat = refs[:-1], refs[-1]

        @pl.when(pl.program_id(0) == 0)
        def _():
            for q in range(count):
                flat[:, q * sub : (q + 1) * sub] = gated_ref[q]

        total = dot(flat[...], weights_ref[...]).astype(BF16)
        @pl.when(pl.program_id(0) == 0)
        def _():
            outs[0][...] = total

        for shift in range(1, parts):

            @pl.when(pl.program_id(0) == shift)
            def _():
                outs[shift][...] = total[:half]
                outs[parts - 1 + shift][...] = total[half:]

    outs = pl.pallas_call(
        kernel,
        grid_spec=pltpu.PrefetchScalarGridSpec(
            num_scalar_prefetch=1,
            grid=(parts,),
            in_specs=[
                pl.BlockSpec(gated.shape, lambda q, where: (0, 0, 0)),
                pl.BlockSpec((chans, width), lambda q, where: (0, where[q])),
            ],
            out_specs=[pl.BlockSpec((rows, width), lambda q, where: (0, 0))]
            + [pl.BlockSpec((half, width), lambda q, where: (0, 0))] * (2 * parts - 2),
            scratch_shapes=[pltpu.VMEM((rows, chans), BF16)],
        ),
        out_shape=[jax.ShapeDtypeStruct((rows, width), BF16)]
        + [jax.ShapeDtypeStruct((half, width), BF16)] * (2 * parts - 2),
        compiler_params=PARAMS,
        name="output_projection",
    )(targets(dp, parts), gated, weights)
    return outs[0], outs[1:parts], outs[parts:]


def ctx_swap_in(value, section):
    me = lax.axis_index("ctx")
    count = value.shape[0]
    came = [pick(value, me)]
    for r in range(1, count):
        came.append(ctx_xor(pick(value, me ^ r), r, (section,)))
    came = jnp.stack(came)
    return [pick(came, me ^ q) for q in range(count)]


def ctx_swap(value):
    return lax.all_to_all(value, "ctx", split_axis=0, concat_axis=0, tiled=True)


def local(
    token_ids, embedding, project_in, short_taps, filter_taps, decay_rates, project_out, cotangent
):
    n_ctx, n_dp = lax.axis_size("ctx"), lax.axis_size("dp")
    sec, dp, ctx = (lax.axis_index(axis) for axis in ("section", "dp", "ctx"))
    first = sec == 0
    rows, vocab = token_ids.shape[0], embedding.shape[0]
    seq = rows * n_ctx
    weights_in = jnp.transpose(project_in[0], (1, 0, 2))
    weights_out = project_out[0]
    feats, chans = weights_out.shape[1], weights_out.shape[0]
    full_width = feats * n_ctx
    sub = chans // n_ctx

    if n_ctx == n_dp:
        half = vocab // 2
        mine = lax.dynamic_slice_in_dim(embedding, sec * half, half, 0)
        came = []
        for i in range(1, n_dp):
            shifts = (i, i % (n_dp - 1) + 1)
            came.append(
                send(
                    mine,
                    ("section", "dp", "ctx"),
                    lambda s, z, k: (0, (z + shifts[s]) % n_dp, k) if z == k else None,
                )
            )
        offset = (dp - ctx) % n_dp
        low, high = embedding[:half], embedding[half:]
        for i in range(1, n_dp):
            low = jnp.where(offset == i, came[i - 1], low)
            high = jnp.where(offset == i % (n_dp - 1) + 1, came[i - 1], high)
        table = jnp.concatenate([low, high], axis=0)
    else:
        table = lax.dynamic_slice_in_dim(
            lax.all_gather(embedding, "dp", axis=1, tiled=True), ctx * feats, feats, 1
        )
    table_float = table.astype(F32)
    squares = jnp.sum(table_float * table_float, axis=1)
    tokens = token_ids.astype(F32)[None]
    held = [0]
    bit = n_ctx // 2
    while bit:
        came = ctx_xor(jnp.concatenate([squares, tokens.reshape(-1)]), bit, (0,))
        squares = squares + came[:vocab]
        tokens = jnp.concatenate([tokens, came[vocab:].reshape(-1, rows)], axis=0)
        held += [r | bit for r in held]
        bit //= 2
    table_inv = lax.rsqrt(squares[:, None] / full_width + EPSILON)
    tokens = jnp.stack([tokens[held.index(r)] for r in range(n_ctx)])
    tokens = jnp.concatenate([pick(tokens, ctx ^ q) for q in range(n_ctx)]).astype(jnp.int32)

    def own(value):
        return lax.dynamic_slice_in_dim(value, ctx * sub, sub, value.ndim - 1)

    taps = own(short_taps[0]).reshape(9, sub)
    filters = own(filter_taps[0])
    tap_count = filters.shape[0]
    positions = jnp.arange(tap_count).astype(F32)[:, None]
    damping = jnp.exp(-own(decay_rates) * positions / tap_count)
    kern = filters * damping
    matrices = spectra(tap_count)

    vocabulary = jnp.arange(vocab, dtype=jnp.int32)[None, :]
    first_input = dot((token_ids[:, None] == vocabulary).astype(BF16), embedding)

    out_full = lax.all_gather(weights_out, "ctx", axis=1, tiled=True)
    in_far = far_gather(weights_in, (1,))
    far = sorted(in_far)[1:]

    order = scatter_order(n_ctx)
    kept = order[: n_ctx // 2]
    sent = table_projection(table, weights_in, ctx, [r | 1 for r in kept], BF16)
    arrived = ctx_xor(sent, 1, (0,))
    partial = table_projection(table, weights_in, ctx, kept, F32) + arrived.astype(F32)
    bit = 2
    while bit < n_ctx:
        stays, gone = jnp.split(partial, 2, axis=0)
        partial = stays + ctx_xor(gone.astype(BF16), bit, (0,)).astype(F32)
        bit *= 2
    table_proj = (partial[0] * table_inv).astype(BF16)
    gated_0, *saved_0, proj_0 = conv_forward(table_proj, taps, kern, matrices, tokens)
    cot_stack = jnp.stack(dp_gather(cotangent, 1))
    gated_0, cot_stack = together(gated_0, cot_stack)
    gated_rows = jnp.stack(ctx_swap_in(gated_0.reshape(n_ctx, rows, sub), 0))
    shares = output_projection(gated_rows, out_full, dp)
    middle_stack, (gated_0,), late = cross_gather(
        shares, first_input, 0, [gated_0], [in_far[r] for r in far]
    )
    gated_all_0 = ctx_gather(gated_0, (0,))

    in_far.update(zip(far, late))
    in_pieces = []
    for r in sorted(in_far):
        in_pieces += [in_far[r], ctx_xor(in_far[r], 1, (1,))]
    def gated_gradient(parts):
        total = dot_t(jnp.concatenate(parts, axis=1), out_full).astype(BF16)
        split = jnp.transpose(total.reshape(rows, n_ctx, sub), (1, 0, 2))
        return ctx_swap(split).reshape(seq, sub)

    cot_parts = in_order(cot_stack, dp)
    middle_stack, gated_grad_1 = together(middle_stack, gated_gradient(cot_parts))
    middle_all = jnp.concatenate(in_order(middle_stack, dp), axis=1)
    normed, proj_rows, scale = input_projection(middle_all, in_pieces, ctx)
    proj_1 = ctx_swap(proj_rows)
    gated_1, *saved_1 = conv_forward(proj_1, taps, kern, matrices)

    gproj_1, gkern_1, gtaps_1 = conv_backward(
        gated_grad_1, proj_1, taps, kern, matrices, saved_1
    )
    gproj_1, *gated_all_0 = together(gproj_1, *gated_all_0)
    gproj_rows = ctx_swap(gproj_1)
    shares = input_gradient(gproj_rows, in_pieces, middle_all, scale, ctx, dp)
    back_stack, _, (normed, gproj_1, gated_1) = cross_gather(
        shares, cotangent, 1, [], [normed, gproj_1, gated_1]
    )

    normed_cols = jnp.concatenate([part.T for part in ctx_swap_in(normed, 1)], axis=1)
    gproj_1 = gproj_1.transpose(1, 0, 2, 3).reshape(3, seq, sub)
    gproj_all = ctx_gather(jnp.concatenate([gproj_1, gated_1[None]]), (1,))

    back_stack, normed_cols, *gproj_all = together(back_stack, normed_cols, *gproj_all)
    back_parts = in_order(back_stack, dp)
    table_grad, gkern_0, gtaps_0 = conv_backward(
        gated_gradient(back_parts), proj_0, taps, kern, matrices, saved_0, tokens, table_inv
    )

    grads = jnp.stack([jnp.where(first, a, b) for a, b in zip(back_parts, cot_parts)])
    grad_cols = ctx_swap(grads).reshape(seq, feats)
    grad_cols, table_grad = together(grad_cols, table_grad)
    grad_out = grad_out_kernel(gated_all_0, gproj_all, grad_cols, ctx, sec)
    table_pieces = ctx_gather(table_grad, (0,))
    grad_in = lax.cond(
        first,
        lambda: grad_in_kernel(table.T, table_pieces, ctx),
        lambda: grad_in_kernel(normed_cols, gproj_all, ctx),
    )

    gkern = jnp.where(first, gkern_0, gkern_1)
    gtaps = jnp.where(first, gtaps_0, gtaps_1)
    gdecay = -jnp.sum(gkern * kern * positions, axis=0, keepdims=True) / tap_count
    small = jnp.concatenate([gkern * damping, gdecay, gtaps], axis=0)
    small = jnp.stack(ctx_gather(small, (0, 1)))
    small = jnp.concatenate([pick(small, ctx ^ q) for q in range(n_ctx)], axis=1)
    return (
        jnp.transpose(grad_in, (1, 0, 2))[None],
        grad_out[None],
        small[:tap_count][None],
        small[tap_count][None],
        small[tap_count + 1 :].reshape(1, 3, 3, chans),
    )


def solution(mesh):
    return jax.shard_map(
        local,
        mesh=mesh,
        in_specs=(
            P("ctx"),
            P(None, "dp"),
            P("section", "ctx", None, "dp"),
            P("section", None, None, "dp"),
            P("section", None, "dp"),
            P("section", "dp"),
            P("section", "dp", "ctx"),
            P("ctx", "dp"),
        ),
        out_specs=(
            P("section", "ctx", None, "dp"),
            P("section", "dp", "ctx"),
            P("section", None, "dp"),
            P("section", "dp"),
            P("section", None, None, "dp"),
        ),
        check_vma=False,
    )
```

```python
import functools

import jax
import jax.numpy as jnp
import numpy as np
from jax import lax
from jax.experimental import pallas as pl
from jax.experimental.pallas import tpu as pltpu
from jax.sharding import PartitionSpec as P

EPSILON = 1e-06
F32 = jnp.float32
BF16 = jnp.bfloat16


def dot(left, right):
    return jnp.dot(left, right, preferred_element_type=F32)


def dot_t(left, right):
    return lax.dot_general(left, right, (((1,), (1,)), ((), ())), preferred_element_type=F32)


def exact(left, right):
    return jnp.dot(left, right, preferred_element_type=F32, precision=lax.Precision.HIGHEST)


def pick(stack, index):
    return lax.dynamic_index_in_dim(stack, index, 0, keepdims=False)


def send(value, axes, route):
    sizes = [lax.axis_size(axis) for axis in axes]
    pairs = []
    for source, place in enumerate(np.ndindex(*sizes)):
        target = route(*place)
        if target is not None:
            pairs.append((source, int(np.ravel_multi_index(target, sizes))))
    return lax.ppermute(value, axes, pairs)


def ctx_xor(value, mask, sections):
    return send(
        value, ("section", "ctx"), lambda s, k: (s, k ^ mask) if s in sections else None
    )


def ctx_gather(value, sections):
    count = lax.axis_size("ctx")
    held = {0: value}
    bit = count // 2
    while bit:
        for r in list(held):
            held[r | bit] = ctx_xor(held[r], bit, sections)
        bit //= 2
    return [held[r] for r in range(count)]


def far_gather(value, sections):
    held = {0: value}
    bit = lax.axis_size("ctx") // 2
    while bit > 1:
        for r in list(held):
            held[r | bit] = ctx_xor(held[r], bit, sections)
        bit //= 2
    return held


def scatter_order(count):
    if count == 1:
        return [0]
    inner = scatter_order(count // 2)
    return [2 * r for r in inner] + [2 * r + 1 for r in inner]


def dp_gather(value, section):
    count = lax.axis_size("dp")
    pieces = [value]
    for _ in range(count - 1):
        pieces.append(
            send(
                pieces[-1],
                ("section", "dp"),
                lambda s, z: (s, (z + 1) % count) if s == section else None,
            )
        )
    return pieces


def cross_gather(shares, base, source, early, late=(), begin=None):
    count = lax.axis_size("dp")
    half = base.shape[0] // 2
    def move(value, shift):
        return send(
            value,
            ("section", "dp"),
            lambda s, z: (1 - s, (z + shift) % count) if s == source else None,
        )

    straight, *shares = shares
    straight = move(straight, 0)
    arrivals = [[move(shares[0][shift - 1], shift) for shift in range(1, count)]]
    tied = together(*arrivals[0], *shares[1])
    arrivals[0], shares_left = list(tied[: count - 1]), tied[count - 1 :]
    arrivals.append([move(shares_left[shift - 1], shift) for shift in range(1, count)])
    for index, start in enumerate((0, half)):
        arrivals[index].append(straight[start : start + half])

    def total(index, values):
        start = index * half
        result = base[start : start + half].astype(F32)
        for value in values:
            result = result + value.astype(F32)
        return result.astype(BF16)

    part = total(0, arrivals[0])
    if early:
        part, *early = together(part, *early)
    begun = begin(*early) if begin else []
    first = dp_gather(part, 1 - source)
    marker = min(2, count - 1)
    first[marker], *arrivals[1] = together(first[marker], *arrivals[1])
    part, *late = together(total(1, arrivals[1]), *late)
    second = dp_gather(part, 1 - source)
    if begun and count > 1:
        second[1], *begun = together(second[1], *begun)
    stack = jnp.stack([jnp.concatenate(pair, axis=0) for pair in zip(first, second)])
    return stack, early, begun or late


def in_order(stack, me):
    return [pick(stack, (me - q) % stack.shape[0]) for q in range(stack.shape[0])]


def spectra(taps):
    freq = np.arange(taps)[:, None]
    time = np.arange(taps)[None, :]
    angle = np.pi * freq * time / taps
    nyquist = np.where(time % 2 == 0, 1.0, -1.0)
    forward = np.concatenate(
        [np.cos(angle), np.where(freq == 0, nyquist, -np.sin(angle))], axis=0
    )
    weight = np.where(freq == 0, 1.0, 2.0) / (2 * taps)
    inverse = np.concatenate(
        [weight * np.cos(angle), np.where(freq == 0, nyquist, -2 * np.sin(angle)) * np.where(freq == 0, weight, 1.0 / (2 * taps))],
        axis=0,
    ).T
    sign = np.where(np.arange(2 * taps) % taps % 2 == 0, 1.0, -1.0)
    return [jnp.asarray(m, BF16) for m in (forward, inverse, inverse * sign[None, :])]


def later(current, before, steps, row):
    return jnp.where(row < steps, pltpu.roll(before, steps, 0), pltpu.roll(current, steps, 0))


def sooner(current, after, steps, row):
    count = current.shape[0]
    return jnp.where(
        row >= count - steps,
        pltpu.roll(after, count - steps, 0),
        pltpu.roll(current, count - steps, 0),
    )


def kernel_spectrum(fwd_ref, kern_ref, row):
    tap_count = kern_ref.shape[0]
    kern = dot(fwd_ref[...], kern_ref[...].astype(BF16))
    real, imag = kern[:tap_count], kern[tap_count:]
    return real, jnp.where(row == 0, 0.0, imag), jnp.where(row == 0, imag, real)


def proj_block(projs, m, b, tap_count):
    chunk, start = divmod(b * tap_count, projs[m].shape[1])
    return projs[m][chunk, start : start + tap_count, :].astype(F32)


def short_filter(taps_ref, m, current, before, row):
    return (
        taps_ref[m : m + 1, :] * current
        + taps_ref[3 + m : 4 + m, :] * later(current, before, 1, row)
        + taps_ref[6 + m : 7 + m, :] * later(current, before, 2, row)
    )


def lookup_kernel(
    tokens_ref, table_ref, taps_ref, kern_ref, fwd_ref, inv_ref,
    gated_ref, filt_ref, spec_ref, proj_ref,
):
    tap_count, vocab = kern_ref.shape[0], table_ref.shape[1]
    entry = lax.broadcasted_iota(jnp.int32, (tap_count, vocab), 1)
    for b in range(filt_ref.shape[0] // tap_count):
        here = pl.ds(b * tap_count, tap_count)
        chosen = (entry == tokens_ref[here, :]).astype(F32).astype(BF16)
        for m in range(3):
            proj_ref[0, m, here, :] = dot(chosen, table_ref[m]).astype(BF16)
    forward_kernel(
        proj_ref, taps_ref, kern_ref, fwd_ref, inv_ref, gated_ref, filt_ref, spec_ref
    )


def collect_kernel(
    tokens_ref, scale_ref, gg_ref, proj_ref, taps_ref, kern_ref, fwd_ref, inv_ref, filt_ref, spec_ref,
    table_ref, gkern_ref, gtaps_ref, grad_spec, gproj_ref,
):
    backward_kernel(
        gg_ref, proj_ref, taps_ref, kern_ref, fwd_ref, inv_ref, filt_ref, spec_ref,
        gproj_ref, gkern_ref, gtaps_ref, grad_spec,
    )
    _, vocab, _ = table_ref.shape
    seq = filt_ref.shape[0]
    entry = lax.broadcasted_iota(jnp.int32, (vocab, seq), 0)
    chosen = (entry == tokens_ref[...]).astype(F32).astype(BF16)
    for m in range(3):
        table_ref[m] = (dot(chosen, gproj_ref[0, m]) * scale_ref[...]).astype(BF16)


def forward_kernel(proj_ref, taps_ref, kern_ref, fwd_ref, inv_ref, gated_ref, filt_ref, spec_ref):
    projs = [proj_ref.at[:, m] for m in range(3)]
    tap_count, chans = kern_ref.shape
    blocks = filt_ref.shape[0] // tap_count
    row = lax.broadcasted_iota(jnp.int32, (tap_count, chans), 0)
    sign = jnp.where(row % 2 == 0, 1.0, -1.0)
    kr, ki, kn = kernel_spectrum(fwd_ref, kern_ref, row)
    zero = jnp.zeros((tap_count, chans), F32)
    before = [zero] * 3
    last_r, last_i = zero, zero
    for b in range(blocks):
        here = pl.ds(b * tap_count, tap_count)
        streams = []
        for m in range(3):
            current = proj_block(projs, m, b, tap_count)
            streams.append(short_filter(taps_ref, m, current, before[m], row))
            before[m] = current
        part = dot(fwd_ref[...], (streams[1] * streams[2]).astype(BF16))
        pr, pi = part[:tap_count], part[tap_count:]
        wr = last_r + sign * pr
        wi = last_i + sign * pi
        last_r, last_i = pr, pi
        spec_ref[b, :tap_count, :] = wr.astype(BF16)
        spec_ref[b, tap_count:, :] = wi.astype(BF16)
        mixed = jnp.concatenate([wr * kr - wi * ki, wr * ki + wi * kn], axis=0)
        filtered = dot(inv_ref[...], mixed.astype(BF16))
        filt_ref[here, :] = filtered.astype(BF16)
        gated_ref[here, :] = (streams[0] * filtered).astype(BF16)


def backward_kernel(
    gg_ref, proj_ref, taps_ref, kern_ref, fwd_ref, inv_ref, filt_ref, spec_ref,
    gproj_ref, gkern_ref, gtaps_ref, grad_spec,
):
    projs = [proj_ref.at[:, m] for m in range(3)]
    tap_count, chans = kern_ref.shape
    blocks = filt_ref.shape[0] // tap_count
    row = lax.broadcasted_iota(jnp.int32, (tap_count, chans), 0)
    sign = jnp.where(row % 2 == 0, 1.0, -1.0)
    kr, ki, kn = kernel_spectrum(fwd_ref, kern_ref, row)
    zero = jnp.zeros((tap_count, chans), F32)
    sum_r, sum_i = zero, zero
    last = zero
    for b in range(blocks):
        here = pl.ds(b * tap_count, tap_count)
        current = proj_block(projs, 0, b, tap_count)
        query = short_filter(taps_ref, 0, current, last, row)
        last = current
        part = dot(fwd_ref[...], (gg_ref[here, :].astype(F32) * query).astype(BF16))
        grad_spec[b] = part
        gr, gi = sign * part[:tap_count], sign * part[tap_count:]
        wr = spec_ref[b, :tap_count, :].astype(F32)
        wi = spec_ref[b, tap_count:, :].astype(F32)
        rr, ii = wr * gr, wi * gi
        sum_r = sum_r + jnp.where(row == 0, rr, rr + ii)
        sum_i = sum_i + jnp.where(row == 0, ii, wr * gi - wi * gr)
    gkern_ref[...] = exact(
        inv_ref[...].astype(F32), jnp.concatenate([sum_r, sum_i], axis=0)
    )
    after = [zero] * 3
    next_r, next_i = zero, zero
    sums = [jnp.zeros((1, chans), F32) for _ in range(9)]
    for b in reversed(range(blocks)):
        chunk, start = divmod(b * tap_count, projs[0].shape[1])
        here = pl.ds(b * tap_count, tap_count)
        gr, gi = grad_spec[b, :tap_count, :], grad_spec[b, tap_count:, :]
        vr, vi = gr + sign * next_r, gi + sign * next_i
        next_r, next_i = gr, gi
        mixed = jnp.concatenate([vr * kr + vi * ki, vi * kn - vr * ki], axis=0)
        grad_prod = dot(inv_ref[...], mixed.astype(BF16))
        shifts, shorts = [], []
        for m in range(3):
            current = proj_block(projs, m, b, tap_count)
            before = proj_block(projs, m, b - 1, tap_count) if b else zero
            shifts.append([current, later(current, before, 1, row), later(current, before, 2, row)])
            if m:
                shorts.append(sum(taps_ref[3 * j + m : 3 * j + m + 1, :] * shifts[m][j] for j in range(3)))
        grads = [
            gg_ref[here, :].astype(F32) * filt_ref[here, :].astype(F32),
            grad_prod * shorts[1],
            grad_prod * shorts[0],
        ]
        for m in range(3):
            grad = grads[m]
            out = (
                taps_ref[m : m + 1, :] * grad
                + taps_ref[3 + m : 4 + m, :] * sooner(grad, after[m], 1, row)
                + taps_ref[6 + m : 7 + m, :] * sooner(grad, after[m], 2, row)
            )
            after[m] = grad
            gproj_ref[chunk, m, start : start + tap_count, :] = out.astype(BF16)
            for j in range(3):
                sums[3 * j + m] = sums[3 * j + m] + jnp.sum(
                    grad * shifts[m][j], axis=0, keepdims=True
                )
    for index in range(9):
        gtaps_ref[index : index + 1, :] = sums[index]


PARAMS = pltpu.CompilerParams(vmem_limit_bytes=56 * 1024 * 1024)


def conv_forward(proj, taps, kern, matrices, tokens=None):
    tap_count, chans = kern.shape
    seq = proj.shape[0] * proj.shape[2] if tokens is None else tokens.shape[0]
    results = [
        jax.ShapeDtypeStruct((seq, chans), BF16),
        jax.ShapeDtypeStruct((seq, chans), BF16),
        jax.ShapeDtypeStruct((seq // tap_count, 2 * tap_count, chans), BF16),
    ]
    operands = (proj, taps, kern, matrices[0], matrices[2])
    if tokens is not None:
        results.append(jax.ShapeDtypeStruct((1, 3, seq, chans), BF16))
        operands = (tokens[:, None], *operands)
    return pl.pallas_call(
        forward_kernel if tokens is None else lookup_kernel,
        out_shape=results,
        compiler_params=PARAMS,
        name="conv_forward",
    )(*operands)


def conv_backward(gg, proj, taps, kern, matrices, saved, tokens=None, scale=None):
    tap_count, chans = kern.shape
    seq = gg.shape[0]
    scratch = [pltpu.VMEM((seq // tap_count, 2 * tap_count, chans), F32)]
    operands = (gg, proj, taps, kern, matrices[0], matrices[1], *saved)
    first = jax.ShapeDtypeStruct(proj.shape, BF16)
    if tokens is not None:
        first = jax.ShapeDtypeStruct((3, scale.shape[0], chans), BF16)
        scratch.append(pltpu.VMEM(proj.shape, BF16))
        operands = (tokens[None, :], scale, *operands)
    return pl.pallas_call(
        backward_kernel if tokens is None else collect_kernel,
        out_shape=(
            first,
            jax.ShapeDtypeStruct(kern.shape, F32),
            jax.ShapeDtypeStruct((9, chans), F32),
        ),
        scratch_shapes=scratch,
        compiler_params=PARAMS,
        name="conv_backward",
    )(*operands)


def table_projection(table, weights, ctx, order, kind):
    vocab, feats = table.shape
    sub = weights.shape[2] // lax.axis_size("ctx")
    if sub % 128:
        columns = jnp.stack(
            [lax.dynamic_slice_in_dim(weights, (ctx ^ r) * sub, sub, 2) for r in order]
        )
        return jnp.einsum("vd,rmdc->rmvc", table, columns, preferred_element_type=F32).astype(kind)

    def kernel(where_ref, table_ref, weights_ref, out_ref):
        for m in range(3):
            out_ref[0, m] = dot(table_ref[...], weights_ref[m]).astype(kind)

    return pl.pallas_call(
        kernel,
        grid_spec=pltpu.PrefetchScalarGridSpec(
            num_scalar_prefetch=1,
            grid=(len(order),),
            in_specs=[
                pl.BlockSpec((vocab, feats), lambda r, where: (0, 0)),
                pl.BlockSpec((3, feats, sub), lambda r, where: (0, 0, where[r])),
            ],
            out_specs=pl.BlockSpec((1, 3, vocab, sub), lambda r, where: (r, 0, 0, 0)),
        ),
        out_shape=jax.ShapeDtypeStruct((len(order), 3, vocab, sub), kind),
        compiler_params=PARAMS,
        name="table_projection",
    )(jnp.stack([ctx ^ r for r in order]), table, weights)


def input_projection(rows_in, pieces, ctx):
    rows, full_width = rows_in.shape
    feats, chans = pieces[0].shape[1:]
    count = len(pieces)
    sub = chans // count

    def kernel(ctx_ref, rows_ref, *refs):
        weights, (normed_ref, proj_ref, scale_ref) = refs[:count], refs[count:]

        @pl.when(pl.program_id(0) == 0)
        def _():
            total = jnp.zeros((rows, 1), F32)
            for q in range(count):
                part = rows_ref[:, q * feats : (q + 1) * feats].astype(F32)
                total = total + jnp.sum(part * part, axis=1, keepdims=True)
            scale_ref[...] = lax.rsqrt(total / full_width + EPSILON)
            for q in range(count):
                part = rows_ref[:, q * feats : (q + 1) * feats].astype(F32)
                normed_ref[q] = (part * scale_ref[...]).astype(BF16)

        total = jnp.zeros((rows, chans), F32)
        for r in range(count):
            start = pl.multiple_of((ctx_ref[0] ^ r) * feats, feats)
            total = total + dot(rows_ref[:, pl.ds(start, feats)], weights[r][0])
        total = (total * scale_ref[...]).astype(BF16)
        for q in range(count):
            proj_ref[q, 0] = total[:, q * sub : (q + 1) * sub]

    return pl.pallas_call(
        kernel,
        grid_spec=pltpu.PrefetchScalarGridSpec(
            num_scalar_prefetch=1,
            grid=(3,),
            in_specs=[pl.BlockSpec((rows, full_width), lambda m, ctx: (0, 0))]
            + [pl.BlockSpec((1, feats, chans), lambda m, ctx: (m, 0, 0))] * count,
            out_specs=[
                pl.BlockSpec((count, rows, feats), lambda m, ctx: (0, 0, 0)),
                pl.BlockSpec((count, 1, rows, sub), lambda m, ctx: (0, m, 0, 0)),
                pl.BlockSpec((rows, 1), lambda m, ctx: (0, 0)),
            ],
        ),
        out_shape=(
            jax.ShapeDtypeStruct((count, rows, feats), BF16),
            jax.ShapeDtypeStruct((count, 3, rows, sub), BF16),
            jax.ShapeDtypeStruct((rows, 1), F32),
        ),
        compiler_params=PARAMS,
        name="input_projection",
    )(ctx[None], rows_in, *pieces)


def input_gradient(gproj, pieces, rows_in, scale, ctx, dp):
    rows, full_width = rows_in.shape
    feats, chans = pieces[0].shape[1:]
    count = len(pieces)
    sub = chans // count
    tile = min(256, feats)
    steps, half = feats // tile, rows // 2

    def kernel(ctx_ref, gproj_ref, rows_ref, scale_ref, *refs):
        weights, outs, (flat, grads) = refs[:count], refs[count:-2], refs[-2:]
        step = pl.program_id(0)

        @pl.when(step == 0)
        def _():
            for m in range(3):
                for q in range(count):
                    flat[m, :, q * sub : (q + 1) * sub] = gproj_ref[q, m]

        columns = pl.ds(pl.multiple_of(step * tile, tile), tile)
        for r in range(count):
            total = dot_t(flat[0], weights[r][0])
            for m in (1, 2):
                total = total + dot_t(flat[m], weights[r][m])
            grads[ctx_ref[0] ^ r, :, columns] = total * scale_ref[...]

        @pl.when(step == steps - 1)
        def _():
            stat = jnp.zeros((rows, 1), F32)
            for q in range(count):
                part = rows_ref[:, q * feats : (q + 1) * feats].astype(F32)
                stat = stat + jnp.sum(part * grads[q], axis=1, keepdims=True)
            stat = stat * scale_ref[...] * scale_ref[...] / full_width
            for shift in range(count):
                q = ctx_ref[1 + shift]
                start = pl.multiple_of(q * feats, feats)
                part = rows_ref[:, pl.ds(start, feats)].astype(F32)
                total = (grads[q] - part * stat).astype(BF16)
                if shift == 0:
                    outs[0][...] = total
                else:
                    outs[shift][...] = total[:half]
                    outs[count - 1 + shift][...] = total[half:]

    outs = pl.pallas_call(
        kernel,
        grid_spec=pltpu.PrefetchScalarGridSpec(
            num_scalar_prefetch=1,
            grid=(steps,),
            in_specs=[
                pl.BlockSpec(gproj.shape, lambda t, ctx: (0, 0, 0, 0)),
                pl.BlockSpec((rows, full_width), lambda t, ctx: (0, 0)),
                pl.BlockSpec((rows, 1), lambda t, ctx: (0, 0)),
            ]
            + [pl.BlockSpec((3, tile, chans), lambda t, ctx: (0, t, 0))] * count,
            out_specs=[pl.BlockSpec((rows, feats), lambda t, ctx: (0, 0))]
            + [pl.BlockSpec((half, feats), lambda t, ctx: (0, 0))] * (2 * count - 2),
            scratch_shapes=[
                pltpu.VMEM((3, rows, chans), BF16),
                pltpu.VMEM((count, rows, feats), F32),
            ],
        ),
        out_shape=[jax.ShapeDtypeStruct((rows, feats), BF16)]
        + [jax.ShapeDtypeStruct((half, feats), BF16)] * (2 * count - 2),
        compiler_params=PARAMS,
        name="input_gradient",
    )(jnp.concatenate([ctx[None], targets(dp, count)]), gproj, rows_in, scale, *pieces)
    return outs[0], outs[1:count], outs[count:]


def grad_in_kernel(left, pieces, ctx):
    feats, depth = left.shape
    count, sub = len(pieces), pieces[0].shape[2]
    if sub % 128:
        columns = jnp.concatenate([pick(jnp.stack(pieces), ctx ^ q) for q in range(count)], axis=2)
        columns = columns[:3]
        return jnp.einsum("dk,mkc->mdc", left, columns, preferred_element_type=F32)

    tile = min(256, feats)

    def kernel(ctx_ref, left_ref, *refs):
        out_ref = refs[count]
        for r in range(count):
            columns = pl.ds(pl.multiple_of((ctx_ref[0] ^ r) * sub, sub), sub)
            for m in range(3):
                out_ref[m, :, columns] = dot(left_ref[...], refs[r][m])

    return pl.pallas_call(
        kernel,
        grid_spec=pltpu.PrefetchScalarGridSpec(
            num_scalar_prefetch=1,
            grid=(feats // tile,),
            in_specs=[pl.BlockSpec((tile, depth), lambda t, ctx: (t, 0))]
            + [pl.BlockSpec((3, depth, sub), lambda t, ctx: (0, 0, 0))] * count,
            out_specs=pl.BlockSpec((3, tile, sub * count), lambda t, ctx: (0, t, 0)),
        ),
        out_shape=jax.ShapeDtypeStruct((3, feats, sub * count), F32),
        compiler_params=PARAMS,
        name="grad_project_in",
    )(ctx[None], left, *pieces)


def grad_out_kernel(early, late, right, ctx, sec):
    depth, feats = right.shape
    count, sub = len(early), early[0].shape[1]

    def kernel(where_ref, right_ref, *refs):
        out_ref = refs[2 * count]
        for r in range(count):
            for index, piece in ((0, refs[r].at[...]), (1, refs[count + r].at[0])):

                @pl.when((pl.program_id(0) == r) & (where_ref[count] == index))
                def _():
                    out_ref[...] = lax.dot_general(
                        piece[...],
                        right_ref[...],
                        (((0,), (0,)), ((), ())),
                        preferred_element_type=F32,
                    )

    return pl.pallas_call(
        kernel,
        grid_spec=pltpu.PrefetchScalarGridSpec(
            num_scalar_prefetch=1,
            grid=(count,),
            in_specs=[pl.BlockSpec((depth, feats), lambda r, where: (0, 0))]
            + [pl.BlockSpec((depth, sub), lambda r, where: (0, 0))] * count
            + [pl.BlockSpec((1, depth, sub), lambda r, where: (3, 0, 0))] * count,
            out_specs=pl.BlockSpec((sub, feats), lambda r, where: (where[r], 0)),
        ),
        out_shape=jax.ShapeDtypeStruct((sub * count, feats), F32),
        compiler_params=PARAMS,
        name="grad_project_out",
    )(jnp.stack([ctx ^ r for r in range(count)] + [sec]), right, *early, *late)


def together(*values):
    return lax.optimization_barrier(values)


def targets(dp, count):
    return (dp + jnp.arange(count, dtype=jnp.int32)) % count


def output_projection(gated, weights, dp):
    count, rows, sub = gated.shape
    chans, full_width = weights.shape
    parts = lax.axis_size("dp")
    width, half = full_width // parts, rows // 2

    def kernel(where_ref, gated_ref, weights_ref, *refs):
        outs, flat = refs[:-1], refs[-1]

        @pl.when(pl.program_id(0) == 0)
        def _():
            for q in range(count):
                flat[:, q * sub : (q + 1) * sub] = gated_ref[q]

        total = dot(flat[...], weights_ref[...]).astype(BF16)
        @pl.when(pl.program_id(0) == 0)
        def _():
            outs[0][...] = total

        for shift in range(1, parts):

            @pl.when(pl.program_id(0) == shift)
            def _():
                outs[shift][...] = total[:half]
                outs[parts - 1 + shift][...] = total[half:]

    outs = pl.pallas_call(
        kernel,
        grid_spec=pltpu.PrefetchScalarGridSpec(
            num_scalar_prefetch=1,
            grid=(parts,),
            in_specs=[
                pl.BlockSpec(gated.shape, lambda q, where: (0, 0, 0)),
                pl.BlockSpec((chans, width), lambda q, where: (0, where[q])),
            ],
            out_specs=[pl.BlockSpec((rows, width), lambda q, where: (0, 0))]
            + [pl.BlockSpec((half, width), lambda q, where: (0, 0))] * (2 * parts - 2),
            scratch_shapes=[pltpu.VMEM((rows, chans), BF16)],
        ),
        out_shape=[jax.ShapeDtypeStruct((rows, width), BF16)]
        + [jax.ShapeDtypeStruct((half, width), BF16)] * (2 * parts - 2),
        compiler_params=PARAMS,
        name="output_projection",
    )(targets(dp, parts), gated, weights)
    return outs[0], outs[1:parts], outs[parts:]


def ctx_swap_in(value, section):
    me = lax.axis_index("ctx")
    count = value.shape[0]
    came = [pick(value, me)]
    for r in range(1, count):
        came.append(ctx_xor(pick(value, me ^ r), r, (section,)))
    came = jnp.stack(came)
    return [pick(came, me ^ q) for q in range(count)]


def ctx_swap(value):
    return lax.all_to_all(value, "ctx", split_axis=0, concat_axis=0, tiled=True)


def local(
    token_ids, embedding, project_in, short_taps, filter_taps, decay_rates, project_out, cotangent
):
    n_ctx, n_dp = lax.axis_size("ctx"), lax.axis_size("dp")
    sec, dp, ctx = (lax.axis_index(axis) for axis in ("section", "dp", "ctx"))
    first = sec == 0
    rows, vocab = token_ids.shape[0], embedding.shape[0]
    seq = rows * n_ctx
    weights_in = jnp.transpose(project_in[0], (1, 0, 2))
    weights_out = project_out[0]
    feats, chans = weights_out.shape[1], weights_out.shape[0]
    full_width = feats * n_ctx
    sub = chans // n_ctx

    if n_ctx == n_dp:
        half = vocab // 2
        mine = lax.dynamic_slice_in_dim(embedding, sec * half, half, 0)
        came = []
        for i in range(1, n_dp):
            shifts = (i, i % (n_dp - 1) + 1)
            came.append(
                send(
                    mine,
                    ("section", "dp", "ctx"),
                    lambda s, z, k: (0, (z + shifts[s]) % n_dp, k) if z == k else None,
                )
            )
        offset = (dp - ctx) % n_dp
        low, high = embedding[:half], embedding[half:]
        for i in range(1, n_dp):
            low = jnp.where(offset == i, came[i - 1], low)
            high = jnp.where(offset == i % (n_dp - 1) + 1, came[i - 1], high)
        table = jnp.concatenate([low, high], axis=0)
    else:
        table = lax.dynamic_slice_in_dim(
            lax.all_gather(embedding, "dp", axis=1, tiled=True), ctx * feats, feats, 1
        )
    out_full = lax.all_gather(weights_out, "ctx", axis=1, tiled=True)
    in_far = far_gather(weights_in, (1,))
    far = sorted(in_far)[1:]
    sibling = ctx_xor(weights_in, 1, (0, 1))
    table, sibling = together(table, sibling)

    table_float = table.astype(F32)
    squares = jnp.sum(table_float * table_float, axis=1)
    tokens = token_ids.astype(F32)[None]
    held = [0]
    bit = n_ctx // 2
    while bit:
        came = ctx_xor(jnp.concatenate([squares, tokens.reshape(-1)]), bit, (0,))
        squares = squares + came[:vocab]
        tokens = jnp.concatenate([tokens, came[vocab:].reshape(-1, rows)], axis=0)
        held += [r | bit for r in held]
        bit //= 2
    table_inv = lax.rsqrt(squares[:, None] / full_width + EPSILON)
    tokens = jnp.stack([tokens[held.index(r)] for r in range(n_ctx)])
    tokens = jnp.concatenate([pick(tokens, ctx ^ q) for q in range(n_ctx)]).astype(jnp.int32)

    def own(value):
        return lax.dynamic_slice_in_dim(value, ctx * sub, sub, value.ndim - 1)

    taps = own(short_taps[0]).reshape(9, sub)
    filters = own(filter_taps[0])
    tap_count = filters.shape[0]
    positions = jnp.arange(tap_count).astype(F32)[:, None]
    damping = jnp.exp(-own(decay_rates) * positions / tap_count)
    kern = filters * damping
    matrices = spectra(tap_count)

    vocabulary = jnp.arange(vocab, dtype=jnp.int32)[None, :]
    first_input = dot((token_ids[:, None] == vocabulary).astype(BF16), embedding)

    order = scatter_order(n_ctx)
    kept = order[: n_ctx // 2]
    sent = table_projection(table, weights_in, ctx, [r | 1 for r in kept], BF16)
    arrived = ctx_xor(sent, 1, (0,))
    partial = table_projection(table, weights_in, ctx, kept, F32) + arrived.astype(F32)
    bit = 2
    while bit < n_ctx:
        stays, gone = jnp.split(partial, 2, axis=0)
        partial = stays + ctx_xor(gone.astype(BF16), bit, (0,)).astype(F32)
        bit *= 2
    table_proj = (partial[0] * table_inv).astype(BF16)
    gated_0, *saved_0, proj_0 = conv_forward(table_proj, taps, kern, matrices, tokens)
    cot_stack = jnp.stack(dp_gather(cotangent, 1))
    gated_0, cot_stack = together(gated_0, cot_stack)
    gated_rows = jnp.stack(ctx_swap_in(gated_0.reshape(n_ctx, rows, sub), 0))
    shares = output_projection(gated_rows, out_full, dp)
    middle_stack, (gated_0,), late = cross_gather(
        shares, first_input, 0, [gated_0], [in_far[r] for r in far]
    )
    gated_all_0 = ctx_gather(gated_0, (0,))

    in_far.update(zip(far, late))
    in_pieces = []
    for r in sorted(in_far):
        in_pieces += [in_far[r], ctx_xor(in_far[r], 1, (1,)) if r else sibling]
    def gated_gradient(parts):
        total = dot_t(jnp.concatenate(parts, axis=1), out_full).astype(BF16)
        split = jnp.transpose(total.reshape(rows, n_ctx, sub), (1, 0, 2))
        return ctx_swap(split).reshape(seq, sub)

    cot_parts = in_order(cot_stack, dp)
    middle_all = jnp.concatenate(in_order(middle_stack, dp), axis=1)
    normed, proj_rows, scale = input_projection(middle_all, in_pieces, ctx)
    proj_1 = ctx_swap(proj_rows)
    gated_1, *saved_1 = conv_forward(proj_1, taps, kern, matrices)

    gproj_1, gkern_1, gtaps_1 = conv_backward(
        gated_gradient(cot_parts), proj_1, taps, kern, matrices, saved_1
    )
    gproj_1, *gated_all_0 = together(gproj_1, *gated_all_0)
    gproj_rows = ctx_swap(gproj_1)
    shares = input_gradient(gproj_rows, in_pieces, middle_all, scale, ctx, dp)
    def begin_gather(normed, gproj, gated):
        planes = gproj.transpose(1, 0, 2, 3).reshape(3, seq, sub)
        planes = far_gather(jnp.concatenate([planes, gated[None]]), (1,))
        return [normed] + [planes[r] for r in sorted(planes)]

    back_stack, _, (normed, *planes) = cross_gather(
        shares, cotangent, 1, [normed, gproj_1, gated_1], (), begin_gather
    )

    normed_cols = jnp.concatenate([part.T for part in ctx_swap_in(normed, 1)], axis=1)
    gproj_all = []
    for plane in planes:
        gproj_all += [plane, ctx_xor(plane, 1, (1,))]

    back_stack, normed_cols, *gproj_all = together(back_stack, normed_cols, *gproj_all)
    back_parts = in_order(back_stack, dp)
    table_grad, gkern_0, gtaps_0 = conv_backward(
        gated_gradient(back_parts), proj_0, taps, kern, matrices, saved_0, tokens, table_inv
    )

    grads = jnp.stack([jnp.where(first, a, b) for a, b in zip(back_parts, cot_parts)])
    grad_cols = ctx_swap(grads).reshape(seq, feats)
    grad_out = grad_out_kernel(gated_all_0, gproj_all, grad_cols, ctx, sec)
    table_pieces = ctx_gather(table_grad, (0,))
    grad_in = lax.cond(
        first,
        lambda: grad_in_kernel(table.T, table_pieces, ctx),
        lambda: grad_in_kernel(normed_cols, gproj_all, ctx),
    )

    gkern = jnp.where(first, gkern_0, gkern_1)
    gtaps = jnp.where(first, gtaps_0, gtaps_1)
    gdecay = -jnp.sum(gkern * kern * positions, axis=0, keepdims=True) / tap_count
    small = jnp.concatenate([gkern * damping, gdecay, gtaps], axis=0)
    small = jnp.stack(ctx_gather(small, (0, 1)))
    small = jnp.concatenate([pick(small, ctx ^ q) for q in range(n_ctx)], axis=1)
    return (
        jnp.transpose(grad_in, (1, 0, 2))[None],
        grad_out[None],
        small[:tap_count][None],
        small[tap_count][None],
        small[tap_count + 1 :].reshape(1, 3, 3, chans),
    )


def solution(mesh):
    return jax.shard_map(
        local,
        mesh=mesh,
        in_specs=(
            P("ctx"),
            P(None, "dp"),
            P("section", "ctx", None, "dp"),
            P("section", None, None, "dp"),
            P("section", None, "dp"),
            P("section", "dp"),
            P("section", "dp", "ctx"),
            P("ctx", "dp"),
        ),
        out_specs=(
            P("section", "ctx", None, "dp"),
            P("section", "dp", "ctx"),
            P("section", None, "dp"),
            P("section", "dp"),
            P("section", None, None, "dp"),
        ),
        check_vma=False,
    )
```

```python
import functools

import jax
import jax.numpy as jnp
import numpy as np
from jax import lax
from jax.experimental import pallas as pl
from jax.experimental.pallas import tpu as pltpu
from jax.sharding import PartitionSpec as P

EPSILON = 1e-06
F32 = jnp.float32
BF16 = jnp.bfloat16


def dot(left, right):
    return jnp.dot(left, right, preferred_element_type=F32)


def dot_t(left, right):
    return lax.dot_general(left, right, (((1,), (1,)), ((), ())), preferred_element_type=F32)


def exact(left, right):
    return jnp.dot(left, right, preferred_element_type=F32, precision=lax.Precision.HIGHEST)


def pick(stack, index):
    return lax.dynamic_index_in_dim(stack, index, 0, keepdims=False)


def send(value, axes, route):
    sizes = [lax.axis_size(axis) for axis in axes]
    pairs = []
    for source, place in enumerate(np.ndindex(*sizes)):
        target = route(*place)
        if target is not None:
            pairs.append((source, int(np.ravel_multi_index(target, sizes))))
    return lax.ppermute(value, axes, pairs)


def ctx_xor(value, mask, sections):
    return send(
        value, ("section", "ctx"), lambda s, k: (s, k ^ mask) if s in sections else None
    )


def ctx_gather(value, sections):
    count = lax.axis_size("ctx")
    held = {0: value}
    bit = count // 2
    while bit:
        for r in list(held):
            held[r | bit] = ctx_xor(held[r], bit, sections)
        bit //= 2
    return [held[r] for r in range(count)]


def far_gather(value, sections):
    held = {0: value}
    bit = lax.axis_size("ctx") // 2
    while bit > 1:
        for r in list(held):
            held[r | bit] = ctx_xor(held[r], bit, sections)
        bit //= 2
    return held


def scatter_order(count):
    if count == 1:
        return [0]
    inner = scatter_order(count // 2)
    return [2 * r for r in inner] + [2 * r + 1 for r in inner]


def dp_gather(value, section):
    count = lax.axis_size("dp")
    pieces = [value]
    for _ in range(count - 1):
        pieces.append(
            send(
                pieces[-1],
                ("section", "dp"),
                lambda s, z: (s, (z + 1) % count) if s == section else None,
            )
        )
    return pieces


def cross_gather(shares, base, source, early, late=(), begin=None):
    count = lax.axis_size("dp")
    half = base.shape[0] // 2
    def move(value, shift):
        return send(
            value,
            ("section", "dp"),
            lambda s, z: (1 - s, (z + shift) % count) if s == source else None,
        )

    straight, *shares = shares
    straight = move(straight, 0)
    arrivals = [[move(shares[0][shift - 1], shift) for shift in range(1, count)]]
    tied = together(*arrivals[0], *shares[1])
    arrivals[0], shares_left = list(tied[: count - 1]), tied[count - 1 :]
    arrivals.append([move(shares_left[shift - 1], shift) for shift in range(1, count)])
    for index, start in enumerate((0, half)):
        arrivals[index].append(straight[start : start + half])

    def total(index, values):
        start = index * half
        result = base[start : start + half].astype(F32)
        for value in values:
            result = result + value.astype(F32)
        return result.astype(BF16)

    part = total(0, arrivals[0])
    if early:
        part, *early = together(part, *early)
    begun = begin(*early) if begin else []
    first = dp_gather(part, 1 - source)
    marker = min(2, count - 1)
    first[marker], *arrivals[1] = together(first[marker], *arrivals[1])
    second = dp_gather(total(1, arrivals[1]), 1 - source)
    if late:
        first[-1], second[-1], *late = together(first[-1], second[-1], *late)
    if begun and count > 1:
        second[1], *begun = together(second[1], *begun)
    stack = jnp.stack([jnp.concatenate(pair, axis=0) for pair in zip(first, second)])
    return stack, early, begun or late


def in_order(stack, me):
    return [pick(stack, (me - q) % stack.shape[0]) for q in range(stack.shape[0])]


def spectra(taps):
    freq = np.arange(taps)[:, None]
    time = np.arange(taps)[None, :]
    angle = np.pi * freq * time / taps
    nyquist = np.where(time % 2 == 0, 1.0, -1.0)
    forward = np.concatenate(
        [np.cos(angle), np.where(freq == 0, nyquist, -np.sin(angle))], axis=0
    )
    weight = np.where(freq == 0, 1.0, 2.0) / (2 * taps)
    inverse = np.concatenate(
        [weight * np.cos(angle), np.where(freq == 0, nyquist, -2 * np.sin(angle)) * np.where(freq == 0, weight, 1.0 / (2 * taps))],
        axis=0,
    ).T
    sign = np.where(np.arange(2 * taps) % taps % 2 == 0, 1.0, -1.0)
    return [jnp.asarray(m, BF16) for m in (forward, inverse, inverse * sign[None, :])]


def later(current, before, steps, row):
    return jnp.where(row < steps, pltpu.roll(before, steps, 0), pltpu.roll(current, steps, 0))


def sooner(current, after, steps, row):
    count = current.shape[0]
    return jnp.where(
        row >= count - steps,
        pltpu.roll(after, count - steps, 0),
        pltpu.roll(current, count - steps, 0),
    )


def kernel_spectrum(fwd_ref, kern_ref, row):
    tap_count = kern_ref.shape[0]
    kern = dot(fwd_ref[...], kern_ref[...].astype(BF16))
    real, imag = kern[:tap_count], kern[tap_count:]
    return real, jnp.where(row == 0, 0.0, imag), jnp.where(row == 0, imag, real)


def proj_block(projs, m, b, tap_count):
    chunk, start = divmod(b * tap_count, projs[m].shape[1])
    return projs[m][chunk, start : start + tap_count, :].astype(F32)


def short_filter(taps_ref, m, current, before, row):
    return (
        taps_ref[m : m + 1, :] * current
        + taps_ref[3 + m : 4 + m, :] * later(current, before, 1, row)
        + taps_ref[6 + m : 7 + m, :] * later(current, before, 2, row)
    )


def lookup_kernel(
    tokens_ref, table_ref, taps_ref, kern_ref, fwd_ref, inv_ref,
    gated_ref, filt_ref, spec_ref, proj_ref,
):
    tap_count, vocab = kern_ref.shape[0], table_ref.shape[1]
    entry = lax.broadcasted_iota(jnp.int32, (tap_count, vocab), 1)
    for b in range(filt_ref.shape[0] // tap_count):
        here = pl.ds(b * tap_count, tap_count)
        chosen = (entry == tokens_ref[here, :]).astype(F32).astype(BF16)
        for m in range(3):
            proj_ref[0, m, here, :] = dot(chosen, table_ref[m]).astype(BF16)
    forward_kernel(
        proj_ref, taps_ref, kern_ref, fwd_ref, inv_ref, gated_ref, filt_ref, spec_ref
    )


def collect_kernel(
    tokens_ref, scale_ref, gg_ref, proj_ref, taps_ref, kern_ref, fwd_ref, inv_ref, filt_ref, spec_ref,
    table_ref, gkern_ref, gtaps_ref, grad_spec, gproj_ref,
):
    backward_kernel(
        gg_ref, proj_ref, taps_ref, kern_ref, fwd_ref, inv_ref, filt_ref, spec_ref,
        gproj_ref, gkern_ref, gtaps_ref, grad_spec,
    )
    _, vocab, _ = table_ref.shape
    seq = filt_ref.shape[0]
    entry = lax.broadcasted_iota(jnp.int32, (vocab, seq), 0)
    chosen = (entry == tokens_ref[...]).astype(F32).astype(BF16)
    for m in range(3):
        table_ref[m] = (dot(chosen, gproj_ref[0, m]) * scale_ref[...]).astype(BF16)


def forward_kernel(proj_ref, taps_ref, kern_ref, fwd_ref, inv_ref, gated_ref, filt_ref, spec_ref):
    projs = [proj_ref.at[:, m] for m in range(3)]
    tap_count, chans = kern_ref.shape
    blocks = filt_ref.shape[0] // tap_count
    row = lax.broadcasted_iota(jnp.int32, (tap_count, chans), 0)
    sign = jnp.where(row % 2 == 0, 1.0, -1.0)
    kr, ki, kn = kernel_spectrum(fwd_ref, kern_ref, row)
    zero = jnp.zeros((tap_count, chans), F32)
    before = [zero] * 3
    last_r, last_i = zero, zero
    for b in range(blocks):
        here = pl.ds(b * tap_count, tap_count)
        streams = []
        for m in range(3):
            current = proj_block(projs, m, b, tap_count)
            streams.append(short_filter(taps_ref, m, current, before[m], row))
            before[m] = current
        part = dot(fwd_ref[...], (streams[1] * streams[2]).astype(BF16))
        pr, pi = part[:tap_count], part[tap_count:]
        wr = last_r + sign * pr
        wi = last_i + sign * pi
        last_r, last_i = pr, pi
        spec_ref[b, :tap_count, :] = wr.astype(BF16)
        spec_ref[b, tap_count:, :] = wi.astype(BF16)
        mixed = jnp.concatenate([wr * kr - wi * ki, wr * ki + wi * kn], axis=0)
        filtered = dot(inv_ref[...], mixed.astype(BF16))
        filt_ref[here, :] = filtered.astype(BF16)
        gated_ref[here, :] = (streams[0] * filtered).astype(BF16)


def backward_kernel(
    gg_ref, proj_ref, taps_ref, kern_ref, fwd_ref, inv_ref, filt_ref, spec_ref,
    gproj_ref, gkern_ref, gtaps_ref, grad_spec,
):
    projs = [proj_ref.at[:, m] for m in range(3)]
    tap_count, chans = kern_ref.shape
    blocks = filt_ref.shape[0] // tap_count
    row = lax.broadcasted_iota(jnp.int32, (tap_count, chans), 0)
    sign = jnp.where(row % 2 == 0, 1.0, -1.0)
    kr, ki, kn = kernel_spectrum(fwd_ref, kern_ref, row)
    zero = jnp.zeros((tap_count, chans), F32)
    sum_r, sum_i = zero, zero
    last = zero
    for b in range(blocks):
        here = pl.ds(b * tap_count, tap_count)
        current = proj_block(projs, 0, b, tap_count)
        query = short_filter(taps_ref, 0, current, last, row)
        last = current
        part = dot(fwd_ref[...], (gg_ref[here, :].astype(F32) * query).astype(BF16))
        grad_spec[b] = part
        gr, gi = sign * part[:tap_count], sign * part[tap_count:]
        wr = spec_ref[b, :tap_count, :].astype(F32)
        wi = spec_ref[b, tap_count:, :].astype(F32)
        rr, ii = wr * gr, wi * gi
        sum_r = sum_r + jnp.where(row == 0, rr, rr + ii)
        sum_i = sum_i + jnp.where(row == 0, ii, wr * gi - wi * gr)
    gkern_ref[...] = exact(
        inv_ref[...].astype(F32), jnp.concatenate([sum_r, sum_i], axis=0)
    )
    after = [zero] * 3
    next_r, next_i = zero, zero
    sums = [jnp.zeros((1, chans), F32) for _ in range(9)]
    for b in reversed(range(blocks)):
        chunk, start = divmod(b * tap_count, projs[0].shape[1])
        here = pl.ds(b * tap_count, tap_count)
        gr, gi = grad_spec[b, :tap_count, :], grad_spec[b, tap_count:, :]
        vr, vi = gr + sign * next_r, gi + sign * next_i
        next_r, next_i = gr, gi
        mixed = jnp.concatenate([vr * kr + vi * ki, vi * kn - vr * ki], axis=0)
        grad_prod = dot(inv_ref[...], mixed.astype(BF16))
        shifts, shorts = [], []
        for m in range(3):
            current = proj_block(projs, m, b, tap_count)
            before = proj_block(projs, m, b - 1, tap_count) if b else zero
            shifts.append([current, later(current, before, 1, row), later(current, before, 2, row)])
            if m:
                shorts.append(sum(taps_ref[3 * j + m : 3 * j + m + 1, :] * shifts[m][j] for j in range(3)))
        grads = [
            gg_ref[here, :].astype(F32) * filt_ref[here, :].astype(F32),
            grad_prod * shorts[1],
            grad_prod * shorts[0],
        ]
        for m in range(3):
            grad = grads[m]
            out = (
                taps_ref[m : m + 1, :] * grad
                + taps_ref[3 + m : 4 + m, :] * sooner(grad, after[m], 1, row)
                + taps_ref[6 + m : 7 + m, :] * sooner(grad, after[m], 2, row)
            )
            after[m] = grad
            gproj_ref[chunk, m, start : start + tap_count, :] = out.astype(BF16)
            for j in range(3):
                sums[3 * j + m] = sums[3 * j + m] + jnp.sum(
                    grad * shifts[m][j], axis=0, keepdims=True
                )
    for index in range(9):
        gtaps_ref[index : index + 1, :] = sums[index]


PARAMS = pltpu.CompilerParams(vmem_limit_bytes=56 * 1024 * 1024)


def conv_forward(proj, taps, kern, matrices, tokens=None):
    tap_count, chans = kern.shape
    seq = proj.shape[0] * proj.shape[2] if tokens is None else tokens.shape[0]
    results = [
        jax.ShapeDtypeStruct((seq, chans), BF16),
        jax.ShapeDtypeStruct((seq, chans), BF16),
        jax.ShapeDtypeStruct((seq // tap_count, 2 * tap_count, chans), BF16),
    ]
    operands = (proj, taps, kern, matrices[0], matrices[2])
    if tokens is not None:
        results.append(jax.ShapeDtypeStruct((1, 3, seq, chans), BF16))
        operands = (tokens[:, None], *operands)
    return pl.pallas_call(
        forward_kernel if tokens is None else lookup_kernel,
        out_shape=results,
        compiler_params=PARAMS,
        name="conv_forward",
    )(*operands)


def conv_backward(gg, proj, taps, kern, matrices, saved, tokens=None, scale=None):
    tap_count, chans = kern.shape
    seq = gg.shape[0]
    scratch = [pltpu.VMEM((seq // tap_count, 2 * tap_count, chans), F32)]
    operands = (gg, proj, taps, kern, matrices[0], matrices[1], *saved)
    first = jax.ShapeDtypeStruct(proj.shape, BF16)
    if tokens is not None:
        first = jax.ShapeDtypeStruct((3, scale.shape[0], chans), BF16)
        scratch.append(pltpu.VMEM(proj.shape, BF16))
        operands = (tokens[None, :], scale, *operands)
    return pl.pallas_call(
        backward_kernel if tokens is None else collect_kernel,
        out_shape=(
            first,
            jax.ShapeDtypeStruct(kern.shape, F32),
            jax.ShapeDtypeStruct((9, chans), F32),
        ),
        scratch_shapes=scratch,
        compiler_params=PARAMS,
        name="conv_backward",
    )(*operands)


def table_projection(table, weights, ctx, order, kind):
    vocab, feats = table.shape
    sub = weights.shape[2] // lax.axis_size("ctx")
    if sub % 128:
        columns = jnp.stack(
            [lax.dynamic_slice_in_dim(weights, (ctx ^ r) * sub, sub, 2) for r in order]
        )
        return jnp.einsum("vd,rmdc->rmvc", table, columns, preferred_element_type=F32).astype(kind)

    def kernel(where_ref, table_ref, weights_ref, out_ref):
        for m in range(3):
            out_ref[0, m] = dot(table_ref[...], weights_ref[m]).astype(kind)

    return pl.pallas_call(
        kernel,
        grid_spec=pltpu.PrefetchScalarGridSpec(
            num_scalar_prefetch=1,
            grid=(len(order),),
            in_specs=[
                pl.BlockSpec((vocab, feats), lambda r, where: (0, 0)),
                pl.BlockSpec((3, feats, sub), lambda r, where: (0, 0, where[r])),
            ],
            out_specs=pl.BlockSpec((1, 3, vocab, sub), lambda r, where: (r, 0, 0, 0)),
        ),
        out_shape=jax.ShapeDtypeStruct((len(order), 3, vocab, sub), kind),
        compiler_params=PARAMS,
        name="table_projection",
    )(jnp.stack([ctx ^ r for r in order]), table, weights)


def input_projection(rows_in, pieces, ctx):
    rows, full_width = rows_in.shape
    feats, chans = pieces[0].shape[1:]
    count = full_width // feats
    places = sorted(pieces)

    def kernel(ctx_ref, rows_ref, *refs):
        weights, (normed_ref, part_ref, scale_ref) = refs[: len(places)], refs[len(places) :]

        @pl.when(pl.program_id(0) == 0)
        def _():
            total = jnp.zeros((rows, 1), F32)
            for q in range(count):
                part = rows_ref[:, q * feats : (q + 1) * feats].astype(F32)
                total = total + jnp.sum(part * part, axis=1, keepdims=True)
            scale_ref[...] = lax.rsqrt(total / full_width + EPSILON)
            for q in range(count):
                part = rows_ref[:, q * feats : (q + 1) * feats].astype(F32)
                normed_ref[q] = (part * scale_ref[...]).astype(BF16)

        total = jnp.zeros((rows, chans), F32)
        for r, weight in zip(places, weights):
            start = pl.multiple_of((ctx_ref[0] ^ r) * feats, feats)
            total = total + dot(rows_ref[:, pl.ds(start, feats)], weight[0])
        part_ref[0] = total

    return pl.pallas_call(
        kernel,
        grid_spec=pltpu.PrefetchScalarGridSpec(
            num_scalar_prefetch=1,
            grid=(3,),
            in_specs=[pl.BlockSpec((rows, full_width), lambda m, ctx: (0, 0))]
            + [pl.BlockSpec((1, feats, chans), lambda m, ctx: (m, 0, 0))] * len(places),
            out_specs=[
                pl.BlockSpec((count, rows, feats), lambda m, ctx: (0, 0, 0)),
                pl.BlockSpec((1, rows, chans), lambda m, ctx: (m, 0, 0)),
                pl.BlockSpec((rows, 1), lambda m, ctx: (0, 0)),
            ],
        ),
        out_shape=(
            jax.ShapeDtypeStruct((count, rows, feats), BF16),
            jax.ShapeDtypeStruct((3, rows, chans), F32),
            jax.ShapeDtypeStruct((rows, 1), F32),
        ),
        compiler_params=PARAMS,
        name="input_projection",
    )(ctx[None], rows_in, *[pieces[r] for r in places])


def input_projection_rest(rows_in, pieces, part, scale, ctx):
    rows, full_width = rows_in.shape
    chans = part.shape[2]
    feats = next(iter(pieces.values())).shape[1]
    count = full_width // feats
    sub = chans // count
    places = sorted(pieces)

    def kernel(ctx_ref, rows_ref, part_ref, scale_ref, *refs):
        weights, proj_ref = refs[:-1], refs[-1]
        total = part_ref[0]
        for r, weight in zip(places, weights):
            start = pl.multiple_of((ctx_ref[0] ^ r) * feats, feats)
            total = total + dot(rows_ref[:, pl.ds(start, feats)], weight[0])
        total = (total * scale_ref[...]).astype(BF16)
        for q in range(count):
            proj_ref[q, 0] = total[:, q * sub : (q + 1) * sub]

    return pl.pallas_call(
        kernel,
        grid_spec=pltpu.PrefetchScalarGridSpec(
            num_scalar_prefetch=1,
            grid=(3,),
            in_specs=[
                pl.BlockSpec((rows, full_width), lambda m, ctx: (0, 0)),
                pl.BlockSpec((1, rows, chans), lambda m, ctx: (m, 0, 0)),
                pl.BlockSpec((rows, 1), lambda m, ctx: (0, 0)),
            ]
            + [pl.BlockSpec((1, feats, chans), lambda m, ctx: (m, 0, 0))] * len(places),
            out_specs=pl.BlockSpec((count, 1, rows, sub), lambda m, ctx: (0, m, 0, 0)),
        ),
        out_shape=jax.ShapeDtypeStruct((count, 3, rows, sub), BF16),
        compiler_params=PARAMS,
        name="input_projection_rest",
    )(ctx[None], rows_in, part, scale, *[pieces[r] for r in places])


def input_gradient(gproj, pieces, rows_in, scale, ctx, dp):
    rows, full_width = rows_in.shape
    feats, chans = pieces[0].shape[1:]
    count = len(pieces)
    sub = chans // count
    tile = min(256, feats)
    steps, half = feats // tile, rows // 2

    def kernel(ctx_ref, gproj_ref, rows_ref, scale_ref, *refs):
        weights, outs, (flat, grads) = refs[:count], refs[count:-2], refs[-2:]
        step = pl.program_id(0)

        @pl.when(step == 0)
        def _():
            for m in range(3):
                for q in range(count):
                    flat[m, :, q * sub : (q + 1) * sub] = gproj_ref[q, m]

        columns = pl.ds(pl.multiple_of(step * tile, tile), tile)
        for r in range(count):
            total = dot_t(flat[0], weights[r][0])
            for m in (1, 2):
                total = total + dot_t(flat[m], weights[r][m])
            grads[ctx_ref[0] ^ r, :, columns] = total * scale_ref[...]

        @pl.when(step == steps - 1)
        def _():
            stat = jnp.zeros((rows, 1), F32)
            for q in range(count):
                part = rows_ref[:, q * feats : (q + 1) * feats].astype(F32)
                stat = stat + jnp.sum(part * grads[q], axis=1, keepdims=True)
            stat = stat * scale_ref[...] * scale_ref[...] / full_width
            for shift in range(count):
                q = ctx_ref[1 + shift]
                start = pl.multiple_of(q * feats, feats)
                part = rows_ref[:, pl.ds(start, feats)].astype(F32)
                total = (grads[q] - part * stat).astype(BF16)
                if shift == 0:
                    outs[0][...] = total
                else:
                    outs[shift][...] = total[:half]
                    outs[count - 1 + shift][...] = total[half:]

    outs = pl.pallas_call(
        kernel,
        grid_spec=pltpu.PrefetchScalarGridSpec(
            num_scalar_prefetch=1,
            grid=(steps,),
            in_specs=[
                pl.BlockSpec(gproj.shape, lambda t, ctx: (0, 0, 0, 0)),
                pl.BlockSpec((rows, full_width), lambda t, ctx: (0, 0)),
                pl.BlockSpec((rows, 1), lambda t, ctx: (0, 0)),
            ]
            + [pl.BlockSpec((3, tile, chans), lambda t, ctx: (0, t, 0))] * count,
            out_specs=[pl.BlockSpec((rows, feats), lambda t, ctx: (0, 0))]
            + [pl.BlockSpec((half, feats), lambda t, ctx: (0, 0))] * (2 * count - 2),
            scratch_shapes=[
                pltpu.VMEM((3, rows, chans), BF16),
                pltpu.VMEM((count, rows, feats), F32),
            ],
        ),
        out_shape=[jax.ShapeDtypeStruct((rows, feats), BF16)]
        + [jax.ShapeDtypeStruct((half, feats), BF16)] * (2 * count - 2),
        compiler_params=PARAMS,
        name="input_gradient",
    )(jnp.concatenate([ctx[None], targets(dp, count)]), gproj, rows_in, scale, *pieces)
    return outs[0], outs[1:count], outs[count:]


def grad_in_kernel(left, pieces, ctx):
    feats, depth = left.shape
    count, sub = len(pieces), pieces[0].shape[2]
    if sub % 128:
        columns = jnp.concatenate([pick(jnp.stack(pieces), ctx ^ q) for q in range(count)], axis=2)
        columns = columns[:3]
        return jnp.einsum("dk,mkc->mdc", left, columns, preferred_element_type=F32)

    tile = min(256, feats)

    def kernel(ctx_ref, left_ref, *refs):
        out_ref = refs[count]
        for r in range(count):
            columns = pl.ds(pl.multiple_of((ctx_ref[0] ^ r) * sub, sub), sub)
            for m in range(3):
                out_ref[m, :, columns] = dot(left_ref[...], refs[r][m])

    return pl.pallas_call(
        kernel,
        grid_spec=pltpu.PrefetchScalarGridSpec(
            num_scalar_prefetch=1,
            grid=(feats // tile,),
            in_specs=[pl.BlockSpec((tile, depth), lambda t, ctx: (t, 0))]
            + [pl.BlockSpec((3, depth, sub), lambda t, ctx: (0, 0, 0))] * count,
            out_specs=pl.BlockSpec((3, tile, sub * count), lambda t, ctx: (0, t, 0)),
        ),
        out_shape=jax.ShapeDtypeStruct((3, feats, sub * count), F32),
        compiler_params=PARAMS,
        name="grad_project_in",
    )(ctx[None], left, *pieces)


def grad_out_kernel(early, late, right, ctx, sec):
    depth, feats = right.shape
    count, sub = len(early), early[0].shape[1]

    def kernel(where_ref, right_ref, *refs):
        out_ref = refs[2 * count]
        for r in range(count):
            for index, piece in ((0, refs[r].at[...]), (1, refs[count + r].at[0])):

                @pl.when((pl.program_id(0) == r) & (where_ref[count] == index))
                def _():
                    out_ref[...] = lax.dot_general(
                        piece[...],
                        right_ref[...],
                        (((0,), (0,)), ((), ())),
                        preferred_element_type=F32,
                    )

    return pl.pallas_call(
        kernel,
        grid_spec=pltpu.PrefetchScalarGridSpec(
            num_scalar_prefetch=1,
            grid=(count,),
            in_specs=[pl.BlockSpec((depth, feats), lambda r, where: (0, 0))]
            + [pl.BlockSpec((depth, sub), lambda r, where: (0, 0))] * count
            + [pl.BlockSpec((1, depth, sub), lambda r, where: (3, 0, 0))] * count,
            out_specs=pl.BlockSpec((sub, feats), lambda r, where: (where[r], 0)),
        ),
        out_shape=jax.ShapeDtypeStruct((sub * count, feats), F32),
        compiler_params=PARAMS,
        name="grad_project_out",
    )(jnp.stack([ctx ^ r for r in range(count)] + [sec]), right, *early, *late)


def together(*values):
    return lax.optimization_barrier(values)


def targets(dp, count):
    return (dp + jnp.arange(count, dtype=jnp.int32)) % count


def output_projection(gated, weights, dp):
    count, rows, sub = gated.shape
    chans, full_width = weights.shape
    parts = lax.axis_size("dp")
    width, half = full_width // parts, rows // 2

    def kernel(where_ref, gated_ref, weights_ref, *refs):
        outs, flat = refs[:-1], refs[-1]

        @pl.when(pl.program_id(0) == 0)
        def _():
            for q in range(count):
                flat[:, q * sub : (q + 1) * sub] = gated_ref[q]

        total = dot(flat[...], weights_ref[...]).astype(BF16)
        @pl.when(pl.program_id(0) == 0)
        def _():
            outs[0][...] = total

        for shift in range(1, parts):

            @pl.when(pl.program_id(0) == shift)
            def _():
                outs[shift][...] = total[:half]
                outs[parts - 1 + shift][...] = total[half:]

    outs = pl.pallas_call(
        kernel,
        grid_spec=pltpu.PrefetchScalarGridSpec(
            num_scalar_prefetch=1,
            grid=(parts,),
            in_specs=[
                pl.BlockSpec(gated.shape, lambda q, where: (0, 0, 0)),
                pl.BlockSpec((chans, width), lambda q, where: (0, where[q])),
            ],
            out_specs=[pl.BlockSpec((rows, width), lambda q, where: (0, 0))]
            + [pl.BlockSpec((half, width), lambda q, where: (0, 0))] * (2 * parts - 2),
            scratch_shapes=[pltpu.VMEM((rows, chans), BF16)],
        ),
        out_shape=[jax.ShapeDtypeStruct((rows, width), BF16)]
        + [jax.ShapeDtypeStruct((half, width), BF16)] * (2 * parts - 2),
        compiler_params=PARAMS,
        name="output_projection",
    )(targets(dp, parts), gated, weights)
    return outs[0], outs[1:parts], outs[parts:]


def ctx_swap_in(value, section):
    me = lax.axis_index("ctx")
    count = value.shape[0]
    came = [pick(value, me)]
    for r in range(1, count):
        came.append(ctx_xor(pick(value, me ^ r), r, (section,)))
    came = jnp.stack(came)
    return [pick(came, me ^ q) for q in range(count)]


def ctx_swap(value):
    return lax.all_to_all(value, "ctx", split_axis=0, concat_axis=0, tiled=True)


def local(
    token_ids, embedding, project_in, short_taps, filter_taps, decay_rates, project_out, cotangent
):
    n_ctx, n_dp = lax.axis_size("ctx"), lax.axis_size("dp")
    sec, dp, ctx = (lax.axis_index(axis) for axis in ("section", "dp", "ctx"))
    first = sec == 0
    rows, vocab = token_ids.shape[0], embedding.shape[0]
    seq = rows * n_ctx
    weights_in = jnp.transpose(project_in[0], (1, 0, 2))
    weights_out = project_out[0]
    feats, chans = weights_out.shape[1], weights_out.shape[0]
    full_width = feats * n_ctx
    sub = chans // n_ctx

    if n_ctx == n_dp:
        half = vocab // 2
        mine = lax.dynamic_slice_in_dim(embedding, sec * half, half, 0)
        came = []
        for i in range(1, n_dp):
            shifts = (i, i % (n_dp - 1) + 1)
            came.append(
                send(
                    mine,
                    ("section", "dp", "ctx"),
                    lambda s, z, k: (0, (z + shifts[s]) % n_dp, k) if z == k else None,
                )
            )
        offset = (dp - ctx) % n_dp
        low, high = embedding[:half], embedding[half:]
        for i in range(1, n_dp):
            low = jnp.where(offset == i, came[i - 1], low)
            high = jnp.where(offset == i % (n_dp - 1) + 1, came[i - 1], high)
        table = jnp.concatenate([low, high], axis=0)
    else:
        table = lax.dynamic_slice_in_dim(
            lax.all_gather(embedding, "dp", axis=1, tiled=True), ctx * feats, feats, 1
        )
    out_full = lax.all_gather(weights_out, "ctx", axis=1, tiled=True)
    in_far = far_gather(weights_in, (1,))
    far = sorted(in_far)[1:]
    sibling = ctx_xor(weights_in, 1, (1,))

    table_float = table.astype(F32)
    squares = jnp.sum(table_float * table_float, axis=1)
    tokens = token_ids.astype(F32)[None]
    held = [0]
    bit = n_ctx // 2
    while bit:
        came = ctx_xor(jnp.concatenate([squares, tokens.reshape(-1)]), bit, (0,))
        squares = squares + came[:vocab]
        tokens = jnp.concatenate([tokens, came[vocab:].reshape(-1, rows)], axis=0)
        held += [r | bit for r in held]
        bit //= 2
    table_inv = lax.rsqrt(squares[:, None] / full_width + EPSILON)
    tokens = jnp.stack([tokens[held.index(r)] for r in range(n_ctx)])
    tokens = jnp.concatenate([pick(tokens, ctx ^ q) for q in range(n_ctx)]).astype(jnp.int32)

    def own(value):
        return lax.dynamic_slice_in_dim(value, ctx * sub, sub, value.ndim - 1)

    taps = own(short_taps[0]).reshape(9, sub)
    filters = own(filter_taps[0])
    tap_count = filters.shape[0]
    positions = jnp.arange(tap_count).astype(F32)[:, None]
    damping = jnp.exp(-own(decay_rates) * positions / tap_count)
    kern = filters * damping
    matrices = spectra(tap_count)

    vocabulary = jnp.arange(vocab, dtype=jnp.int32)[None, :]
    first_input = dot((token_ids[:, None] == vocabulary).astype(BF16), embedding)

    order = scatter_order(n_ctx)
    kept = order[: n_ctx // 2]
    sent = table_projection(table, weights_in, ctx, [r | 1 for r in kept], BF16)
    arrived = ctx_xor(sent, 1, (0,))
    partial = table_projection(table, weights_in, ctx, kept, F32) + arrived.astype(F32)
    bit = 2
    while bit < n_ctx:
        stays, gone = jnp.split(partial, 2, axis=0)
        partial = stays + ctx_xor(gone.astype(BF16), bit, (0,)).astype(F32)
        bit *= 2
    table_proj = (partial[0] * table_inv).astype(BF16)
    gated_0, *saved_0, proj_0 = conv_forward(table_proj, taps, kern, matrices, tokens)
    cot_stack = jnp.stack(dp_gather(cotangent, 1))
    gated_0, cot_stack, sibling = together(gated_0, cot_stack, sibling)
    gated_rows = jnp.stack(ctx_swap_in(gated_0.reshape(n_ctx, rows, sub), 0))
    shares = output_projection(gated_rows, out_full, dp)
    middle_stack, (gated_0,), late = cross_gather(
        shares, first_input, 0, [gated_0], [in_far[r] for r in far]
    )
    gated_all_0 = ctx_gather(gated_0, (0,))

    in_far.update(zip(far, late))
    in_pieces = []
    for r in sorted(in_far):
        in_pieces += [in_far[r], ctx_xor(in_far[r], 1, (1,)) if r else sibling]
    def gated_gradient(parts):
        total = dot_t(jnp.concatenate(parts, axis=1), out_full).astype(BF16)
        split = jnp.transpose(total.reshape(rows, n_ctx, sub), (1, 0, 2))
        return ctx_swap(split).reshape(seq, sub)

    cot_parts = in_order(cot_stack, dp)
    middle_all = jnp.concatenate(in_order(middle_stack, dp), axis=1)
    soon = {r: in_pieces[r] for r in range(n_ctx) if r == 1 or r % 2 == 0}
    rest = {r: in_pieces[r] for r in range(n_ctx) if r not in soon}
    normed, part, scale = input_projection(middle_all, soon, ctx)
    proj_1 = ctx_swap(input_projection_rest(middle_all, rest, part, scale, ctx))
    gated_1, *saved_1 = conv_forward(proj_1, taps, kern, matrices)

    gproj_1, gkern_1, gtaps_1 = conv_backward(
        gated_gradient(cot_parts), proj_1, taps, kern, matrices, saved_1
    )
    gproj_1, *gated_all_0 = together(gproj_1, *gated_all_0)
    gproj_rows = ctx_swap(gproj_1)
    shares = input_gradient(gproj_rows, in_pieces, middle_all, scale, ctx, dp)
    def begin_gather(normed, gproj, gated):
        planes = gproj.transpose(1, 0, 2, 3).reshape(3, seq, sub)
        planes = far_gather(jnp.concatenate([planes, gated[None]]), (1,))
        return [normed] + [planes[r] for r in sorted(planes)]

    back_stack, _, (normed, *planes) = cross_gather(
        shares, cotangent, 1, [normed, gproj_1, gated_1], (), begin_gather
    )

    normed_cols = jnp.concatenate([part.T for part in ctx_swap_in(normed, 1)], axis=1)
    gproj_all = []
    for plane in planes:
        gproj_all += [plane, ctx_xor(plane, 1, (1,))]

    back_stack, normed_cols, *gproj_all = together(back_stack, normed_cols, *gproj_all)
    back_parts = in_order(back_stack, dp)
    table_grad, gkern_0, gtaps_0 = conv_backward(
        gated_gradient(back_parts), proj_0, taps, kern, matrices, saved_0, tokens, table_inv
    )

    grads = jnp.stack([jnp.where(first, a, b) for a, b in zip(back_parts, cot_parts)])
    grad_cols = ctx_swap(grads).reshape(seq, feats)
    grad_out = grad_out_kernel(gated_all_0, gproj_all, grad_cols, ctx, sec)
    table_pieces = ctx_gather(table_grad, (0,))
    grad_in = lax.cond(
        first,
        lambda: grad_in_kernel(table.T, table_pieces, ctx),
        lambda: grad_in_kernel(normed_cols, gproj_all, ctx),
    )

    gkern = jnp.where(first, gkern_0, gkern_1)
    gtaps = jnp.where(first, gtaps_0, gtaps_1)
    gdecay = -jnp.sum(gkern * kern * positions, axis=0, keepdims=True) / tap_count
    small = jnp.concatenate([gkern * damping, gdecay, gtaps], axis=0)
    small = jnp.stack(ctx_gather(small, (0, 1)))
    small = jnp.concatenate([pick(small, ctx ^ q) for q in range(n_ctx)], axis=1)
    return (
        jnp.transpose(grad_in, (1, 0, 2))[None],
        grad_out[None],
        small[:tap_count][None],
        small[tap_count][None],
        small[tap_count + 1 :].reshape(1, 3, 3, chans),
    )


def solution(mesh):
    return jax.shard_map(
        local,
        mesh=mesh,
        in_specs=(
            P("ctx"),
            P(None, "dp"),
            P("section", "ctx", None, "dp"),
            P("section", None, None, "dp"),
            P("section", None, "dp"),
            P("section", "dp"),
            P("section", "dp", "ctx"),
            P("ctx", "dp"),
        ),
        out_specs=(
            P("section", "ctx", None, "dp"),
            P("section", "dp", "ctx"),
            P("section", None, "dp"),
            P("section", "dp"),
            P("section", None, None, "dp"),
        ),
        check_vma=False,
    )
```

```python
import functools

import jax
import jax.numpy as jnp
import numpy as np
from jax import lax
from jax.experimental import pallas as pl
from jax.experimental.pallas import tpu as pltpu
from jax.sharding import PartitionSpec as P

EPSILON = 1e-06
F32 = jnp.float32
BF16 = jnp.bfloat16


def dot(left, right):
    return jnp.dot(left, right, preferred_element_type=F32)


def dot_t(left, right):
    return lax.dot_general(left, right, (((1,), (1,)), ((), ())), preferred_element_type=F32)


def exact(left, right):
    return jnp.dot(left, right, preferred_element_type=F32, precision=lax.Precision.HIGHEST)


def pick(stack, index):
    return lax.dynamic_index_in_dim(stack, index, 0, keepdims=False)


def send(value, axes, route):
    sizes = [lax.axis_size(axis) for axis in axes]
    pairs = []
    for source, place in enumerate(np.ndindex(*sizes)):
        target = route(*place)
        if target is not None:
            pairs.append((source, int(np.ravel_multi_index(target, sizes))))
    return lax.ppermute(value, axes, pairs)


def ctx_xor(value, mask, sections):
    return send(
        value, ("section", "ctx"), lambda s, k: (s, k ^ mask) if s in sections else None
    )


def ctx_gather(value, sections):
    count = lax.axis_size("ctx")
    held = {0: value}
    bit = count // 2
    while bit:
        for r in list(held):
            held[r | bit] = ctx_xor(held[r], bit, sections)
        bit //= 2
    return [held[r] for r in range(count)]


def far_gather(value, sections):
    held = {0: value}
    bit = lax.axis_size("ctx") // 2
    while bit > 1:
        for r in list(held):
            held[r | bit] = ctx_xor(held[r], bit, sections)
        bit //= 2
    return held


def scatter_order(count):
    if count == 1:
        return [0]
    inner = scatter_order(count // 2)
    return [2 * r for r in inner] + [2 * r + 1 for r in inner]


def dp_gather(value, section):
    count = lax.axis_size("dp")
    pieces = [value]
    for _ in range(count - 1):
        pieces.append(
            send(
                pieces[-1],
                ("section", "dp"),
                lambda s, z: (s, (z + 1) % count) if s == section else None,
            )
        )
    return pieces


def cross_gather(shares, base, source, early, late=(), begin=None):
    count = lax.axis_size("dp")
    half = base.shape[0] // 2
    def move(value, shift):
        return send(
            value,
            ("section", "dp"),
            lambda s, z: (1 - s, (z + shift) % count) if s == source else None,
        )

    straight, *shares = shares
    straight = move(straight, 0)
    arrivals = [[move(shares[0][shift - 1], shift) for shift in range(1, count)]]
    tied = together(*arrivals[0], *shares[1])
    arrivals[0], shares_left = list(tied[: count - 1]), tied[count - 1 :]
    arrivals.append([move(shares_left[shift - 1], shift) for shift in range(1, count)])
    for index, start in enumerate((0, half)):
        arrivals[index].append(straight[start : start + half])

    def total(index, values):
        start = index * half
        result = base[start : start + half].astype(F32)
        for value in values:
            result = result + value.astype(F32)
        return result.astype(BF16)

    part = total(0, arrivals[0])
    if early:
        part, *early = together(part, *early)
    begun = begin(*early) if begin else []
    first = dp_gather(part, 1 - source)
    marker = min(2, count - 1)
    first[marker], *arrivals[1] = together(first[marker], *arrivals[1])
    second = dp_gather(total(1, arrivals[1]), 1 - source)
    if late:
        first[-1], second[-1], *late = together(first[-1], second[-1], *late)
    if begun and count > 1:
        second[1], *begun = together(second[1], *begun)
    stack = jnp.stack([jnp.concatenate(pair, axis=0) for pair in zip(first, second)])
    return stack, early, begun or late


def in_order(stack, me):
    return [pick(stack, (me - q) % stack.shape[0]) for q in range(stack.shape[0])]


def spectra(taps):
    freq = np.arange(taps)[:, None]
    time = np.arange(taps)[None, :]
    angle = np.pi * freq * time / taps
    nyquist = np.where(time % 2 == 0, 1.0, -1.0)
    forward = np.concatenate(
        [np.cos(angle), np.where(freq == 0, nyquist, -np.sin(angle))], axis=0
    )
    weight = np.where(freq == 0, 1.0, 2.0) / (2 * taps)
    inverse = np.concatenate(
        [weight * np.cos(angle), np.where(freq == 0, nyquist, -2 * np.sin(angle)) * np.where(freq == 0, weight, 1.0 / (2 * taps))],
        axis=0,
    ).T
    sign = np.where(np.arange(2 * taps) % taps % 2 == 0, 1.0, -1.0)
    return [jnp.asarray(m, BF16) for m in (forward, inverse, inverse * sign[None, :])]


def later(current, before, steps, row):
    return jnp.where(row < steps, pltpu.roll(before, steps, 0), pltpu.roll(current, steps, 0))


def sooner(current, after, steps, row):
    count = current.shape[0]
    return jnp.where(
        row >= count - steps,
        pltpu.roll(after, count - steps, 0),
        pltpu.roll(current, count - steps, 0),
    )


def kernel_spectrum(fwd_ref, kern_ref, row):
    tap_count = kern_ref.shape[0]
    kern = dot(fwd_ref[...], kern_ref[...].astype(BF16))
    real, imag = kern[:tap_count], kern[tap_count:]
    return real, jnp.where(row == 0, 0.0, imag), jnp.where(row == 0, imag, real)


def proj_block(projs, m, b, tap_count):
    chunk, start = divmod(b * tap_count, projs[m].shape[1])
    return projs[m][chunk, start : start + tap_count, :].astype(F32)


def short_filter(taps_ref, m, current, before, row):
    return (
        taps_ref[m : m + 1, :] * current
        + taps_ref[3 + m : 4 + m, :] * later(current, before, 1, row)
        + taps_ref[6 + m : 7 + m, :] * later(current, before, 2, row)
    )


def lookup_kernel(
    tokens_ref, table_ref, taps_ref, kern_ref, fwd_ref, inv_ref,
    gated_ref, filt_ref, spec_ref, proj_ref,
):
    tap_count, vocab = kern_ref.shape[0], table_ref.shape[1]
    entry = lax.broadcasted_iota(jnp.int32, (tap_count, vocab), 1)
    for b in range(filt_ref.shape[0] // tap_count):
        here = pl.ds(b * tap_count, tap_count)
        chosen = (entry == tokens_ref[here, :]).astype(F32).astype(BF16)
        for m in range(3):
            proj_ref[0, m, here, :] = dot(chosen, table_ref[m]).astype(BF16)
    forward_kernel(
        proj_ref, taps_ref, kern_ref, fwd_ref, inv_ref, gated_ref, filt_ref, spec_ref
    )


def collect_kernel(
    tokens_ref, scale_ref, gg_ref, proj_ref, taps_ref, kern_ref, fwd_ref, inv_ref, filt_ref, spec_ref,
    table_ref, gkern_ref, gtaps_ref, grad_spec, gproj_ref,
):
    backward_kernel(
        gg_ref, proj_ref, taps_ref, kern_ref, fwd_ref, inv_ref, filt_ref, spec_ref,
        gproj_ref, gkern_ref, gtaps_ref, grad_spec,
    )
    _, vocab, _ = table_ref.shape
    seq = filt_ref.shape[0]
    entry = lax.broadcasted_iota(jnp.int32, (vocab, seq), 0)
    chosen = (entry == tokens_ref[...]).astype(F32).astype(BF16)
    for m in range(3):
        table_ref[m] = (dot(chosen, gproj_ref[0, m]) * scale_ref[...]).astype(BF16)


def forward_kernel(proj_ref, taps_ref, kern_ref, fwd_ref, inv_ref, gated_ref, filt_ref, spec_ref):
    projs = [proj_ref.at[:, m] for m in range(3)]
    tap_count, chans = kern_ref.shape
    blocks = filt_ref.shape[0] // tap_count
    row = lax.broadcasted_iota(jnp.int32, (tap_count, chans), 0)
    sign = jnp.where(row % 2 == 0, 1.0, -1.0)
    kr, ki, kn = kernel_spectrum(fwd_ref, kern_ref, row)
    zero = jnp.zeros((tap_count, chans), F32)
    before = [zero] * 3
    last_r, last_i = zero, zero
    for b in range(blocks):
        here = pl.ds(b * tap_count, tap_count)
        streams = []
        for m in range(3):
            current = proj_block(projs, m, b, tap_count)
            streams.append(short_filter(taps_ref, m, current, before[m], row))
            before[m] = current
        part = dot(fwd_ref[...], (streams[1] * streams[2]).astype(BF16))
        pr, pi = part[:tap_count], part[tap_count:]
        wr = last_r + sign * pr
        wi = last_i + sign * pi
        last_r, last_i = pr, pi
        spec_ref[b, :tap_count, :] = wr.astype(BF16)
        spec_ref[b, tap_count:, :] = wi.astype(BF16)
        mixed = jnp.concatenate([wr * kr - wi * ki, wr * ki + wi * kn], axis=0)
        filtered = dot(inv_ref[...], mixed.astype(BF16))
        filt_ref[here, :] = filtered.astype(BF16)
        gated_ref[here, :] = (streams[0] * filtered).astype(BF16)


def backward_kernel(
    gg_ref, proj_ref, taps_ref, kern_ref, fwd_ref, inv_ref, filt_ref, spec_ref,
    gproj_ref, gkern_ref, gtaps_ref, grad_spec,
):
    projs = [proj_ref.at[:, m] for m in range(3)]
    tap_count, chans = kern_ref.shape
    blocks = filt_ref.shape[0] // tap_count
    row = lax.broadcasted_iota(jnp.int32, (tap_count, chans), 0)
    sign = jnp.where(row % 2 == 0, 1.0, -1.0)
    kr, ki, kn = kernel_spectrum(fwd_ref, kern_ref, row)
    zero = jnp.zeros((tap_count, chans), F32)
    sum_r, sum_i = zero, zero
    last = zero
    for b in range(blocks):
        here = pl.ds(b * tap_count, tap_count)
        current = proj_block(projs, 0, b, tap_count)
        query = short_filter(taps_ref, 0, current, last, row)
        last = current
        part = dot(fwd_ref[...], (gg_ref[here, :].astype(F32) * query).astype(BF16))
        grad_spec[b] = part
        gr, gi = sign * part[:tap_count], sign * part[tap_count:]
        wr = spec_ref[b, :tap_count, :].astype(F32)
        wi = spec_ref[b, tap_count:, :].astype(F32)
        rr, ii = wr * gr, wi * gi
        sum_r = sum_r + jnp.where(row == 0, rr, rr + ii)
        sum_i = sum_i + jnp.where(row == 0, ii, wr * gi - wi * gr)
    gkern_ref[...] = exact(
        inv_ref[...].astype(F32), jnp.concatenate([sum_r, sum_i], axis=0)
    )
    after = [zero] * 3
    next_r, next_i = zero, zero
    sums = [jnp.zeros((1, chans), F32) for _ in range(9)]
    for b in reversed(range(blocks)):
        chunk, start = divmod(b * tap_count, projs[0].shape[1])
        here = pl.ds(b * tap_count, tap_count)
        gr, gi = grad_spec[b, :tap_count, :], grad_spec[b, tap_count:, :]
        vr, vi = gr + sign * next_r, gi + sign * next_i
        next_r, next_i = gr, gi
        mixed = jnp.concatenate([vr * kr + vi * ki, vi * kn - vr * ki], axis=0)
        grad_prod = dot(inv_ref[...], mixed.astype(BF16))
        shifts, shorts = [], []
        for m in range(3):
            current = proj_block(projs, m, b, tap_count)
            before = proj_block(projs, m, b - 1, tap_count) if b else zero
            shifts.append([current, later(current, before, 1, row), later(current, before, 2, row)])
            if m:
                shorts.append(sum(taps_ref[3 * j + m : 3 * j + m + 1, :] * shifts[m][j] for j in range(3)))
        grads = [
            gg_ref[here, :].astype(F32) * filt_ref[here, :].astype(F32),
            grad_prod * shorts[1],
            grad_prod * shorts[0],
        ]
        for m in range(3):
            grad = grads[m]
            out = (
                taps_ref[m : m + 1, :] * grad
                + taps_ref[3 + m : 4 + m, :] * sooner(grad, after[m], 1, row)
                + taps_ref[6 + m : 7 + m, :] * sooner(grad, after[m], 2, row)
            )
            after[m] = grad
            gproj_ref[chunk, m, start : start + tap_count, :] = out.astype(BF16)
            for j in range(3):
                sums[3 * j + m] = sums[3 * j + m] + jnp.sum(
                    grad * shifts[m][j], axis=0, keepdims=True
                )
    for index in range(9):
        gtaps_ref[index : index + 1, :] = sums[index]


PARAMS = pltpu.CompilerParams(vmem_limit_bytes=56 * 1024 * 1024)


def conv_forward(proj, taps, kern, matrices, tokens=None):
    tap_count, chans = kern.shape
    seq = proj.shape[0] * proj.shape[2] if tokens is None else tokens.shape[0]
    results = [
        jax.ShapeDtypeStruct((seq, chans), BF16),
        jax.ShapeDtypeStruct((seq, chans), BF16),
        jax.ShapeDtypeStruct((seq // tap_count, 2 * tap_count, chans), BF16),
    ]
    operands = (proj, taps, kern, matrices[0], matrices[2])
    if tokens is not None:
        results.append(jax.ShapeDtypeStruct((1, 3, seq, chans), BF16))
        operands = (tokens[:, None], *operands)
    return pl.pallas_call(
        forward_kernel if tokens is None else lookup_kernel,
        out_shape=results,
        compiler_params=PARAMS,
        name="conv_forward",
    )(*operands)


def conv_backward(gg, proj, taps, kern, matrices, saved, tokens=None, scale=None):
    tap_count, chans = kern.shape
    seq = gg.shape[0]
    scratch = [pltpu.VMEM((seq // tap_count, 2 * tap_count, chans), F32)]
    operands = (gg, proj, taps, kern, matrices[0], matrices[1], *saved)
    first = jax.ShapeDtypeStruct(proj.shape, BF16)
    if tokens is not None:
        first = jax.ShapeDtypeStruct((3, scale.shape[0], chans), BF16)
        scratch.append(pltpu.VMEM(proj.shape, BF16))
        operands = (tokens[None, :], scale, *operands)
    return pl.pallas_call(
        backward_kernel if tokens is None else collect_kernel,
        out_shape=(
            first,
            jax.ShapeDtypeStruct(kern.shape, F32),
            jax.ShapeDtypeStruct((9, chans), F32),
        ),
        scratch_shapes=scratch,
        compiler_params=PARAMS,
        name="conv_backward",
    )(*operands)


def table_projection(table, weights, ctx, order, kind):
    vocab, feats = table.shape
    sub = weights.shape[2] // lax.axis_size("ctx")
    if sub % 128:
        columns = jnp.stack(
            [lax.dynamic_slice_in_dim(weights, (ctx ^ r) * sub, sub, 2) for r in order]
        )
        return jnp.einsum("vd,rmdc->rmvc", table, columns, preferred_element_type=F32).astype(kind)

    def kernel(where_ref, table_ref, weights_ref, out_ref):
        for m in range(3):
            out_ref[0, m] = dot(table_ref[...], weights_ref[m]).astype(kind)

    return pl.pallas_call(
        kernel,
        grid_spec=pltpu.PrefetchScalarGridSpec(
            num_scalar_prefetch=1,
            grid=(len(order),),
            in_specs=[
                pl.BlockSpec((vocab, feats), lambda r, where: (0, 0)),
                pl.BlockSpec((3, feats, sub), lambda r, where: (0, 0, where[r])),
            ],
            out_specs=pl.BlockSpec((1, 3, vocab, sub), lambda r, where: (r, 0, 0, 0)),
        ),
        out_shape=jax.ShapeDtypeStruct((len(order), 3, vocab, sub), kind),
        compiler_params=PARAMS,
        name="table_projection",
    )(jnp.stack([ctx ^ r for r in order]), table, weights)


def input_projection(rows_in, pieces, ctx):
    rows, full_width = rows_in.shape
    feats, chans = pieces[0].shape[1:]
    count = full_width // feats
    places = sorted(pieces)

    def kernel(ctx_ref, rows_ref, *refs):
        weights, (normed_ref, part_ref, scale_ref) = refs[: len(places)], refs[len(places) :]

        @pl.when(pl.program_id(0) == 0)
        def _():
            total = jnp.zeros((rows, 1), F32)
            for q in range(count):
                part = rows_ref[:, q * feats : (q + 1) * feats].astype(F32)
                total = total + jnp.sum(part * part, axis=1, keepdims=True)
            scale_ref[...] = lax.rsqrt(total / full_width + EPSILON)
            for q in range(count):
                part = rows_ref[:, q * feats : (q + 1) * feats].astype(F32)
                normed_ref[q] = (part * scale_ref[...]).astype(BF16)

        total = jnp.zeros((rows, chans), F32)
        for r, weight in zip(places, weights):
            start = pl.multiple_of((ctx_ref[0] ^ r) * feats, feats)
            total = total + dot(rows_ref[:, pl.ds(start, feats)], weight[0])
        part_ref[0] = total

    return pl.pallas_call(
        kernel,
        grid_spec=pltpu.PrefetchScalarGridSpec(
            num_scalar_prefetch=1,
            grid=(3,),
            in_specs=[pl.BlockSpec((rows, full_width), lambda m, ctx: (0, 0))]
            + [pl.BlockSpec((1, feats, chans), lambda m, ctx: (m, 0, 0))] * len(places),
            out_specs=[
                pl.BlockSpec((count, rows, feats), lambda m, ctx: (0, 0, 0)),
                pl.BlockSpec((1, rows, chans), lambda m, ctx: (m, 0, 0)),
                pl.BlockSpec((rows, 1), lambda m, ctx: (0, 0)),
            ],
        ),
        out_shape=(
            jax.ShapeDtypeStruct((count, rows, feats), BF16),
            jax.ShapeDtypeStruct((3, rows, chans), F32),
            jax.ShapeDtypeStruct((rows, 1), F32),
        ),
        compiler_params=PARAMS,
        name="input_projection",
    )(ctx[None], rows_in, *[pieces[r] for r in places])


def input_projection_rest(rows_in, pieces, part, scale, ctx):
    rows, full_width = rows_in.shape
    chans = part.shape[2]
    feats = next(iter(pieces.values())).shape[1]
    count = full_width // feats
    sub = chans // count
    places = sorted(pieces)

    def kernel(ctx_ref, rows_ref, part_ref, scale_ref, *refs):
        weights, proj_ref = refs[:-1], refs[-1]
        total = part_ref[0]
        for r, weight in zip(places, weights):
            start = pl.multiple_of((ctx_ref[0] ^ r) * feats, feats)
            total = total + dot(rows_ref[:, pl.ds(start, feats)], weight[0])
        total = (total * scale_ref[...]).astype(BF16)
        for q in range(count):
            proj_ref[q, 0] = total[:, q * sub : (q + 1) * sub]

    return pl.pallas_call(
        kernel,
        grid_spec=pltpu.PrefetchScalarGridSpec(
            num_scalar_prefetch=1,
            grid=(3,),
            in_specs=[
                pl.BlockSpec((rows, full_width), lambda m, ctx: (0, 0)),
                pl.BlockSpec((1, rows, chans), lambda m, ctx: (m, 0, 0)),
                pl.BlockSpec((rows, 1), lambda m, ctx: (0, 0)),
            ]
            + [pl.BlockSpec((1, feats, chans), lambda m, ctx: (m, 0, 0))] * len(places),
            out_specs=pl.BlockSpec((count, 1, rows, sub), lambda m, ctx: (0, m, 0, 0)),
        ),
        out_shape=jax.ShapeDtypeStruct((count, 3, rows, sub), BF16),
        compiler_params=PARAMS,
        name="input_projection_rest",
    )(ctx[None], rows_in, part, scale, *[pieces[r] for r in places])


def input_gradient(gproj, pieces, rows_in, scale, ctx, dp):
    rows, full_width = rows_in.shape
    feats, chans = pieces[0].shape[1:]
    count = len(pieces)
    sub = chans // count
    tile = min(256, feats)
    steps, half = feats // tile, rows // 2

    def kernel(ctx_ref, gproj_ref, rows_ref, scale_ref, *refs):
        weights, outs, (flat, grads) = refs[:count], refs[count:-2], refs[-2:]
        step = pl.program_id(0)

        @pl.when(step == 0)
        def _():
            for m in range(3):
                for q in range(count):
                    flat[m, :, q * sub : (q + 1) * sub] = gproj_ref[q, m]

        columns = pl.ds(pl.multiple_of(step * tile, tile), tile)
        for r in range(count):
            total = dot_t(flat[0], weights[r][0])
            for m in (1, 2):
                total = total + dot_t(flat[m], weights[r][m])
            grads[ctx_ref[0] ^ r, :, columns] = total * scale_ref[...]

        @pl.when(step == steps - 1)
        def _():
            stat = jnp.zeros((rows, 1), F32)
            for q in range(count):
                part = rows_ref[:, q * feats : (q + 1) * feats].astype(F32)
                stat = stat + jnp.sum(part * grads[q], axis=1, keepdims=True)
            stat = stat * scale_ref[...] * scale_ref[...] / full_width
            for shift in range(count):
                q = ctx_ref[1 + shift]
                start = pl.multiple_of(q * feats, feats)
                part = rows_ref[:, pl.ds(start, feats)].astype(F32)
                total = (grads[q] - part * stat).astype(BF16)
                if shift == 0:
                    outs[0][...] = total
                else:
                    outs[shift][...] = total[:half]
                    outs[count - 1 + shift][...] = total[half:]

    outs = pl.pallas_call(
        kernel,
        grid_spec=pltpu.PrefetchScalarGridSpec(
            num_scalar_prefetch=1,
            grid=(steps,),
            in_specs=[
                pl.BlockSpec(gproj.shape, lambda t, ctx: (0, 0, 0, 0)),
                pl.BlockSpec((rows, full_width), lambda t, ctx: (0, 0)),
                pl.BlockSpec((rows, 1), lambda t, ctx: (0, 0)),
            ]
            + [pl.BlockSpec((3, tile, chans), lambda t, ctx: (0, t, 0))] * count,
            out_specs=[pl.BlockSpec((rows, feats), lambda t, ctx: (0, 0))]
            + [pl.BlockSpec((half, feats), lambda t, ctx: (0, 0))] * (2 * count - 2),
            scratch_shapes=[
                pltpu.VMEM((3, rows, chans), BF16),
                pltpu.VMEM((count, rows, feats), F32),
            ],
        ),
        out_shape=[jax.ShapeDtypeStruct((rows, feats), BF16)]
        + [jax.ShapeDtypeStruct((half, feats), BF16)] * (2 * count - 2),
        compiler_params=PARAMS,
        name="input_gradient",
    )(jnp.concatenate([ctx[None], targets(dp, count)]), gproj, rows_in, scale, *pieces)
    return outs[0], outs[1:count], outs[count:]


def grad_in_kernel(left, pieces, ctx):
    feats, depth = left.shape
    count, sub = len(pieces), pieces[0].shape[2]
    if sub % 128:
        columns = jnp.concatenate([pick(jnp.stack(pieces), ctx ^ q) for q in range(count)], axis=2)
        columns = columns[:3]
        return jnp.einsum("dk,mkc->mdc", left, columns, preferred_element_type=F32)

    tile = min(256, feats)

    def kernel(ctx_ref, left_ref, *refs):
        out_ref = refs[count]
        for r in range(count):
            columns = pl.ds(pl.multiple_of((ctx_ref[0] ^ r) * sub, sub), sub)
            for m in range(3):
                out_ref[m, :, columns] = dot(left_ref[...], refs[r][m])

    return pl.pallas_call(
        kernel,
        grid_spec=pltpu.PrefetchScalarGridSpec(
            num_scalar_prefetch=1,
            grid=(feats // tile,),
            in_specs=[pl.BlockSpec((tile, depth), lambda t, ctx: (t, 0))]
            + [pl.BlockSpec((3, depth, sub), lambda t, ctx: (0, 0, 0))] * count,
            out_specs=pl.BlockSpec((3, tile, sub * count), lambda t, ctx: (0, t, 0)),
        ),
        out_shape=jax.ShapeDtypeStruct((3, feats, sub * count), F32),
        compiler_params=PARAMS,
        name="grad_project_in",
    )(ctx[None], left, *pieces)


def grad_out_kernel(early, late, right, ctx, sec):
    depth, feats = right.shape
    count, sub = len(early), early[0].shape[1]

    def kernel(where_ref, right_ref, *refs):
        out_ref = refs[2 * count]
        for r in range(count):
            for index, piece in ((0, refs[r].at[...]), (1, refs[count + r].at[0])):

                @pl.when((pl.program_id(0) == r) & (where_ref[count] == index))
                def _():
                    out_ref[...] = lax.dot_general(
                        piece[...],
                        right_ref[...],
                        (((0,), (0,)), ((), ())),
                        preferred_element_type=F32,
                    )

    return pl.pallas_call(
        kernel,
        grid_spec=pltpu.PrefetchScalarGridSpec(
            num_scalar_prefetch=1,
            grid=(count,),
            in_specs=[pl.BlockSpec((depth, feats), lambda r, where: (0, 0))]
            + [pl.BlockSpec((depth, sub), lambda r, where: (0, 0))] * count
            + [pl.BlockSpec((1, depth, sub), lambda r, where: (3, 0, 0))] * count,
            out_specs=pl.BlockSpec((sub, feats), lambda r, where: (where[r], 0)),
        ),
        out_shape=jax.ShapeDtypeStruct((sub * count, feats), F32),
        compiler_params=PARAMS,
        name="grad_project_out",
    )(jnp.stack([ctx ^ r for r in range(count)] + [sec]), right, *early, *late)


def together(*values):
    return lax.optimization_barrier(values)


def targets(dp, count):
    return (dp + jnp.arange(count, dtype=jnp.int32)) % count


def output_projection(gated, weights, dp):
    count, rows, sub = gated.shape
    chans, full_width = weights.shape
    parts = lax.axis_size("dp")
    width, half = full_width // parts, rows // 2

    def kernel(where_ref, gated_ref, weights_ref, *refs):
        outs, flat = refs[:-1], refs[-1]

        @pl.when(pl.program_id(0) == 0)
        def _():
            for q in range(count):
                flat[:, q * sub : (q + 1) * sub] = gated_ref[q]

        total = dot(flat[...], weights_ref[...]).astype(BF16)
        @pl.when(pl.program_id(0) == 0)
        def _():
            outs[0][...] = total

        for shift in range(1, parts):

            @pl.when(pl.program_id(0) == shift)
            def _():
                outs[shift][...] = total[:half]
                outs[parts - 1 + shift][...] = total[half:]

    outs = pl.pallas_call(
        kernel,
        grid_spec=pltpu.PrefetchScalarGridSpec(
            num_scalar_prefetch=1,
            grid=(parts,),
            in_specs=[
                pl.BlockSpec(gated.shape, lambda q, where: (0, 0, 0)),
                pl.BlockSpec((chans, width), lambda q, where: (0, where[q])),
            ],
            out_specs=[pl.BlockSpec((rows, width), lambda q, where: (0, 0))]
            + [pl.BlockSpec((half, width), lambda q, where: (0, 0))] * (2 * parts - 2),
            scratch_shapes=[pltpu.VMEM((rows, chans), BF16)],
        ),
        out_shape=[jax.ShapeDtypeStruct((rows, width), BF16)]
        + [jax.ShapeDtypeStruct((half, width), BF16)] * (2 * parts - 2),
        compiler_params=PARAMS,
        name="output_projection",
    )(targets(dp, parts), gated, weights)
    return outs[0], outs[1:parts], outs[parts:]


def ctx_swap_in(value, section):
    me = lax.axis_index("ctx")
    count = value.shape[0]
    came = [pick(value, me)]
    for r in range(1, count):
        came.append(ctx_xor(pick(value, me ^ r), r, (section,)))
    came = jnp.stack(came)
    return [pick(came, me ^ q) for q in range(count)]


def ctx_swap(value):
    return lax.all_to_all(value, "ctx", split_axis=0, concat_axis=0, tiled=True)


def local(
    token_ids, embedding, project_in, short_taps, filter_taps, decay_rates, project_out, cotangent
):
    n_ctx, n_dp = lax.axis_size("ctx"), lax.axis_size("dp")
    sec, dp, ctx = (lax.axis_index(axis) for axis in ("section", "dp", "ctx"))
    first = sec == 0
    rows, vocab = token_ids.shape[0], embedding.shape[0]
    seq = rows * n_ctx
    weights_in = jnp.transpose(project_in[0], (1, 0, 2))
    weights_out = project_out[0]
    feats, chans = weights_out.shape[1], weights_out.shape[0]
    full_width = feats * n_ctx
    sub = chans // n_ctx

    if n_ctx == n_dp:
        half = vocab // 2
        mine = lax.dynamic_slice_in_dim(embedding, sec * half, half, 0)
        came = []
        for i in range(1, n_dp):
            shifts = (i, i % (n_dp - 1) + 1)
            came.append(
                send(
                    mine,
                    ("section", "dp", "ctx"),
                    lambda s, z, k: (0, (z + shifts[s]) % n_dp, k) if z == k else None,
                )
            )
        offset = (dp - ctx) % n_dp
        low, high = embedding[:half], embedding[half:]
        for i in range(1, n_dp):
            low = jnp.where(offset == i, came[i - 1], low)
            high = jnp.where(offset == i % (n_dp - 1) + 1, came[i - 1], high)
        table = jnp.concatenate([low, high], axis=0)
    else:
        table = lax.dynamic_slice_in_dim(
            lax.all_gather(embedding, "dp", axis=1, tiled=True), ctx * feats, feats, 1
        )
    out_full = lax.all_gather(weights_out, "ctx", axis=1, tiled=True)
    in_far = far_gather(weights_in, (1,))
    far = sorted(in_far)[1:]
    sibling = ctx_xor(weights_in, 1, (1,))

    table_float = table.astype(F32)
    squares = jnp.sum(table_float * table_float, axis=1)
    tokens = token_ids.astype(F32)[None]
    held = [0]
    bit = n_ctx // 2
    while bit:
        came = ctx_xor(jnp.concatenate([squares, tokens.reshape(-1)]), bit, (0,))
        squares = squares + came[:vocab]
        tokens = jnp.concatenate([tokens, came[vocab:].reshape(-1, rows)], axis=0)
        held += [r | bit for r in held]
        bit //= 2
    table_inv = lax.rsqrt(squares[:, None] / full_width + EPSILON)
    tokens = jnp.stack([tokens[held.index(r)] for r in range(n_ctx)])
    tokens = jnp.concatenate([pick(tokens, ctx ^ q) for q in range(n_ctx)]).astype(jnp.int32)

    def own(value):
        return lax.dynamic_slice_in_dim(value, ctx * sub, sub, value.ndim - 1)

    taps = own(short_taps[0]).reshape(9, sub)
    filters = own(filter_taps[0])
    tap_count = filters.shape[0]
    positions = jnp.arange(tap_count).astype(F32)[:, None]
    damping = jnp.exp(-own(decay_rates) * positions / tap_count)
    kern = filters * damping
    matrices = spectra(tap_count)

    vocabulary = jnp.arange(vocab, dtype=jnp.int32)[None, :]
    first_input = dot((token_ids[:, None] == vocabulary).astype(BF16), embedding)

    order = scatter_order(n_ctx)
    kept = order[: n_ctx // 2]
    sent = table_projection(table, weights_in, ctx, [r | 1 for r in kept], BF16)
    arrived = ctx_xor(sent, 1, (0,))
    partial = table_projection(table, weights_in, ctx, kept, F32) + arrived.astype(F32)
    bit = 2
    while bit < n_ctx:
        stays, gone = jnp.split(partial, 2, axis=0)
        partial = stays + ctx_xor(gone.astype(BF16), bit, (0,)).astype(F32)
        bit *= 2
    table_proj = (partial[0] * table_inv).astype(BF16)
    gated_0, *saved_0, proj_0 = conv_forward(table_proj, taps, kern, matrices, tokens)
    cot_stack = jnp.stack(dp_gather(cotangent, 1))
    gated_0, cot_stack, sibling = together(gated_0, cot_stack, sibling)
    gated_rows = jnp.stack(ctx_swap_in(gated_0.reshape(n_ctx, rows, sub), 0))
    shares = output_projection(gated_rows, out_full, dp)
    middle_stack, (gated_0,), late = cross_gather(
        shares, first_input, 0, [gated_0], [in_far[r] for r in far]
    )

    in_far.update(zip(far, late))
    in_pieces = []
    for r in sorted(in_far):
        in_pieces += [in_far[r], ctx_xor(in_far[r], 1, (1,)) if r else sibling]
    def gated_gradient(parts):
        total = dot_t(jnp.concatenate(parts, axis=1), out_full).astype(BF16)
        split = jnp.transpose(total.reshape(rows, n_ctx, sub), (1, 0, 2))
        return ctx_swap(split).reshape(seq, sub)

    cot_parts = in_order(cot_stack, dp)
    middle_all = jnp.concatenate(in_order(middle_stack, dp), axis=1)
    soon = {r: in_pieces[r] for r in range(n_ctx) if r == 1 or r % 2 == 0}
    rest = {r: in_pieces[r] for r in range(n_ctx) if r not in soon}
    normed, part, scale = input_projection(middle_all, soon, ctx)
    proj_rows = input_projection_rest(middle_all, rest, part, scale, ctx)
    proj_rows, gated_0 = together(proj_rows, gated_0)
    gated_all_0 = ctx_gather(gated_0, (0,))
    proj_1 = ctx_swap(proj_rows)
    gated_1, *saved_1 = conv_forward(proj_1, taps, kern, matrices)

    gproj_1, gkern_1, gtaps_1 = conv_backward(
        gated_gradient(cot_parts), proj_1, taps, kern, matrices, saved_1
    )
    gproj_1, *gated_all_0 = together(gproj_1, *gated_all_0)
    gproj_rows = ctx_swap(gproj_1)
    shares = input_gradient(gproj_rows, in_pieces, middle_all, scale, ctx, dp)
    def begin_gather(normed, gproj, gated):
        planes = gproj.transpose(1, 0, 2, 3).reshape(3, seq, sub)
        planes = far_gather(jnp.concatenate([planes, gated[None]]), (1,))
        return [normed] + [planes[r] for r in sorted(planes)]

    back_stack, _, (normed, *planes) = cross_gather(
        shares, cotangent, 1, [normed, gproj_1, gated_1], (), begin_gather
    )

    normed_cols = jnp.concatenate([part.T for part in ctx_swap_in(normed, 1)], axis=1)
    gproj_all = []
    for plane in planes:
        gproj_all += [plane, ctx_xor(plane, 1, (1,))]

    back_stack, normed_cols, *gproj_all = together(back_stack, normed_cols, *gproj_all)
    back_parts = in_order(back_stack, dp)
    table_grad, gkern_0, gtaps_0 = conv_backward(
        gated_gradient(back_parts), proj_0, taps, kern, matrices, saved_0, tokens, table_inv
    )

    grads = jnp.stack([jnp.where(first, a, b) for a, b in zip(back_parts, cot_parts)])
    grad_cols = ctx_swap(grads).reshape(seq, feats)
    grad_out = grad_out_kernel(gated_all_0, gproj_all, grad_cols, ctx, sec)
    table_pieces = ctx_gather(table_grad, (0,))
    grad_in = lax.cond(
        first,
        lambda: grad_in_kernel(table.T, table_pieces, ctx),
        lambda: grad_in_kernel(normed_cols, gproj_all, ctx),
    )

    gkern = jnp.where(first, gkern_0, gkern_1)
    gtaps = jnp.where(first, gtaps_0, gtaps_1)
    gdecay = -jnp.sum(gkern * kern * positions, axis=0, keepdims=True) / tap_count
    small = jnp.concatenate([gkern * damping, gdecay, gtaps], axis=0)
    small = jnp.stack(ctx_gather(small, (0, 1)))
    small = jnp.concatenate([pick(small, ctx ^ q) for q in range(n_ctx)], axis=1)
    return (
        jnp.transpose(grad_in, (1, 0, 2))[None],
        grad_out[None],
        small[:tap_count][None],
        small[tap_count][None],
        small[tap_count + 1 :].reshape(1, 3, 3, chans),
    )


def solution(mesh):
    return jax.shard_map(
        local,
        mesh=mesh,
        in_specs=(
            P("ctx"),
            P(None, "dp"),
            P("section", "ctx", None, "dp"),
            P("section", None, None, "dp"),
            P("section", None, "dp"),
            P("section", "dp"),
            P("section", "dp", "ctx"),
            P("ctx", "dp"),
        ),
        out_specs=(
            P("section", "ctx", None, "dp"),
            P("section", "dp", "ctx"),
            P("section", None, "dp"),
            P("section", "dp"),
            P("section", None, None, "dp"),
        ),
        check_vma=False,
    )
```
